32 devices in a mesh: dp: 16 (over z, y, core), tensor: 2 (over x).
Axes of the slice: x: 2, y: 2, z: 4, core: 2. Of those that a mesh axis runs over, the one named last changes fastest.
Arguments:
- hidden_in: bfloat16 [16384, 1536], P(('dp', 'tensor')), may hold values from -6 to 6
- segment: int32 [16384], P('dp'), may hold values from -1 to 1, as said below
- norm_gain: bfloat16 [1536], P('dp'), may hold values from 0.5 to 1.5
- in_gate: bfloat16 [1536, 3072], P('dp', 'tensor'), may hold values from -0.15625 to 0.15625
- in_value: bfloat16 [1536, 3072], P('dp', 'tensor'), may hold values from -0.15625 to 0.15625
- in_shared: bfloat16 [1536, 256], P('dp'), may hold values from -0.15625 to 0.15625
- in_step: bfloat16 [1536, 48], P('dp', 'tensor'), may hold values from -0.15625 to 0.15625
- value_taps: float32 [4, 3072], P(None, 'tensor'), may hold values from -3 to 3
- shared_taps: float32 [4, 256], replicated, may hold values from -3 to 3
- step_bias: float32 [48], P('tensor'), may hold values from -6 to -2
- decay_log: float32 [48], P('tensor'), may hold values from 0 to 2.77
- skip_gain: float32 [48], P('tensor'), may hold values from 0.5 to 1.5
- gate_gain: float32 [3072], P('tensor'), may hold values from 0.5 to 1.5
- out_proj: bfloat16 [3072, 1536], P('tensor', 'dp'), may hold values from -0.109375 to 0.109375
- cotangent: bfloat16 [16384, 1536], P(('dp', 'tensor')), may hold values from -6 to 6
Outputs:
- block_out: bfloat16 [16384, 1536], P(('dp', 'tensor'))
- input_grad: bfloat16 [16384, 1536], P(('dp', 'tensor'))
- norm_grad: float32 [1536], P('dp')
- gate_grad: float32 [1536, 3072], P('dp', 'tensor')
- value_grad: float32 [1536, 3072], P('dp', 'tensor')
- shared_grad: float32 [1536, 256], P('dp')
- step_grad: float32 [1536, 48], P('dp', 'tensor')
- taps_grad: float32 [4, 3072], P(None, 'tensor')
- sharetaps_grad: float32 [4, 256], replicated
- bias_grad: float32 [48], P('tensor')
- decay_grad: float32 [48], P('tensor')
- skip_grad: float32 [48], P('tensor')
- gating_grad: float32 [3072], P('tensor')
- proj_grad: float32 [3072, 1536], P('tensor', 'dp')
The draws below stay inside these ranges and needn't reach their ends.
Inputs may be any that keep to these rules, and one draw needn't show every extreme that they name: `segment`: within each pack of 1024 rows: one or two sequences numbered 0 and 1 in order, each starting at a block boundary, the first at the pack's first row; a sequence's rows are consecutive, its live rows first and then -1 up to the end of its last block; the blocks after the last sequence hold -1. One sequence of every pack covers the last block of the pack's first half and the first block of its second half. A sequence has at most 1024 live rows, and some pack's has that many.
All inputs are finite; a program needn't handle non-finite values.
Results may differ from the reference program's by a relative error of at most 0.012.
Values may be sent and summed in bfloat16 or wider, within the bound.
No kernel may reach another device: no remote copies, remote signals or barrier semaphores. Data moves between devices by JAX's collectives and lax.ppermute only.
A program may use at most 192 MiB of HBM per device.

```python
import jax
import jax.numpy as jnp
from jax import lax

D = 1536
HEADS = 48
HEAD_DIM = 64
STATE = 128
KERNEL = 4
QLEN = 256
STRETCHES = 4
INNER = 3072
ROWS = 16384
N_TENSOR = 2


def draw_segment(key, part):
    key = jax.random.fold_in(key, 11)
    group_rows = STRETCHES * QLEN
    groups = ROWS // group_rows
    halfway = STRETCHES // 2
    subkeys = jax.random.split(key, 4)
    starts = jax.random.randint(subkeys[0], (groups,), 0, halfway)
    span_ends = jax.random.randint(subkeys[1], (groups,), halfway + 1, STRETCHES + 1)
    tails_first = jax.random.randint(subkeys[2], (groups,), 1, QLEN + 1)
    tails_span = jax.random.randint(subkeys[3], (groups,), 1, QLEN + 1)
    group_ids = jnp.arange(groups)
    starts = jnp.where(group_ids == 0, 0, jnp.where(group_ids == 1, 1, starts))
    span_ends = jnp.where(group_ids == 0, STRETCHES, jnp.where(group_ids == 1, halfway + 1, span_ends))
    tails_span = jnp.where(group_ids == 0, QLEN, tails_span)
    row_ids = jnp.arange(group_rows)
    block_of = (row_ids // QLEN)[None, :]
    offsets = (row_ids % QLEN)[None, :]
    start_col = starts[:, None]
    end_col = span_ends[:, None]
    live_first = (block_of < start_col) & ((block_of < start_col - 1) | (offsets < tails_first[:, None]))
    in_span = (block_of >= start_col) & (block_of < end_col)
    live_span = in_span & ((block_of < end_col - 1) | (offsets < tails_span[:, None]))
    span_id = (start_col > 0).astype(jnp.int32)
    result = jnp.where(live_first, 0, jnp.where(live_span, span_id, -1))
    return result.reshape(-1).astype(jnp.int32)


def spiked(values, own_key, source, target, parts, factor):
    owner, partner = [(jnp.arange(values.shape[dim]) // (values.shape[dim] // parts)).reshape([-1 if axis == dim else 1 for axis in range(values.ndim)]) for dim in (source, target)]
    chosen = jax.random.permutation(own_key, parts)[partner]
    strong = (owner == chosen) | (owner == (partner + parts // 2) % parts)
    return jnp.where(strong, factor * values, values)


def levels(stream_key, shape, pieces, smallest, high):
    def one(dim, parts):
        draws = jax.random.uniform(jax.random.fold_in(jax.random.fold_in(stream_key, 6), dim), (parts,), jnp.float32, smallest / len(pieces), high / len(pieces))
        return jnp.repeat(jnp.exp(draws), shape[dim] // parts).reshape((-1,) + (1,) * (len(shape) - dim - 1))

    factor_of = one(*pieces[0])
    for cut in pieces[1:]:
        factor_of = factor_of * one(*cut)
    return factor_of


def gaussian(rng, extent, scale, most, cuts=(), kind=jnp.bfloat16):
    values = scale * jax.random.normal(rng, extent, jnp.float32)
    if cuts:
        values = values * levels(rng, extent, cuts, -0.22, 0.18)
    return jnp.clip(values, -most, most).astype(kind)


def bell_draw_with(own_key, dims, spread, bound, cuts, heavy, kind=jnp.bfloat16):
    drawn = spread * jax.random.normal(own_key, dims, jnp.float32)
    if cuts:
        drawn = drawn * levels(own_key, dims, cuts, -0.22, 0.18)
    return jnp.clip(spiked(drawn, jax.random.fold_in(own_key, 3), *heavy), -bound, bound).astype(kind)


def setup_inputs(seed: int = 0) -> dict:
    arg_keys = jax.random.split(jax.random.key(seed), 16)
    hidden_in = bell_draw_with(arg_keys[0], (ROWS, D), 1.0, 6.0, ((0, 32),), (0, 1, 32, 2.75))
    segment = draw_segment(jax.random.fold_in(arg_keys[15], 71), 0)
    norm_gain = jnp.clip(1.0 + 0.1 * jax.random.normal(arg_keys[2], (D,), jnp.float32), 0.5, 1.5).astype(jnp.bfloat16)
    in_gate = gaussian(arg_keys[3], (D, INNER), D ** -0.5, 0.15625, ((0, 16), (1, 2)))
    in_value = gaussian(arg_keys[4], (D, INNER), D ** -0.5, 0.15625, ((0, 16), (1, 2)))
    in_shared = gaussian(arg_keys[5], (D, 2 * STATE), D ** -0.5, 0.15625, ((0, 16),))
    in_step = gaussian(arg_keys[6], (D, HEADS), D ** -0.5, 0.15625, ((0, 16), (1, 2)))
    value_taps = gaussian(arg_keys[7], (KERNEL, INNER), KERNEL ** -0.5, 3.0, ((1, 2),), jnp.float32)
    shared_taps = gaussian(arg_keys[8], (KERNEL, 2 * STATE), KERNEL ** -0.5, 3.0, (), jnp.float32)
    step_bias = jnp.clip(-6.0 + 4.0 * jax.random.uniform(arg_keys[9], (HEADS,), jnp.float32) ** levels(arg_keys[9], (HEADS,), ((0, 2),), -0.2, 0.2), -6.0, -2.0)
    decay_log = jnp.clip(2.77 * jax.random.uniform(arg_keys[10], (HEADS,), jnp.float32) ** levels(arg_keys[10], (HEADS,), ((0, 2),), -0.2, 0.2), 0.0, 2.77)
    skip_gain = jnp.clip(0.5 + 1.0 * jax.random.uniform(arg_keys[11], (HEADS,), jnp.float32) ** levels(arg_keys[11], (HEADS,), ((0, 2),), -0.2, 0.2), 0.5, 1.5)
    gate_gain = jnp.clip(1.0 + 0.1 * jax.random.normal(arg_keys[12], (INNER,), jnp.float32), 0.5, 1.5)
    out_proj = gaussian(arg_keys[13], (INNER, D), INNER ** -0.5, 0.109375, ((0, 2), (1, 16)))
    cotangent = bell_draw_with(arg_keys[14], (ROWS, D), 1.0, 6.0, ((0, 32),), (0, 1, 32, 2.75))
    return {"hidden_in": hidden_in, "segment": segment, "norm_gain": norm_gain, "in_gate": in_gate, "in_value": in_value, "in_shared": in_shared, "in_step": in_step, "value_taps": value_taps, "shared_taps": shared_taps, "step_bias": step_bias, "decay_log": decay_log, "skip_gain": skip_gain, "gate_gain": gate_gain, "out_proj": out_proj, "cotangent": cotangent}


@jax.custom_vjp
def low(v):
    return lax.optimization_barrier(v.astype(jnp.bfloat16)).astype(jnp.float32)

@jax.custom_vjp
def low_back(v):
    return v

def low_keep(v):
    return (low(v), None)

def low_pass(kept, grad):
    return (grad,)

def back_keep(v):
    return (v, None)

def back_low(kept, grad):
    return (low(grad),)
low.defvjp(low_keep, low_pass)
low_back.defvjp(back_keep, back_low)
EPSILON = 1e-05
PRECISE = lax.Precision.HIGHEST

def lag_masks(segment_rows):
    row_total = segment_rows.shape[0]
    firsts = segment_rows[::QLEN]
    keep_flags = jnp.concatenate([jnp.zeros((1,), jnp.float32), (firsts[1:] == firsts[:-1]).astype(jnp.float32)])
    offsets = jnp.arange(row_total) % QLEN
    keep_rows = jnp.repeat(keep_flags, QLEN)
    allowed = jnp.stack([jnp.maximum((offsets >= lag_count).astype(jnp.float32), keep_rows) for lag_count in range(KERNEL)])
    return (keep_flags, allowed)

def conv_taps(signal, weights, allowed):
    width_k = weights.shape[0]
    row_total = signal.shape[0]
    padded = jnp.pad(signal, ((width_k - 1, 0), (0, 0)))
    summed = jnp.zeros_like(signal)
    for position in range(width_k):
        summed = summed + padded[position:position + row_total] * allowed[width_k - 1 - position][:, None] * weights[position]
    return summed

def scan_core(value_act, b_act, c_act, step_rows, logdec, keep_flags):
    row_total, nheads = step_rows.shape
    blocks = row_total // QLEN
    value_blk = value_act.reshape(blocks, QLEN, nheads, HEAD_DIM)
    b_blk = b_act.reshape(blocks, QLEN, STATE)
    c_blk = c_act.reshape(blocks, QLEN, STATE)
    cumdec = jnp.cumsum(logdec.reshape(blocks, QLEN, nheads), axis=1).transpose(0, 2, 1)
    step_blk = step_rows.reshape(blocks, QLEN, nheads).transpose(0, 2, 1)
    causal = jnp.tril(jnp.ones((QLEN, QLEN), dtype=bool))
    expdiff = jnp.where(causal, jnp.exp(jnp.where(causal, cumdec[..., :, None] - cumdec[..., None, :], 0.0)), 0.0)
    gram_mat = low_back(jnp.einsum('cin,cjn->cij', c_blk, b_blk, precision=PRECISE))
    mixmat = low(gram_mat[:, None] * (expdiff * step_blk[..., None, :]))
    within = jnp.einsum('chij,cjhp->cihp', mixmat, value_blk, precision=PRECISE)
    weights = jnp.exp(cumdec[..., -1:] - cumdec) * step_blk
    scaled = low(value_blk * weights.transpose(0, 2, 1)[..., None])
    states = low_back(jnp.einsum('cjhp,cjn->chpn', scaled, b_blk, precision=PRECISE))
    entries = [jnp.zeros(states.shape[1:], jnp.float32)]
    for current in range(blocks - 1):
        entries.append(keep_flags[current + 1] * (jnp.exp(cumdec[current, :, -1])[:, None, None] * entries[-1] + states[current]))
    entry_low = low(jnp.stack(entries))
    across = low_back(jnp.einsum('cin,chpn->cihp', c_blk, entry_low, precision=PRECISE))
    between = across * jnp.exp(cumdec).transpose(0, 2, 1)[..., None]
    return (within + between).reshape(row_total, nheads * HEAD_DIM)

def block_group(params, hidden_rows, segment_rows):
    norm_gain, in_gate, in_value, in_shared, in_step, value_taps, shared_taps, step_bias, decay_log, skip_gain, gate_gain, out_proj = params
    keep_flags, allowed = lag_masks(segment_rows)
    live_rows = (segment_rows >= 0).astype(jnp.float32)[:, None]
    normed = low(hidden_rows * lax.rsqrt(lax.optimization_barrier(jnp.mean(hidden_rows * hidden_rows, axis=-1, keepdims=True)) + EPSILON) * norm_gain)
    gate_rows = low_back(jnp.dot(normed, in_gate, precision=PRECISE))
    value_rows = low_back(jnp.dot(normed, in_value, precision=PRECISE))
    raw_rows = low_back(jnp.dot(normed, in_step, precision=PRECISE))
    shared_rows = jnp.dot(normed, in_shared, precision=PRECISE)
    value_act = low(jax.nn.silu(conv_taps(value_rows, value_taps, allowed)))
    step_rows = jax.nn.softplus(raw_rows + step_bias)
    logdec = step_rows * -jnp.exp(decay_log)
    head_count = HEADS // N_TENSOR
    width_half = head_count * HEAD_DIM
    core_list = []
    for half_index in range(N_TENSOR):
        shared_act = low(jax.nn.silu(conv_taps(low_back(shared_rows), shared_taps, allowed)))
        heads_cut = slice(half_index * head_count, (half_index + 1) * head_count)
        core_list.append(scan_core(value_act[:, half_index * width_half:(half_index + 1) * width_half], shared_act[:, :STATE], shared_act[:, STATE:], step_rows[:, heads_cut], logdec[:, heads_cut], keep_flags))
    core_out = low_back(jnp.concatenate(core_list, axis=-1))
    out_rows = core_out + value_act * jnp.repeat(skip_gain, HEAD_DIM)
    product_rows = out_rows * jax.nn.silu(gate_rows)
    scale_rows = lax.rsqrt(lax.optimization_barrier(jnp.mean(product_rows * product_rows, axis=-1, keepdims=True)) + EPSILON)
    gated_low = low(product_rows * scale_rows * gate_gain)
    branch = low_back(jnp.dot(gated_low, out_proj, precision=PRECISE))
    return hidden_rows + live_rows * branch

def reference(hidden_in, segment, norm_gain, in_gate, in_value, in_shared, in_step, value_taps, shared_taps, step_bias, decay_log, skip_gain, gate_gain, out_proj, cotangent):
    params = tuple((array.astype(jnp.float32) for array in (norm_gain, in_gate, in_value, in_shared, in_step, value_taps, shared_taps, step_bias, decay_log, skip_gain, gate_gain, out_proj)))
    hidden_all = hidden_in.astype(jnp.float32)
    group_rows = STRETCHES * QLEN
    segment_groups = segment.reshape(-1, group_rows)
    run_group = jax.checkpoint(block_group)

    def forward(hidden_rows_all, weights_all):
        hidden_groups = hidden_rows_all.reshape(-1, group_rows, hidden_rows_all.shape[-1])
        outputs = lax.map(lambda paired: run_group(weights_all, paired[0], paired[1]), (hidden_groups, segment_groups))
        return outputs.reshape(hidden_rows_all.shape)
    block_out, pull_back = jax.vjp(forward, hidden_all, params)
    input_grad, weight_grads = pull_back(cotangent.astype(jnp.float32))
    return (block_out.astype(jnp.bfloat16), input_grad.astype(jnp.bfloat16), weight_grads[0], weight_grads[1], weight_grads[2], weight_grads[3], weight_grads[4], weight_grads[5], weight_grads[6], weight_grads[7], weight_grads[8], weight_grads[9], weight_grads[10], weight_grads[11])
```

```python
import functools

import jax
import jax.numpy as jnp
from jax import lax
from jax.experimental import pallas as pl
from jax.experimental.pallas import tpu as pltpu
from jax.sharding import PartitionSpec as P

HEAD_DIM = 64
STATE = 128
KERNEL = 4
QLEN = 256
INNER = 3072
EPSILON = 1e-05
TILE = 256
SIDE = 384
LANES = 128
HALF = QLEN // 2
PER = TILE // HEAD_DIM

BF = jnp.bfloat16
F32 = jnp.float32
HIGH = lax.Precision.HIGHEST
ROOM = 48 * 1024 * 1024
WEIGHT = 3


def dot(left, right, left_dim=1, right_dim=0, precision=None):
    return lax.dot_general(
        left,
        right,
        (((left_dim,), (right_dim,)), ((), ())),
        preferred_element_type=F32,
        precision=precision,
    )


def iota(shape, dim):
    return lax.broadcasted_iota(jnp.int32, shape, dim)


def split_dot(values, chooser):
    high = values.astype(BF)
    rest = (values - high.astype(F32)).astype(BF)
    return dot(high, chooser) + dot(rest, chooser)


def whole(shape):
    return pl.BlockSpec(shape, lambda *_: (0,) * len(shape))


def smem():
    return pl.BlockSpec(memory_space=pltpu.SMEM)


def call(
    body,
    grid,
    in_specs,
    out_specs,
    out_shape,
    scratch,
    flops,
    moved,
    *args,
    deps=(),
    prefetch=0,
    aliases=None,
):
    count = len(args)

    def held(*refs):
        body(*refs[:count], *refs[count + len(deps) :])

    anywhere = [pl.BlockSpec(memory_space=pl.ANY)] * len(deps)
    return pl.pallas_call(
        held,
        grid_spec=pltpu.PrefetchScalarGridSpec(
            num_scalar_prefetch=prefetch,
            grid=grid,
            in_specs=list(in_specs) + anywhere,
            out_specs=out_specs,
            scratch_shapes=scratch,
        ),
        out_shape=[jax.ShapeDtypeStruct(shape, kind) for shape, kind in out_shape],
        input_output_aliases=aliases or {},
        compiler_params=pltpu.CompilerParams(vmem_limit_bytes=ROOM),
        cost_estimate=pl.CostEstimate(
            flops=flops * WEIGHT, bytes_accessed=moved, transcendentals=0
        ),
    )(*args, *deps)


def tied(value, *deps):
    anywhere = pl.BlockSpec(memory_space=pl.ANY)
    return pl.pallas_call(
        lambda *refs: None,
        in_specs=[anywhere] * (1 + len(deps)),
        out_specs=anywhere,
        out_shape=jax.ShapeDtypeStruct(value.shape, value.dtype),
        input_output_aliases={0: 0},
        compiler_params=pltpu.CompilerParams(vmem_limit_bytes=ROOM),
    )(value, *deps)


def silu_slope(sigma, inputs):
    return sigma * (1.0 + inputs * (1.0 - sigma))


def expand(narrow):
    first = iota((QLEN, LANES), 1) < HEAD_DIM
    parts = []
    for pair in range(PER // 2):
        left = jnp.broadcast_to(narrow[:, 2 * pair : 2 * pair + 1], (QLEN, LANES))
        right = jnp.broadcast_to(narrow[:, 2 * pair + 1 : 2 * pair + 2], (QLEN, LANES))
        parts.append(jnp.where(first, left, right))
    return jnp.concatenate(parts, axis=1)


def head_rows(narrow):
    return jnp.concatenate(
        [jnp.broadcast_to(narrow[:, h : h + 1], (HEAD_DIM, STATE)) for h in range(PER)], axis=0
    )


def lane_masks():
    first = iota((1, LANES), 1) < HEAD_DIM
    return (first.astype(BF), jnp.logical_not(first).astype(BF))


def fill_weight(out_ref, rows_ref, pieces):
    at = 0
    for piece in pieces:
        count, height = piece.shape[0], piece.shape[1]
        for i in range(count):
            start = pl.multiple_of(rows_ref[at], 16) if height % 16 == 0 else rows_ref[at]
            out_ref[pl.ds(start, height), :] = piece[i]
            at += 1


def conv_sum(ext, taps):
    total = taps[KERNEL - 1 : KERNEL, :] * ext[8 : 8 + QLEN, :]
    for lag in range(1, KERNEL):
        total = total + taps[KERNEL - 1 - lag : KERNEL - lag, :] * ext[8 - lag : 8 - lag + QLEN, :]
    return total


def norm_body(
    half_blocks,
    pieces_total,
    gain_lane,
    rows_ref,
    place,
    keep,
    own,
    got,
    taps,
    bias,
    decay,
    *refs,
):
    pieces = refs[:pieces_total]
    (
        feat,
        feat_t,
        shared,
        b_out,
        c_out,
        gram,
        gram_t,
        cols,
        pack,
        rowpack,
        side_w,
        gain,
        hold,
        ext,
    ) = refs[pieces_total:]
    b = pl.program_id(0)
    mine = (b // half_blocks) == place[0]

    @pl.when(b == 0)
    def _():
        fill_weight(side_w, rows_ref, pieces)
        edge = gain_lane // LANES * LANES
        spread = side_w[:, edge : edge + LANES].astype(F32).T
        gain[...] = spread[gain_lane - edge : gain_lane - edge + 1, :]

    @pl.when(mine)
    def _():
        hold[...] = own[...].astype(F32)

    @pl.when(jnp.logical_not(mine))
    def _():
        hold[...] = got[...].astype(F32)

    rows = hold[...]
    inverse = lax.rsqrt(jnp.mean(rows * rows, axis=1, keepdims=True) + EPSILON)
    normed = (rows * inverse * gain[...]).astype(BF)
    feat[...] = normed
    feat_t[...] = normed.T
    side = dot(normed, side_w[...])
    pre = side[:, :TILE]
    shared[...] = pre

    @pl.when(b == 0)
    def _():
        ext[...] = jnp.zeros_like(ext)

    ext[0:8, :] = ext[QLEN : QLEN + 8, :] * keep[b]
    ext[8 : 8 + QLEN, :] = pre
    conv = conv_sum(ext, taps)
    act = (conv * jax.nn.sigmoid(conv)).astype(BF)
    b_low = act[:, :STATE]
    c_low = act[:, STATE:]
    b_out[...] = b_low
    c_out[...] = c_low
    lower = iota((QLEN, QLEN), 0) >= iota((QLEN, QLEN), 1)
    upper = iota((QLEN, QLEN), 0) <= iota((QLEN, QLEN), 1)
    gram[0] = jnp.where(lower, dot(c_low, b_low, 1, 1), 0.0)
    gram_t[0] = jnp.where(upper, dot(b_low, c_low, 1, 1), 0.0)
    raw = side[:, TILE:] + bias[...]
    step = jnp.maximum(raw, 0.0) + jnp.log1p(jnp.exp(-jnp.abs(raw)))
    logdec = step * -jnp.exp(decay[...])
    cum = dot(lower.astype(F32), logdec, precision=HIGH)
    cols[0] = raw
    cols[1] = step
    cols[2] = logdec
    cum_t = cum.T
    step_t = step.T
    for j in range(pack.shape[0]):
        heads = slice(PER * j, PER * j + PER)
        pack[j] = jnp.concatenate([cum[:, heads], step[:, heads]], axis=1)
        rowpack[j, 0] = jnp.concatenate([cum_t[heads, :], step_t[heads, :]], axis=0)


def value_body(
    pieces_total,
    blocks,
    past,
    rows_ref,
    keep,
    feat,
    *refs,
):
    pieces = refs[:pieces_total]
    refs = refs[: pieces_total + 7] + refs[pieces_total + 7 + past :]
    (
        taps,
        skip,
        pack,
        rowpack,
        b_ref,
        c_ref,
        gram,
        weight,
        pre_out,
        act_out,
        out_rows,
        entry,
        pre,
        ext,
        state,
    ) = refs[pieces_total:]
    fill_weight(weight, rows_ref, pieces)
    masks = lane_masks()
    for b in range(blocks):
        span = slice(b * QLEN, (b + 1) * QLEN)
        pre[...] = dot(feat[span, :], weight[...])
        pre_out[span, :] = pre[...].astype(BF)
        if b == 0:
            ext[0:8, :] = jnp.zeros((8, TILE), F32)
            state[...] = jnp.zeros_like(state)
        else:
            ext[0:8, :] = ext[QLEN : QLEN + 8, :] * keep[b]
        ext[8 : 8 + QLEN, :] = pre[...]
        conv = conv_sum(ext, taps)
        act_low = (conv * jax.nn.sigmoid(conv)).astype(BF)
        act_out[span, :] = act_low
        act = act_low.astype(F32)
        narrow = pack[0, span, :]
        cum = narrow[:, :PER]
        step = narrow[:, PER:]
        last = cum[QLEN - 1 : QLEN, :]
        stepped = (act * expand(step)).astype(BF)
        scaled = (act * expand(jnp.exp(last - cum) * step)).astype(BF)
        row_cum = rowpack[0, b]
        parts = []
        for pair in range(PER // 2):
            lanes = slice(pair * LANES, (pair + 1) * LANES)
            tops, lows, values = [], [], []
            for k in range(2):
                h = 2 * pair + k
                col = cum[:, h : h + 1]
                row = row_cum[h : h + 1, :]
                e00 = jnp.exp(jnp.minimum(col[:HALF] - row[:, :HALF], 0.0))
                e10 = jnp.exp(col[HALF:] - row[:, :HALF])
                e11 = jnp.exp(jnp.minimum(col[HALF:] - row[:, HALF:], 0.0))
                tops.append((gram[b, :HALF, :HALF] * e00).astype(BF))
                lows.append((gram[b, HALF:, :HALF] * e10).astype(BF))
                lows.append((gram[b, HALF:, HALF:] * e11).astype(BF))
                values.append(stepped[:, lanes] * masks[k])
            top = dot(
                jnp.concatenate(tops, axis=1),
                jnp.concatenate([v[:HALF] for v in values], axis=0),
            )
            low = dot(jnp.concatenate(lows, axis=1), jnp.concatenate(values, axis=0))
            parts.append(jnp.concatenate([top, low], axis=0))
        within = jnp.concatenate(parts, axis=1)
        held = state[...]
        entry[b] = held
        across = dot(c_ref[span, :], held.astype(BF), 1, 1)
        core = within + across * expand(jnp.exp(cum))
        out_rows[span, :] = core + act * skip[...]
        if b + 1 < blocks:
            fresh = dot(scaled, b_ref[span, :], 0, 0)
            state[...] = keep[b + 1] * (head_rows(jnp.exp(last)) * held + fresh)


def gate_body(pieces_total, rows_ref, feat, *refs):
    pieces = refs[:pieces_total]
    out_rows, weight, gate_out, squares = refs[pieces_total:]
    fill_weight(weight, rows_ref, pieces)

    @pl.when(pl.program_id(0) == 0)
    def _():
        squares[...] = jnp.zeros_like(squares)

    for b in range(feat.shape[0] // QLEN):
        span = slice(b * QLEN, (b + 1) * QLEN)
        gate = dot(feat[span, :], weight[...])
        gate_out[span, :] = gate.astype(BF)
        product = out_rows[span, :] * (gate * jax.nn.sigmoid(gate))
        power = product * product
        squares[span, :] += power[:, :LANES] + power[:, LANES:]


def mask_body(half_blocks, place, own, got, live, out, out_t):
    b = pl.program_id(0)
    mine = (b // half_blocks) == place[0]

    @pl.when(mine)
    def _():
        out[...] = own[...] * live[...]

    @pl.when(jnp.logical_not(mine))
    def _():
        out[...] = got[...] * live[...]

    out_t[...] = out[...].T


def proj_body(place, left, out_rows, gate_ref, scale_ref, gain, gated_out, *outs):
    for b in range(gated_out.shape[0] // QLEN):
        span = slice(b * QLEN, (b + 1) * QLEN)
        gate = gate_ref[span, :].astype(F32)
        product = out_rows[span, :] * (gate * jax.nn.sigmoid(gate))
        gated_out[span, :] = (product * scale_ref[span, :] * gain[...]).astype(BF)
    emit_outer(place, dot(left[...], gated_out[...]), outs)


def branch_body(pieces_total, place, rows_ref, gated, grad, *refs):
    pieces = refs[:pieces_total]
    weight, send, mine, row_dot = refs[pieces_total:]
    s = pl.program_id(0)

    @pl.when(s == 0)
    def _():
        fill_weight(weight, rows_ref, pieces)

    branch = dot(gated[...], weight[...], 1, 1)
    row_dot[...] = jnp.sum(branch * grad[...].astype(F32), axis=1, keepdims=True)

    @pl.when(s < pl.num_programs(0) // 2)
    def _():
        send[...] = branch.astype(BF)

    @pl.when(s >= pl.num_programs(0) // 2)
    def _():
        mine[...] = branch


def gating_body(
    grad, weight, out_ref, gate_ref, act_ref, scale_ref, row_dot, gain, core, gate_grad, sums
):
    gating = jnp.zeros((1, TILE), F32)
    skipping = jnp.zeros((1, TILE), F32)
    for b in range(grad.shape[0] // QLEN):
        span = slice(b * QLEN, (b + 1) * QLEN)
        grad_gated = dot(grad[span, :], weight[...])
        gate = gate_ref[span, :].astype(F32)
        sigma = jax.nn.sigmoid(gate)
        act = gate * sigma
        out_rows = out_ref[span, :]
        scale = scale_ref[span, :]
        normal = out_rows * act * scale
        gating = gating + jnp.sum(grad_gated * normal, axis=0, keepdims=True)
        grad_product = scale * (
            grad_gated * gain[...] - normal * (row_dot[span, :] * (1.0 / INNER))
        )
        grad_out = grad_product * act
        core[span, :] = grad_out.astype(BF)
        gate_grad[span, :] = (grad_product * out_rows * silu_slope(sigma, gate)).astype(BF)
        skipping = skipping + jnp.sum(
            grad_out * act_ref[span, :].astype(F32), axis=0, keepdims=True
        )
    sums[...] = jnp.concatenate([gating, skipping], axis=0)


def scan_body(
    blocks,
    keep,
    core_ref,
    act_ref,
    pre_ref,
    out_ref,
    skip,
    taps,
    pack,
    rowpack,
    b_ref,
    c_ref,
    gram_t,
    entry,
    *refs,
):
    past = refs[:-9]
    grad_pre, taps_grad, gram_grad, b_grad, c_grad, stats, ext, tail, carry = refs[-9:]

    @pl.when(pl.program_id(0) == 0)
    def _():
        if past:
            gram_grad[...] = past[0][...]
            b_grad[...] = past[1][...]
            c_grad[...] = past[2][...]
        else:
            gram_grad[...] = jnp.zeros_like(gram_grad)
            b_grad[...] = jnp.zeros_like(b_grad)
            c_grad[...] = jnp.zeros_like(c_grad)

    masks = lane_masks()
    owner = iota((TILE, LANES), 0) // HEAD_DIM
    lane = iota((TILE, LANES), 1)
    chooser = [(lane == owner + PER * q).astype(BF) for q in range(4)]
    final_row = iota((QLEN, LANES), 0) == QLEN - 1
    ones = jnp.ones((8, STATE), BF)
    tap_sums = [jnp.zeros((1, TILE), F32) for _ in range(KERNEL)]
    for b in reversed(range(blocks)):
        span = slice(b * QLEN, (b + 1) * QLEN)
        final = b == blocks - 1
        grad_low = core_ref[span, :]
        grad = grad_low.astype(F32)
        act = act_ref[span, :].astype(F32)
        narrow = pack[0, span, :]
        cum = narrow[:, :PER]
        step = narrow[:, PER:]
        last = cum[QLEN - 1 : QLEN, :]
        step_wide = expand(step)
        stepped = (act * step_wide).astype(BF)
        row_cum = rowpack[0, b]
        parts = []
        upper_sum = None
        lower_sum = None
        for pair in range(PER // 2):
            lanes = slice(pair * LANES, (pair + 1) * LANES)
            grad_pair = grad_low[:, lanes]
            tops, lows, grads = [], [], []
            for k in range(2):
                h = 2 * pair + k
                col = cum[:, h : h + 1]
                row = row_cum[h : h + 1, :]
                e00 = jnp.exp(jnp.minimum(row[:, :HALF] - col[:HALF], 0.0))
                e01 = jnp.exp(row[:, HALF:] - col[:HALF])
                e11 = jnp.exp(jnp.minimum(row[:, HALF:] - col[HALF:], 0.0))
                value = stepped[:, lanes] * masks[k]
                upper = dot(value[:HALF], grad_pair, 1, 1) * jnp.concatenate([e00, e01], axis=1)
                lower = dot(value[HALF:], grad_pair[HALF:], 1, 1) * e11
                upper_sum = upper if upper_sum is None else upper_sum + upper
                lower_sum = lower if lower_sum is None else lower_sum + lower
                tops.append((gram_t[b, :HALF, :HALF] * e00).astype(BF))
                tops.append((gram_t[b, :HALF, HALF:] * e01).astype(BF))
                lows.append((gram_t[b, HALF:, HALF:] * e11).astype(BF))
                grads.append(grad_pair * masks[k])
            top = dot(jnp.concatenate(tops, axis=1), jnp.concatenate(grads, axis=0))
            low = dot(
                jnp.concatenate(lows, axis=1),
                jnp.concatenate([g[HALF:] for g in grads], axis=0),
            )
            parts.append(jnp.concatenate([top, low], axis=0))
        gram_grad[b, :HALF, :] += upper_sum
        gram_grad[b, HALF:, HALF:] += lower_sum
        mixed = jnp.concatenate(parts, axis=1)
        between = out_ref[span, :] - act * skip[...]
        flows = stepped.astype(F32) * mixed
        grad_value = step_wide * mixed + skip[...] * grad
        held = entry[b]
        across_low = (grad * expand(jnp.exp(cum))).astype(BF)
        c_grad[span, :] += dot(across_low, held.astype(BF))
        totals = split_dot(grad * between, chooser[1])
        if not final:
            states = carry[...]
            states_low = states.astype(BF)
            weights = expand(jnp.exp(last - cum) * step)
            pulled = dot(b_ref[span, :], states_low, 1, 1) * weights
            grad_value = grad_value + pulled
            weighted = act * pulled
            scaled = (act * weights).astype(BF)
            b_grad[span, :] += dot(scaled, states_low)
            totals = totals + split_dot(flows + weighted, chooser[0])
            totals = totals + split_dot(weighted, chooser[2])
            passed = head_rows(jnp.exp(last)) * states
            spread = passed * held
            high = spread.astype(BF)
            rest = (spread - high.astype(F32)).astype(BF)
            summed = dot(ones, high, 1, 1) + dot(ones, rest, 1, 1)
            last_sum = split_dot(summed, chooser[3])
            totals = totals + jnp.where(final_row, last_sum[0:1, :], 0.0)
        else:
            totals = totals + split_dot(flows, chooser[0])
        stats[0, span, :] = totals[:, : 4 * PER]
        if b > 0:
            fresh = dot(across_low, c_ref[span, :], 0, 0)
            carry[...] = keep[b] * (fresh if final else fresh + passed)
        if b > 0:
            ext[0:8, :] = pre_ref[b * QLEN - 16 : b * QLEN, :].astype(F32)[8:, :] * keep[b]
        else:
            ext[0:8, :] = jnp.zeros((8, TILE), F32)
        ext[8 : 8 + QLEN, :] = pre_ref[span, :].astype(F32)
        conv = conv_sum(ext, taps)
        sigma = jax.nn.sigmoid(conv)
        slope = grad_value * silu_slope(sigma, conv)
        for lag in range(KERNEL):
            tap_sums[KERNEL - 1 - lag] = tap_sums[KERNEL - 1 - lag] + jnp.sum(
                slope * ext[8 - lag : 8 - lag + QLEN, :], axis=0, keepdims=True
            )
        if final:
            tail[QLEN : QLEN + 8, :] = jnp.zeros((8, TILE), F32)
        else:
            tail[QLEN : QLEN + 8, :] = tail[0:8, :] * keep[b + 1]
        tail[0:QLEN, :] = slope
        pulled_back = taps[KERNEL - 1 : KERNEL, :] * slope
        for lag in range(1, KERNEL):
            pulled_back = (
                pulled_back
                + taps[KERNEL - 1 - lag : KERNEL - lag, :] * tail[lag : lag + QLEN, :]
            )
        grad_pre[span, :] = pulled_back.astype(BF)
    taps_grad[...] = jnp.concatenate(tap_sums, axis=0)


def side_body(
    blocks,
    keep,
    gram_grad,
    b_grad,
    c_grad,
    b_ref,
    c_ref,
    shared,
    taps,
    cols,
    decay,
    *refs,
):
    stats = refs[:-5]
    out, taps_grad, sums, ext, tail = refs[-5:]
    lower = iota((QLEN, QLEN), 0) >= iota((QLEN, QLEN), 1)
    upper = iota((QLEN, QLEN), 0) <= iota((QLEN, QLEN), 1)
    final_row = iota((QLEN, LANES), 0) == QLEN - 1
    rate = jnp.exp(decay[...])
    tap_sums = [jnp.zeros((1, TILE), F32) for _ in range(KERNEL)]
    decay_sum = jnp.zeros((1, LANES), F32)
    bias_sum = jnp.zeros((1, LANES), F32)
    tiles = sum(part.shape[0] for part in stats)
    padding = jnp.zeros((QLEN, LANES - PER * tiles), F32)
    for b in reversed(range(blocks)):
        span = slice(b * QLEN, (b + 1) * QLEN)
        final = b == blocks - 1
        gathered = [
            jnp.concatenate(
                [
                    part[j, span, PER * q : PER * q + PER]
                    for part in stats
                    for j in range(part.shape[0])
                ]
                + [padding],
                axis=1,
            )
            for q in range(4)
        ]
        pulled = gathered[0]
        grad_cum = gathered[1] - pulled + gathered[3]
        grad_cum = grad_cum + jnp.where(
            final_row, jnp.sum(gathered[2], axis=0, keepdims=True), 0.0
        )
        grad_log = dot(upper.astype(F32), grad_cum, precision=HIGH)
        raw = cols[0, span, :]
        step = cols[1, span, :]
        sigma = jax.nn.sigmoid(raw)
        ratio = jnp.where(raw < -20.0, 1.0, sigma / jnp.maximum(step, 1e-30))
        grad_raw = pulled * ratio - rate * grad_log * sigma
        decay_sum = decay_sum + jnp.sum(grad_log * cols[2, span, :], axis=0, keepdims=True)
        bias_sum = bias_sum + jnp.sum(grad_raw, axis=0, keepdims=True)
        out[span, TILE:] = grad_raw.astype(BF)
        gram_low = jnp.where(upper, gram_grad[b], 0.0).astype(BF)
        b_total = b_grad[span, :] + dot(gram_low, c_ref[span, :])
        c_total = c_grad[span, :] + dot(gram_low, b_ref[span, :], 0, 0)
        grad_act = jnp.concatenate([b_total, c_total], axis=1)
        if b > 0:
            ext[0:8, :] = shared[b * QLEN - 8 : b * QLEN, :] * keep[b]
        else:
            ext[0:8, :] = jnp.zeros((8, TILE), F32)
        ext[8 : 8 + QLEN, :] = shared[span, :]
        conv = conv_sum(ext, taps)
        slope = grad_act * silu_slope(jax.nn.sigmoid(conv), conv)
        for lag in range(KERNEL):
            tap_sums[KERNEL - 1 - lag] = tap_sums[KERNEL - 1 - lag] + jnp.sum(
                slope * ext[8 - lag : 8 - lag + QLEN, :], axis=0, keepdims=True
            )
        if final:
            tail[QLEN : QLEN + 8, :] = jnp.zeros((8, TILE), F32)
        else:
            tail[QLEN : QLEN + 8, :] = tail[0:8, :] * keep[b + 1]
        tail[0:QLEN, :] = slope
        pulled_back = taps[KERNEL - 1 : KERNEL, :] * slope
        for lag in range(1, KERNEL):
            pulled_back = (
                pulled_back
                + taps[KERNEL - 1 - lag : KERNEL - lag, :] * tail[lag : lag + QLEN, :]
            )
        out[span, :TILE] = pulled_back.astype(BF)
    taps_grad[...] = jnp.concatenate(tap_sums, axis=0)
    sums[...] = jnp.concatenate([decay_sum, bias_sum], axis=0)


def emit_outer(place, total, outs):
    if len(outs) == 1:
        outs[0][...] = total
        return
    mine, send = outs
    low = total.astype(BF).reshape(mine.shape[0], 2, mine.shape[1], total.shape[1])

    @pl.when(place[0] == 0)
    def _():
        mine[...] = low[:, 0]
        send[...] = low[:, 1]

    @pl.when(place[0] == 1)
    def _():
        mine[...] = low[:, 1]
        send[...] = low[:, 0]


def outer_body(place, left, right, *outs):
    emit_outer(place, dot(left[...], right[...]), outs)


def back_body(parts, place, gate_grad, side_grad, gate_w, value_w, side_w, *refs):
    value_grads = refs[:parts]
    out = refs[parts]
    total = dot(gate_grad[...], gate_w[...], 1, 1)
    total = total + dot(side_grad[...], side_w[...], 1, 1)
    at = 0
    for value_grad in value_grads:
        end = at + value_grad.shape[1]
        total = total + dot(value_grad[...], value_w[:, at:end], 1, 1)
        at = end
    out[...] = total.astype(out.dtype)


def input_body(mine, got, hidden, cot, gain, out):
    total = (mine[...] + got[...].astype(F32)) * gain[...]
    rows = hidden[...].astype(F32)
    inverse = lax.rsqrt(jnp.mean(rows * rows, axis=1, keepdims=True) + EPSILON)
    hat = rows * inverse
    spread = jnp.mean(total * hat, axis=1, keepdims=True)
    out[...] = (cot[...].astype(F32) + (total - hat * spread) * inverse).astype(BF)


def out_body(mine, got, hidden, live, out):
    out[...] = (
        hidden[...].astype(F32) + live[...] * (mine[...] + got[...].astype(F32))
    ).astype(BF)


class Links:
    def __init__(self, devices, shard_rows):
        self.devices = devices
        self.height = shard_rows
        self.paired = devices % 4 == 0 and shard_rows % 16 == 0
        self.ring = max(devices // 4, 1)
        spot = lax.axis_index("dp")
        self.a, self.b, self.c = spot // 4, (spot // 2) % 2, spot % 2
        self.spot = spot

    def moved(self, rule):
        pairs = []
        for a in range(self.ring):
            for b in range(2):
                for c in range(2):
                    ta, tb, tc = rule(a, b, c)
                    pairs.append(((a * 2 + b) * 2 + c, (ta * 2 + tb) * 2 + tc))
        return pairs

    def over_core(self, x):
        return lax.ppermute(x, "dp", self.moved(lambda a, b, c: (a, b, 1 - c)))

    def over_pair(self, x):
        return lax.ppermute(x, "dp", self.moved(lambda a, b, c: (a, 1 - b, c)))

    def over_ring(self, x, k):
        return lax.ppermute(x, "dp", self.moved(lambda a, b, c: ((a + k) % self.ring, b, c)))

    def gather_fast(self, shard):
        if not self.paired:
            return [lax.all_gather(shard, "dp", axis=0, tiled=True)[None]], (shard,)
        near = [k for k in range(1, self.ring) if k in (1, self.ring - 1)]
        far = [k for k in range(1, self.ring) if k not in near]
        held = {0: shard}
        other = {0: self.over_pair(shard)}
        for k in near:
            held[k] = self.over_ring(shard, k)
        later = tied(shard, other[0], *[held[k] for k in near])
        for k in far:
            held[k] = self.over_ring(later, k)
        for k in near + far:
            other[k] = self.over_pair(held[k])
        pieces = [held[k] for k in range(self.ring)] + [other[k] for k in range(self.ring)]
        pieces = pieces + [self.over_core(x) for x in pieces]
        return [x[None] for x in pieces], (held[(near + far)[-1]], other[near[0]])

    def ring_parts(self, shard):
        if not self.paired:
            return [shard]
        return [shard] + [self.over_ring(shard, k) for k in range(1, self.ring)]

    def ring_stack(self, parts, *deps):
        if not self.paired:
            return parts[0]
        return jnp.stack(parts[:-1] + [tied(parts[-1], *deps)])

    def gather_rest(self, held, *deps):
        if not self.paired:
            return [lax.all_gather(held, "dp", axis=0, tiled=True)[None]]
        other = tied(self.over_pair(held), *deps)
        return [held, other, self.over_core(held), self.over_core(other)]

    def ring_halves(self, parts):
        if not self.paired:
            return [parts[0]]
        cut = max(self.ring // 2, 1)
        return [jnp.stack(parts[:cut])] + ([jnp.stack(parts[cut:])] if parts[cut:] else [])

    def pair_halves(self, halves):
        return [self.over_pair(h) for h in halves] if self.paired else []

    def join_halves(self, halves, others):
        if not self.paired:
            return [lax.all_gather(halves[0], "dp", axis=0, tiled=True)[None]]
        pieces = halves + others
        return pieces + [self.over_core(x) for x in pieces]

    def starts(self):
        if not self.paired:
            return jnp.zeros((1,), jnp.int32)
        rows = []
        for c in (self.c, 1 - self.c):
            for b in (self.b, 1 - self.b):
                for k in range(self.ring):
                    a = lax.rem(self.a - k + self.ring, self.ring)
                    rows.append(((a * 2 + b) * 2 + c) * self.height)
        return jnp.stack(rows).astype(jnp.int32)

    def scatter_core(self, parts):
        if not self.paired:
            return parts
        mine, send = parts
        shape = (self.ring, 2) + mine.shape[1:]
        got = self.over_core(send)
        mine, got = mine.reshape(shape), got.reshape(shape)
        away = self.pick(mine, 1 - self.b, 1).astype(F32) + self.pick(got, 1 - self.b, 1).astype(F32)
        return [away.astype(BF), mine, got]

    def pick(self, x, i, dim):
        return lax.dynamic_index_in_dim(x, i, dim, keepdims=False)

    def scatter_pair(self, parts, *deps):
        if not self.paired:
            return parts
        away, mine, got = parts
        near = tied(self.over_pair(away), *deps) if deps else self.over_pair(away)

        def summed(i):
            total = self.pick(self.pick(mine, self.b, 1), i, 0).astype(F32)
            total = total + self.pick(self.pick(got, self.b, 1), i, 0).astype(F32)
            return total + self.pick(near, i, 0).astype(F32)

        leaving = [
            summed(lax.rem(self.a + k, self.ring)).astype(BF) for k in range(1, self.ring)
        ]
        return leaving + [summed(self.a)]

    def scatter_ring(self, parts):
        if not self.paired:
            return lax.psum_scatter(parts[0], "dp", scatter_dimension=0, tiled=True)
        total = parts[-1]
        for k in range(1, self.ring):
            total = total + self.over_ring(parts[k - 1], k).astype(F32)
        return total

    def reduce(self, x):
        if not self.paired:
            return lax.psum(x, "dp")
        x = x + self.over_core(x)
        x = x + self.over_pair(x)
        total = x
        for k in range(1, self.ring):
            total = total + self.over_ring(x, k)
        return total


def over_tensor(x):
    return lax.ppermute(x, "tensor", [(0, 1), (1, 0)])


def on_device(
    hidden_in,
    segment,
    norm_gain,
    in_gate,
    in_value,
    in_shared,
    in_step,
    value_taps,
    shared_taps,
    step_bias,
    decay_log,
    skip_gain,
    gate_gain,
    out_proj,
    cotangent,
    devices,
):
    half_rows, width = hidden_in.shape
    rows = segment.shape[0]
    blocks = rows // QLEN
    half_blocks = half_rows // QLEN
    wide = in_value.shape[1]
    tiles = wide // TILE
    heads = step_bias.shape[0]
    height = in_value.shape[0]
    links = Links(devices, height)
    tensor = lax.axis_index("tensor")
    place = jnp.reshape(tensor, (1,)).astype(jnp.int32)
    core = jnp.reshape(links.c, (1,)).astype(jnp.int32)

    firsts = segment[::QLEN]
    keep = jnp.concatenate(
        [jnp.zeros((1,), F32), (firsts[1:] == firsts[:-1]).astype(F32)]
    )
    live = (segment >= 0).astype(F32)[:, None]
    live_own = lax.dynamic_slice_in_dim(live, tensor * half_rows, half_rows)
    pad = SIDE - 2 * STATE - heads - 1
    value_shard = jnp.concatenate(
        [in_value, in_shared, in_step, norm_gain[:, None], jnp.zeros((height, pad), BF)], axis=1
    )
    hidden_got = over_tensor(hidden_in)
    starts = links.starts()
    value_pieces, value_last = links.gather_fast(value_shard)
    gate_shard = tied(in_gate, *value_last)
    gate_ring = links.ring_parts(gate_shard)
    cot_sent = tied(cotangent, hidden_got)
    cot_got = over_tensor(cot_sent)

    bias_row = jnp.pad(step_bias, (0, LANES - heads)).reshape(1, LANES)
    decay_row = jnp.pad(decay_log, (0, LANES - heads)).reshape(1, LANES)
    skip_row = jnp.repeat(skip_gain, HEAD_DIM).reshape(1, wide)
    gate_row = gate_gain.reshape(1, wide)

    block_rows = lambda n: pl.BlockSpec((QLEN, n), lambda b, *_: (b, 0))
    half_spec = pl.BlockSpec((QLEN, width), lambda b, *_: (b % half_blocks, 0))
    (
        feat,
        feat_t,
        shared,
        b_low,
        c_low,
        gram,
        gram_t,
        cols,
        pack,
        rowpack,
        side_w,
        gain_row,
    ) = call(
        functools.partial(norm_body, half_blocks, len(value_pieces), 2 * STATE + heads),
        (blocks,),
        [
            smem(),
            smem(),
            smem(),
            half_spec,
            half_spec,
            whole((KERNEL, TILE)),
            whole((1, LANES)),
            whole((1, LANES)),
        ]
        + [
            pl.BlockSpec(p.shape[:2] + (SIDE,), lambda b: (0, 0, wide // SIDE))
            for p in value_pieces
        ],
        [
            block_rows(width),
            pl.BlockSpec((width, QLEN), lambda b: (0, b)),
            block_rows(TILE),
            block_rows(STATE),
            block_rows(STATE),
            pl.BlockSpec((1, QLEN, QLEN), lambda b: (b, 0, 0)),
            pl.BlockSpec((1, QLEN, QLEN), lambda b: (b, 0, 0)),
            pl.BlockSpec((3, QLEN, LANES), lambda b: (0, b, 0)),
            pl.BlockSpec((tiles, QLEN, 2 * PER), lambda b: (0, b, 0)),
            pl.BlockSpec((tiles, 1, 2 * PER, QLEN), lambda b: (0, b, 0, 0)),
            whole((width, SIDE)),
            whole((1, width)),
        ],
        [
            ((rows, width), BF),
            ((width, rows), BF),
            ((rows, TILE), F32),
            ((rows, STATE), BF),
            ((rows, STATE), BF),
            ((blocks, QLEN, QLEN), F32),
            ((blocks, QLEN, QLEN), F32),
            ((3, rows, LANES), F32),
            ((tiles, rows, 2 * PER), F32),
            ((tiles, blocks, 2 * PER, QLEN), F32),
            ((width, SIDE), BF),
            ((1, width), F32),
        ],
        [pltpu.VMEM((QLEN, width), F32), pltpu.VMEM((QLEN + 8, TILE), F32)],
        2 * rows * width * SIDE,
        20 * rows * width,
        starts,
        place,
        keep,
        hidden_in,
        hidden_got,
        shared_taps,
        bias_row,
        decay_row,
        *value_pieces,
        deps=(gate_shard, cot_sent),
    )

    def tile_cols(n, first=0):
        return pl.BlockSpec((n, TILE), lambda j: (0, j + first))

    def pack_spec(first):
        return pl.BlockSpec((1, rows, 2 * PER), lambda j: (j + first, 0, 0))

    def rowpack_spec(first):
        return pl.BlockSpec((1, blocks, 2 * PER, QLEN), lambda j: (j + first, 0, 0, 0))

    def entry_spec(first):
        return pl.BlockSpec((blocks, TILE, STATE), lambda j: (0, j + first, 0))

    def piece_tiles(pieces, first=0):
        return [
            pl.BlockSpec(p.shape[:2] + (TILE,), lambda j: (0, 0, j + first)) for p in pieces
        ]

    def value_part(first, count, past, deps):
        anywhere = [pl.BlockSpec(memory_space=pl.ANY)] * len(past)
        at = 3 + len(value_pieces) + 7
        return call(
            functools.partial(value_body, len(value_pieces), blocks, len(past)),
            (count,),
            [smem(), smem(), whole((rows, width))]
            + piece_tiles(value_pieces, first)
            + [
                tile_cols(KERNEL, first),
                tile_cols(1, first),
                pack_spec(first),
                rowpack_spec(first),
                whole((rows, STATE)),
                whole((rows, STATE)),
                whole((blocks, QLEN, QLEN)),
            ]
            + anywhere,
            [tile_cols(n, first) for n in (width, rows, rows, rows)] + [entry_spec(first)],
            [
                ((width, wide), BF),
                ((rows, wide), BF),
                ((rows, wide), BF),
                ((rows, wide), F32),
                ((blocks, wide, STATE), F32),
            ],
            [
                pltpu.VMEM((QLEN, TILE), F32),
                pltpu.VMEM((QLEN + 8, TILE), F32),
                pltpu.VMEM((TILE, STATE), F32),
            ],
            4 * rows * width * count * TILE,
            20 * rows * count * TILE,
            starts,
            keep,
            feat,
            *value_pieces,
            value_taps,
            skip_row,
            pack,
            rowpack,
            b_low,
            c_low,
            gram,
            *past,
            deps=deps,
            aliases={at + i: i for i in range(len(past))},
        )

    cut = tiles // 3
    scanned = value_part(0, cut, (), ())
    gate_held = links.ring_stack(gate_ring, scanned[2])
    proj_shard = tied(out_proj.T, gate_held)
    proj_ring = links.ring_parts(proj_shard)
    scanned = value_part(cut, tiles - cut, scanned, (gate_held, proj_shard))
    value_w, pre_low, act_low, out_rows, entry = scanned
    gate_pieces = links.gather_rest(gate_held, act_low, cot_got, *proj_ring[1:])
    proj_halves = links.ring_halves(proj_ring)
    proj_others = links.pair_halves(proj_halves)

    grad, grad_t = call(
        functools.partial(mask_body, half_blocks),
        (blocks,),
        [smem(), half_spec, half_spec, block_rows(1)],
        [block_rows(width), pl.BlockSpec((width, QLEN), lambda b: (0, b))],
        [((rows, width), BF), ((width, rows), BF)],
        [],
        rows * width,
        8 * rows * width,
        place,
        cotangent,
        cot_got,
        live.astype(BF),
        deps=(entry,),
    )

    gate_w, gate, squares = call(
        functools.partial(gate_body, len(gate_pieces)),
        (tiles,),
        [smem(), whole((rows, width))] + piece_tiles(gate_pieces) + [tile_cols(rows)],
        [tile_cols(width), tile_cols(rows), whole((rows, LANES))],
        [((width, wide), BF), ((rows, wide), BF), ((rows, LANES), F32)],
        [],
        2 * rows * width * wide,
        12 * rows * wide,
        starts,
        feat,
        *gate_pieces,
        out_rows,
    )
    square_sum = jnp.sum(squares, axis=1).reshape(8, rows // 8)
    square_sum = square_sum + over_tensor(tied(square_sum, *proj_others[:1]))
    scale = lax.rsqrt(square_sum / INNER + EPSILON).reshape(rows, 1)

    def outer_outs(columns):
        by_rows = columns % TILE != 0
        steps = 4 if by_rows else columns // TILE
        step = columns if by_rows else TILE
        at = (lambda j: (j, 0)) if by_rows else (lambda j: (0, j))
        high = width // steps if by_rows else width
        if not links.paired:
            return steps, at, high, step, [pl.BlockSpec((high, step), at)], [((width, columns), F32)]
        slots = devices // 2 // (steps if by_rows else 1)
        at_slots = (lambda j: (j, 0, 0)) if by_rows else (lambda j: (0, 0, j))
        spec = pl.BlockSpec((slots, height, step), at_slots)
        return steps, at, high, step, [spec] * 2, [((devices // 2, height, columns), BF)] * 2

    def outer(left, right, deps=()):
        columns = right.shape[1]
        steps, at, high, step, specs, outs = outer_outs(columns)
        by_rows = step == columns
        return call(
            outer_body,
            (steps,),
            [
                smem(),
                pl.BlockSpec((high, rows), at if by_rows else (lambda j: (0, 0))),
                pl.BlockSpec((rows, step), (lambda j: (0, 0)) if by_rows else at),
            ],
            specs,
            outs,
            [],
            2 * rows * width * columns,
            4 * width * columns,
            core,
            left,
            right,
            deps=deps,
        )

    specs, outs = outer_outs(wide)[4:]
    gated, *proj_parts = call(
        proj_body,
        (tiles,),
        [
            smem(),
            whole((width, rows)),
            tile_cols(rows),
            tile_cols(rows),
            whole((rows, 1)),
            tile_cols(1),
        ],
        [tile_cols(rows)] + specs,
        [((rows, wide), BF)] + outs,
        [],
        2 * rows * width * wide,
        14 * rows * wide,
        core,
        grad_t,
        out_rows,
        gate,
        scale,
        gate_row,
    )
    proj_parts = links.scatter_core(proj_parts)
    proj_others = [tied(x, gated) for x in proj_others]
    proj_pieces = links.join_halves(proj_halves, proj_others)

    def swapped(s, place_ref):
        return ((s // half_blocks + 1 - place_ref[0]) % 2) * half_blocks + s % half_blocks

    def swap_rows(n):
        return pl.BlockSpec((QLEN, n), lambda s, p, r: (swapped(s, p), 0))

    proj_w, branch_send, branch_own, row_dot = call(
        functools.partial(branch_body, len(proj_pieces)),
        (blocks,),
        [swap_rows(wide), swap_rows(width)] + [whole(p.shape) for p in proj_pieces],
        [
            whole((width, wide)),
            pl.BlockSpec((QLEN, width), lambda s, p, r: (jnp.minimum(s, half_blocks - 1), 0)),
            pl.BlockSpec((QLEN, width), lambda s, p, r: (jnp.maximum(s - half_blocks, 0), 0)),
            swap_rows(1),
        ],
        [
            ((width, wide), BF),
            ((half_rows, width), BF),
            ((half_rows, width), F32),
            ((rows, 1), F32),
        ],
        [],
        2 * rows * width * wide,
        8 * rows * wide,
        place,
        starts,
        gated,
        grad,
        *proj_pieces,
        prefetch=2,
    )
    row_total = row_dot.reshape(8, rows // 8)
    row_total = (row_total + over_tensor(row_total)).reshape(rows, 1)
    branch_got = over_tensor(branch_send)

    core_grad, gate_grad, channel_sums = call(
        gating_body,
        (tiles,),
        [
            whole((rows, width)),
            tile_cols(width),
            tile_cols(rows),
            tile_cols(rows),
            tile_cols(rows),
            whole((rows, 1)),
            whole((rows, 1)),
            tile_cols(1),
        ],
        [tile_cols(rows), tile_cols(rows), tile_cols(2)],
        [((rows, wide), BF), ((rows, wide), BF), ((2, wide), F32)],
        [],
        2 * rows * width * wide,
        14 * rows * wide,
        grad,
        proj_w,
        out_rows,
        gate,
        act_low,
        scale,
        row_total,
        gate_row,
        deps=(proj_parts[0],),
    )
    proj_parts = links.scatter_pair(proj_parts)
    gate_parts = outer(feat_t, gate_grad)
    proj_sum = links.scatter_ring(proj_parts)

    def scan_part(first, count, past, deps):
        summed = [whole((blocks, QLEN, QLEN)), whole((rows, STATE)), whole((rows, STATE))]
        return call(
            functools.partial(scan_body, blocks),
            (count,),
            [smem()]
            + [tile_cols(n, first) for n in (rows, rows, rows, rows, 1, KERNEL)]
            + [
                pack_spec(first),
                rowpack_spec(first),
                whole((rows, STATE)),
                whole((rows, STATE)),
                whole((blocks, QLEN, QLEN)),
                entry_spec(first),
            ]
            + (summed if past else []),
            [tile_cols(rows), tile_cols(KERNEL)]
            + summed
            + [pl.BlockSpec((1, rows, 4 * PER), lambda j: (j, 0, 0))],
            [
                ((rows, count * TILE), BF),
                ((KERNEL, count * TILE), F32),
                ((blocks, QLEN, QLEN), F32),
                ((rows, STATE), F32),
                ((rows, STATE), F32),
                ((count, rows, 4 * PER), F32),
            ],
            [
                pltpu.VMEM((QLEN + 8, TILE), F32),
                pltpu.VMEM((QLEN + 8, TILE), F32),
                pltpu.VMEM((TILE, STATE), F32),
            ],
            4 * rows * width * count * TILE,
            20 * rows * count * TILE,
            keep,
            core_grad,
            act_low,
            pre_low,
            out_rows,
            skip_row,
            value_taps,
            pack,
            rowpack,
            b_low,
            c_low,
            gram_t,
            entry,
            *past,
            deps=deps,
        )

    third = -(-tiles // 3)
    scan_a = scan_part(0, third, (), (gate_parts[0], proj_parts[0]))
    gate_parts = links.scatter_core(gate_parts)
    scan_b = scan_part(third, third, scan_a[2:5], (gate_parts[0],))
    early_grad = jnp.concatenate([scan_a[0], scan_b[0]], axis=1)
    early_parts = outer(feat_t, early_grad)
    scan_c = scan_part(
        2 * third, tiles - 2 * third, scan_b[2:5], (proj_sum, early_parts[0])
    )
    gate_parts = links.scatter_pair(gate_parts)
    early_parts = links.scatter_core(early_parts)
    scans = [scan_a, scan_b, scan_c]
    gram_grad, b_grad, c_grad = scan_c[2:5]
    taps_part = jnp.concatenate([part[1] for part in scans], axis=1)

    side_grad, sharetaps_part, head_sums = call(
        functools.partial(side_body, blocks),
        (1,),
        [
            smem(),
            whole((blocks, QLEN, QLEN)),
            whole((rows, STATE)),
            whole((rows, STATE)),
            whole((rows, STATE)),
            whole((rows, STATE)),
            whole((rows, TILE)),
            whole((KERNEL, TILE)),
            whole((3, rows, LANES)),
            whole((1, LANES)),
        ]
        + [whole(part[5].shape) for part in scans],
        [whole((rows, SIDE)), whole((KERNEL, TILE)), whole((2, LANES))],
        [((rows, SIDE), BF), ((KERNEL, TILE), F32), ((2, LANES), F32)],
        [pltpu.VMEM((QLEN + 8, TILE), F32), pltpu.VMEM((QLEN + 8, TILE), F32)],
        rows * width * STATE,
        20 * rows * TILE,
        keep,
        gram_grad,
        b_grad,
        c_grad,
        b_low,
        c_low,
        shared,
        shared_taps,
        cols,
        decay_row,
        *[part[5] for part in scans],
        deps=(gate_parts[0], early_parts[0]),
    )

    value_grads = [early_grad, scan_c[0]]

    def back(other, kind, deps=()):
        def at(s, p):
            half = (1 - p[0]) if other else p[0]
            return (half * half_blocks + s, 0)

        return call(
            functools.partial(back_body, len(value_grads)),
            (half_blocks,),
            [
                pl.BlockSpec((QLEN, wide), at),
                pl.BlockSpec((QLEN, SIDE), at),
                whole((width, wide)),
                whole((width, wide)),
                whole((width, SIDE)),
            ]
            + [pl.BlockSpec((QLEN, g.shape[1]), at) for g in value_grads],
            [block_rows(width)],
            [((half_rows, width), kind)],
            [],
            2 * rows * width * wide,
            16 * rows * wide,
            place,
            gate_grad,
            side_grad,
            gate_w,
            value_w,
            side_w,
            *value_grads,
            deps=deps,
            prefetch=1,
        )[0]

    late_grad = jnp.concatenate([scan_c[0], side_grad], axis=1)
    late_parts = outer(feat_t, late_grad)
    gate_sum = links.scatter_ring(gate_parts)
    early_parts = links.scatter_pair(early_parts)
    back_send = back(True, BF, (late_parts[0],))
    late_parts = links.scatter_core(late_parts)
    back_got = over_tensor(back_send)
    back_own = back(False, F32, (late_parts[0], early_parts[0]))
    late_parts = links.scatter_pair(late_parts, back_own)
    early_sum = links.scatter_ring(early_parts)
    late_sum = links.scatter_ring(late_parts)

    head_row = jnp.concatenate(
        [
            sharetaps_part.reshape(-1),
            head_sums[0, :heads],
            head_sums[1, :heads],
            jnp.sum(channel_sums[1].reshape(heads, HEAD_DIM), axis=1),
            jnp.zeros((wide - KERNEL * TILE - 3 * heads,), F32),
        ]
    ).reshape(1, wide)
    small = jnp.concatenate([taps_part, channel_sums[0:1], head_row], axis=0)
    small = links.reduce(small)
    sharetaps = small[5:6, : KERNEL * TILE]
    sharetaps = sharetaps + over_tensor(sharetaps)

    rest = wide - early_grad.shape[1]
    value_sum = jnp.concatenate([early_sum, late_sum[:, :rest]], axis=1)
    side_sum = late_sum[:, rest : rest + 2 * STATE + heads]
    side_shard = jnp.concatenate([in_shared, in_step], axis=1)
    norm_part = (
        jnp.sum(gate_sum * in_gate.astype(F32), axis=1, keepdims=True)
        + jnp.sum(value_sum * in_value.astype(F32), axis=1, keepdims=True)
        + jnp.sum(side_sum * side_shard.astype(F32), axis=1, keepdims=True)
    ) / norm_gain.astype(F32)[:, None]
    mixed = jnp.concatenate(
        [late_sum[:, rest : rest + 2 * STATE], jnp.broadcast_to(norm_part, (height, LANES))], axis=1
    )
    mixed = mixed + over_tensor(mixed)

    block_out = call(
        out_body,
        (half_blocks,),
        [block_rows(width)] * 3 + [block_rows(1)],
        [block_rows(width)],
        [((half_rows, width), BF)],
        [],
        half_rows * width,
        10 * half_rows * width,
        branch_own,
        branch_got,
        hidden_in,
        live_own,
        deps=(back_own,),
    )[0]
    input_grad = call(
        input_body,
        (half_blocks,),
        [block_rows(width)] * 4 + [whole((1, width))],
        [block_rows(width)],
        [((half_rows, width), BF)],
        [],
        half_rows * width,
        12 * half_rows * width,
        back_own,
        back_got,
        hidden_in,
        cotangent,
        gain_row,
        deps=(block_out,),
    )[0]
    share = KERNEL * TILE
    return (
        block_out,
        input_grad,
        mixed[:, 2 * STATE],
        gate_sum,
        value_sum,
        mixed[:, : 2 * STATE],
        side_sum[:, 2 * STATE :],
        small[0:KERNEL],
        sharetaps.reshape(KERNEL, TILE),
        small[5, share + heads : share + 2 * heads],
        small[5, share : share + heads],
        small[5, share + 2 * heads : share + 3 * heads],
        small[4],
        proj_sum.T,
    )


def solution(mesh):
    in_specs = (
        P(("dp", "tensor"), None),
        P("dp"),
        P("dp"),
        P("dp", "tensor"),
        P("dp", "tensor"),
        P("dp", None),
        P("dp", "tensor"),
        P(None, "tensor"),
        P(),
        P("tensor"),
        P("tensor"),
        P("tensor"),
        P("tensor"),
        P("tensor", "dp"),
        P(("dp", "tensor"), None),
    )
    out_specs = (
        P(("dp", "tensor"), None),
        P(("dp", "tensor"), None),
        P("dp"),
        P("dp", "tensor"),
        P("dp", "tensor"),
        P("dp", None),
        P("dp", "tensor"),
        P(None, "tensor"),
        P(),
        P("tensor"),
        P("tensor"),
        P("tensor"),
        P("tensor"),
        P("tensor", "dp"),
    )
    return jax.shard_map(
        functools.partial(on_device, devices=mesh.shape["dp"]),
        mesh=mesh,
        in_specs=in_specs,
        out_specs=out_specs,
        check_vma=False,
    )
```

```python
import functools

import jax
import jax.numpy as jnp
from jax import lax
from jax.experimental import pallas as pl
from jax.experimental.pallas import tpu as pltpu
from jax.sharding import PartitionSpec as P

HEAD_DIM = 64
STATE = 128
KERNEL = 4
QLEN = 256
INNER = 3072
EPSILON = 1e-05
TILE = 256
SIDE = 384
WIDE_TILE = 512
LANES = 128
HALF = QLEN // 2
PER = TILE // HEAD_DIM

BF = jnp.bfloat16
F32 = jnp.float32
HIGH = lax.Precision.HIGHEST
ROOM = 53 * 1024 * 1024
WEIGHT = 3


def dot(left, right, left_dim=1, right_dim=0, precision=None):
    return lax.dot_general(
        left,
        right,
        (((left_dim,), (right_dim,)), ((), ())),
        preferred_element_type=F32,
        precision=precision,
    )


def iota(shape, dim):
    return lax.broadcasted_iota(jnp.int32, shape, dim)


def split_dot(values, chooser):
    high = values.astype(BF)
    rest = (values - high.astype(F32)).astype(BF)
    return dot(high, chooser) + dot(rest, chooser)


def whole(shape):
    return pl.BlockSpec(shape, lambda *_: (0,) * len(shape))


def smem():
    return pl.BlockSpec(memory_space=pltpu.SMEM)


def call(
    body,
    grid,
    in_specs,
    out_specs,
    out_shape,
    scratch,
    flops,
    moved,
    *args,
    deps=(),
    prefetch=0,
    aliases=None,
):
    count = len(args)

    def held(*refs):
        body(*refs[:count], *refs[count + len(deps) :])

    anywhere = [pl.BlockSpec(memory_space=pl.ANY)] * len(deps)
    return pl.pallas_call(
        held,
        grid_spec=pltpu.PrefetchScalarGridSpec(
            num_scalar_prefetch=prefetch,
            grid=grid,
            in_specs=list(in_specs) + anywhere,
            out_specs=out_specs,
            scratch_shapes=scratch,
        ),
        out_shape=[jax.ShapeDtypeStruct(shape, kind) for shape, kind in out_shape],
        input_output_aliases=aliases or {},
        compiler_params=pltpu.CompilerParams(vmem_limit_bytes=ROOM),
        cost_estimate=pl.CostEstimate(
            flops=flops * WEIGHT, bytes_accessed=moved, transcendentals=0
        ),
    )(*args, *deps)


def tied(value, *deps):
    anywhere = pl.BlockSpec(memory_space=pl.ANY)
    return pl.pallas_call(
        lambda *refs: None,
        in_specs=[anywhere] * (1 + len(deps)),
        out_specs=anywhere,
        out_shape=jax.ShapeDtypeStruct(value.shape, value.dtype),
        input_output_aliases={0: 0},
        compiler_params=pltpu.CompilerParams(vmem_limit_bytes=ROOM),
    )(value, *deps)


def silu_slope(sigma, inputs):
    return sigma * (1.0 + inputs * (1.0 - sigma))


def expand(narrow):
    first = iota((QLEN, LANES), 1) < HEAD_DIM
    parts = []
    for pair in range(PER // 2):
        left = jnp.broadcast_to(narrow[:, 2 * pair : 2 * pair + 1], (QLEN, LANES))
        right = jnp.broadcast_to(narrow[:, 2 * pair + 1 : 2 * pair + 2], (QLEN, LANES))
        parts.append(jnp.where(first, left, right))
    return jnp.concatenate(parts, axis=1)


def head_rows(narrow):
    return jnp.concatenate(
        [jnp.broadcast_to(narrow[:, h : h + 1], (HEAD_DIM, STATE)) for h in range(PER)], axis=0
    )


def lane_masks():
    first = iota((1, LANES), 1) < HEAD_DIM
    return (first.astype(BF), jnp.logical_not(first).astype(BF))


def fill_weight(out_ref, rows_ref, pieces):
    at = 0
    for piece in pieces:
        count, height = piece.shape[0], piece.shape[1]
        for i in range(count):
            start = pl.multiple_of(rows_ref[at], 16) if height % 16 == 0 else rows_ref[at]
            out_ref[pl.ds(start, height), :] = piece[i]
            at += 1


def conv_sum(ext, taps):
    total = taps[KERNEL - 1 : KERNEL, :] * ext[8 : 8 + QLEN, :]
    for lag in range(1, KERNEL):
        total = total + taps[KERNEL - 1 - lag : KERNEL - lag, :] * ext[8 - lag : 8 - lag + QLEN, :]
    return total


def norm_body(
    half_blocks,
    pieces_total,
    gain_lane,
    rows_ref,
    place,
    keep,
    own,
    got,
    taps,
    bias,
    decay,
    *refs,
):
    pieces = refs[:pieces_total]
    (
        feat,
        feat_t,
        shared,
        b_out,
        c_out,
        gram,
        gram_t,
        cols,
        pack,
        rowpack,
        side_w,
        gain,
        hold,
        ext,
    ) = refs[pieces_total:]
    b = pl.program_id(0)
    mine = (b // half_blocks) == place[0]

    @pl.when(b == 0)
    def _():
        fill_weight(side_w, rows_ref, pieces)
        edge = gain_lane // LANES * LANES
        spread = side_w[:, edge : edge + LANES].astype(F32).T
        gain[...] = spread[gain_lane - edge : gain_lane - edge + 1, :]

    @pl.when(mine)
    def _():
        hold[...] = own[...].astype(F32)

    @pl.when(jnp.logical_not(mine))
    def _():
        hold[...] = got[...].astype(F32)

    rows = hold[...]
    inverse = lax.rsqrt(jnp.mean(rows * rows, axis=1, keepdims=True) + EPSILON)
    normed = (rows * inverse * gain[...]).astype(BF)
    feat[...] = normed
    feat_t[...] = normed.T
    side = dot(normed, side_w[...])
    pre = side[:, :TILE]
    shared[...] = pre

    @pl.when(b == 0)
    def _():
        ext[...] = jnp.zeros_like(ext)

    ext[0:8, :] = ext[QLEN : QLEN + 8, :] * keep[b]
    ext[8 : 8 + QLEN, :] = pre
    conv = conv_sum(ext, taps)
    act = (conv * jax.nn.sigmoid(conv)).astype(BF)
    b_low = act[:, :STATE]
    c_low = act[:, STATE:]
    b_out[...] = b_low
    c_out[...] = c_low
    lower = iota((QLEN, QLEN), 0) >= iota((QLEN, QLEN), 1)
    upper = iota((QLEN, QLEN), 0) <= iota((QLEN, QLEN), 1)
    gram[0] = jnp.where(lower, dot(c_low, b_low, 1, 1), 0.0)
    gram_t[0] = jnp.where(upper, dot(b_low, c_low, 1, 1), 0.0)
    raw = side[:, TILE:] + bias[...]
    step = jnp.maximum(raw, 0.0) + jnp.log1p(jnp.exp(-jnp.abs(raw)))
    logdec = step * -jnp.exp(decay[...])
    cum = dot(lower.astype(F32), logdec, precision=HIGH)
    cols[0] = raw
    cols[1] = step
    cols[2] = logdec
    cum_t = cum.T
    step_t = step.T
    for j in range(pack.shape[0]):
        heads = slice(PER * j, PER * j + PER)
        pack[j] = jnp.concatenate([cum[:, heads], step[:, heads]], axis=1)
        rowpack[j, 0] = jnp.concatenate([cum_t[heads, :], step_t[heads, :]], axis=0)


def value_body(
    pieces_total,
    blocks,
    past,
    rows_ref,
    keep,
    feat,
    *refs,
):
    pieces = refs[:pieces_total]
    refs = refs[: pieces_total + 7] + refs[pieces_total + 7 + past :]
    (
        taps,
        skip,
        pack,
        rowpack,
        b_ref,
        c_ref,
        gram,
        weight,
        pre_out,
        act_out,
        slope_out,
        out_rows,
        entry,
        pre,
        ext,
        state,
    ) = refs[pieces_total:]
    fill_weight(weight, rows_ref, pieces)
    masks = lane_masks()
    for b in range(blocks):
        span = slice(b * QLEN, (b + 1) * QLEN)
        pre[...] = dot(feat[span, :], weight[...])
        pre_out[span, :] = pre[...].astype(BF)
        if b == 0:
            ext[0:8, :] = jnp.zeros((8, TILE), F32)
            state[...] = jnp.zeros_like(state)
        else:
            ext[0:8, :] = ext[QLEN : QLEN + 8, :] * keep[b]
        ext[8 : 8 + QLEN, :] = pre[...]
        conv = conv_sum(ext, taps)
        sigma = jax.nn.sigmoid(conv)
        act_low = (conv * sigma).astype(BF)
        act_out[span, :] = act_low
        slope_out[span, :] = silu_slope(sigma, conv).astype(BF)
        act = act_low.astype(F32)
        narrow = pack[0, span, :]
        cum = narrow[:, :PER]
        step = narrow[:, PER:]
        last = cum[QLEN - 1 : QLEN, :]
        stepped = (act * expand(step)).astype(BF)
        scaled = (act * expand(jnp.exp(last - cum) * step)).astype(BF)
        row_cum = rowpack[0, b]
        parts = []
        for pair in range(PER // 2):
            lanes = slice(pair * LANES, (pair + 1) * LANES)
            tops, lows, values = [], [], []
            for k in range(2):
                h = 2 * pair + k
                col = cum[:, h : h + 1]
                row = row_cum[h : h + 1, :]
                e00 = jnp.exp(jnp.minimum(col[:HALF] - row[:, :HALF], 0.0))
                e10 = jnp.exp(col[HALF:] - row[:, :HALF])
                e11 = jnp.exp(jnp.minimum(col[HALF:] - row[:, HALF:], 0.0))
                tops.append((gram[b, :HALF, :HALF] * e00).astype(BF))
                lows.append((gram[b, HALF:, :HALF] * e10).astype(BF))
                lows.append((gram[b, HALF:, HALF:] * e11).astype(BF))
                values.append(stepped[:, lanes] * masks[k])
            top = dot(
                jnp.concatenate(tops, axis=1),
                jnp.concatenate([v[:HALF] for v in values], axis=0),
            )
            low = dot(jnp.concatenate(lows, axis=1), jnp.concatenate(values, axis=0))
            parts.append(jnp.concatenate([top, low], axis=0))
        within = jnp.concatenate(parts, axis=1)
        held = state[...]
        entry[b] = held
        across = dot(c_ref[span, :], held.astype(BF), 1, 1)
        core = within + across * expand(jnp.exp(cum))
        out_rows[span, :] = core + act * skip[...]
        if b + 1 < blocks:
            fresh = dot(scaled, b_ref[span, :], 0, 0)
            state[...] = keep[b + 1] * (head_rows(jnp.exp(last)) * held + fresh)


def gate_body(pieces_total, rows_ref, feat, *refs):
    pieces = refs[:pieces_total]
    out_rows, _, weight, gate_out, squares = refs[pieces_total:]
    fill_weight(weight, rows_ref, pieces)

    @pl.when(pl.program_id(0) == 0)
    def _():
        squares[...] = jnp.zeros_like(squares)

    for b in range(feat.shape[0] // QLEN):
        span = slice(b * QLEN, (b + 1) * QLEN)
        gate = dot(feat[span, :], weight[...])
        gate_out[span, :] = gate.astype(BF)
        product = out_rows[span, :] * (gate * jax.nn.sigmoid(gate))
        power = product * product
        total = squares[span, :]
        for at in range(0, power.shape[1], LANES):
            total = total + power[:, at : at + LANES]
        squares[span, :] = total


def mask_body(half_blocks, place, own, got, live, out, out_t):
    b = pl.program_id(0)
    mine = (b // half_blocks) == place[0]

    @pl.when(mine)
    def _():
        out[...] = own[...] * live[...]

    @pl.when(jnp.logical_not(mine))
    def _():
        out[...] = got[...] * live[...]

    out_t[...] = out[...].T


def proj_body(place, left, out_rows, gate_ref, scale_ref, gain, gated_out, *outs):
    for b in range(gated_out.shape[0] // QLEN):
        span = slice(b * QLEN, (b + 1) * QLEN)
        gate = gate_ref[span, :].astype(F32)
        product = out_rows[span, :] * (gate * jax.nn.sigmoid(gate))
        gated_out[span, :] = (product * scale_ref[span, :] * gain[...]).astype(BF)
    emit_outer(place, dot(left[...], gated_out[...]), outs)


def branch_body(pieces_total, place, rows_ref, gated, grad, *refs):
    pieces = refs[:pieces_total]
    weight, send, mine, row_dot = refs[pieces_total:]
    s = pl.program_id(0)

    @pl.when(s == 0)
    def _():
        fill_weight(weight, rows_ref, pieces)

    branch = dot(gated[...], weight[...], 1, 1)
    row_dot[...] = jnp.sum(branch * grad[...].astype(F32), axis=1, keepdims=True)

    @pl.when(s < pl.num_programs(0) // 2)
    def _():
        send[...] = branch.astype(BF)

    @pl.when(s >= pl.num_programs(0) // 2)
    def _():
        mine[...] = branch


def gating_body(
    place,
    grad,
    weight,
    out_ref,
    gate_ref,
    act_ref,
    scale_ref,
    row_dot,
    gain,
    feat_t,
    _,
    core,
    gate_grad,
    sums,
    *outs,
):
    gating = jnp.zeros(gain.shape, F32)
    skipping = jnp.zeros(gain.shape, F32)
    for b in range(grad.shape[0] // QLEN):
        span = slice(b * QLEN, (b + 1) * QLEN)
        grad_gated = dot(grad[span, :], weight[...])
        gate = gate_ref[span, :].astype(F32)
        sigma = jax.nn.sigmoid(gate)
        act = gate * sigma
        out_rows = out_ref[span, :]
        scale = scale_ref[span, :]
        normal = out_rows * act * scale
        gating = gating + jnp.sum(grad_gated * normal, axis=0, keepdims=True)
        grad_product = scale * (
            grad_gated * gain[...] - normal * (row_dot[span, :] * (1.0 / INNER))
        )
        grad_out = grad_product * act
        core[span, :] = grad_out.astype(BF)
        gate_grad[span, :] = (grad_product * out_rows * silu_slope(sigma, gate)).astype(BF)
        skipping = skipping + jnp.sum(
            grad_out * act_ref[span, :].astype(F32), axis=0, keepdims=True
        )
    sums[...] = jnp.concatenate([gating, skipping], axis=0)
    emit_outer(place, dot(feat_t[...], gate_grad[...]), outs)


def scan_body(
    blocks,
    summed,
    outer_outs,
    place,
    keep,
    feat_t,
    slope_ref,
    core_ref,
    act_ref,
    pre_ref,
    out_ref,
    skip,
    taps,
    pack,
    rowpack,
    b_ref,
    c_ref,
    gram_t,
    entry,
    *refs,
):
    past = refs[:3] if summed else ()
    own = len(refs) - 9 - outer_outs
    outs = refs[own : own + outer_outs]
    grad_pre, taps_grad, gram_grad, b_grad, c_grad, stats = refs[own + outer_outs : -3]
    ext, tail, carry = refs[-3:]

    @pl.when(pl.program_id(0) == 0)
    def _():
        if past:
            gram_grad[...] = past[0][...]
            b_grad[...] = past[1][...]
            c_grad[...] = past[2][...]
        else:
            gram_grad[...] = jnp.zeros_like(gram_grad)
            b_grad[...] = jnp.zeros_like(b_grad)
            c_grad[...] = jnp.zeros_like(c_grad)

    masks = lane_masks()
    owner = iota((TILE, LANES), 0) // HEAD_DIM
    lane = iota((TILE, LANES), 1)
    chooser = [(lane == owner + PER * q).astype(BF) for q in range(4)]
    final_row = iota((QLEN, LANES), 0) == QLEN - 1
    ones = jnp.ones((8, STATE), BF)
    tap_sums = [jnp.zeros((1, TILE), F32) for _ in range(KERNEL)]
    for b in reversed(range(blocks)):
        span = slice(b * QLEN, (b + 1) * QLEN)
        final = b == blocks - 1
        grad_low = core_ref[span, :]
        grad = grad_low.astype(F32)
        act = act_ref[span, :].astype(F32)
        narrow = pack[0, span, :]
        cum = narrow[:, :PER]
        step = narrow[:, PER:]
        last = cum[QLEN - 1 : QLEN, :]
        step_wide = expand(step)
        stepped = (act * step_wide).astype(BF)
        row_cum = rowpack[0, b]
        parts = []
        upper_sum = None
        lower_sum = None
        for pair in range(PER // 2):
            lanes = slice(pair * LANES, (pair + 1) * LANES)
            grad_pair = grad_low[:, lanes]
            tops, lows, grads = [], [], []
            for k in range(2):
                h = 2 * pair + k
                col = cum[:, h : h + 1]
                row = row_cum[h : h + 1, :]
                e00 = jnp.exp(jnp.minimum(row[:, :HALF] - col[:HALF], 0.0))
                e01 = jnp.exp(row[:, HALF:] - col[:HALF])
                e11 = jnp.exp(jnp.minimum(row[:, HALF:] - col[HALF:], 0.0))
                value = stepped[:, lanes] * masks[k]
                upper = dot(value[:HALF], grad_pair, 1, 1) * jnp.concatenate([e00, e01], axis=1)
                lower = dot(value[HALF:], grad_pair[HALF:], 1, 1) * e11
                upper_sum = upper if upper_sum is None else upper_sum + upper
                lower_sum = lower if lower_sum is None else lower_sum + lower
                tops.append((gram_t[b, :HALF, :HALF] * e00).astype(BF))
                tops.append((gram_t[b, :HALF, HALF:] * e01).astype(BF))
                lows.append((gram_t[b, HALF:, HALF:] * e11).astype(BF))
                grads.append(grad_pair * masks[k])
            top = dot(jnp.concatenate(tops, axis=1), jnp.concatenate(grads, axis=0))
            low = dot(
                jnp.concatenate(lows, axis=1),
                jnp.concatenate([g[HALF:] for g in grads], axis=0),
            )
            parts.append(jnp.concatenate([top, low], axis=0))
        gram_grad[b, :HALF, :] += upper_sum
        gram_grad[b, HALF:, HALF:] += lower_sum
        mixed = jnp.concatenate(parts, axis=1)
        between = out_ref[span, :] - act * skip[...]
        flows = stepped.astype(F32) * mixed
        grad_value = step_wide * mixed + skip[...] * grad
        held = entry[b]
        across_low = (grad * expand(jnp.exp(cum))).astype(BF)
        c_grad[span, :] += dot(across_low, held.astype(BF))
        totals = split_dot(grad * between, chooser[1])
        if not final:
            states = carry[...]
            states_low = states.astype(BF)
            weights = expand(jnp.exp(last - cum) * step)
            pulled = dot(b_ref[span, :], states_low, 1, 1) * weights
            grad_value = grad_value + pulled
            weighted = act * pulled
            scaled = (act * weights).astype(BF)
            b_grad[span, :] += dot(scaled, states_low)
            totals = totals + split_dot(flows + weighted, chooser[0])
            totals = totals + split_dot(weighted, chooser[2])
            passed = head_rows(jnp.exp(last)) * states
            spread = passed * held
            high = spread.astype(BF)
            rest = (spread - high.astype(F32)).astype(BF)
            summed = dot(ones, high, 1, 1) + dot(ones, rest, 1, 1)
            last_sum = split_dot(summed, chooser[3])
            totals = totals + jnp.where(final_row, last_sum[0:1, :], 0.0)
        else:
            totals = totals + split_dot(flows, chooser[0])
        stats[0, span, :] = totals[:, : 4 * PER]
        if b > 0:
            fresh = dot(across_low, c_ref[span, :], 0, 0)
            carry[...] = keep[b] * (fresh if final else fresh + passed)
        if b > 0:
            ext[0:8, :] = pre_ref[b * QLEN - 16 : b * QLEN, :].astype(F32)[8:, :] * keep[b]
        else:
            ext[0:8, :] = jnp.zeros((8, TILE), F32)
        ext[8 : 8 + QLEN, :] = pre_ref[span, :].astype(F32)
        slope = grad_value * slope_ref[span, :].astype(F32)
        for lag in range(KERNEL):
            tap_sums[KERNEL - 1 - lag] = tap_sums[KERNEL - 1 - lag] + jnp.sum(
                slope * ext[8 - lag : 8 - lag + QLEN, :], axis=0, keepdims=True
            )
        if final:
            tail[QLEN : QLEN + 8, :] = jnp.zeros((8, TILE), F32)
        else:
            tail[QLEN : QLEN + 8, :] = tail[0:8, :] * keep[b + 1]
        tail[0:QLEN, :] = slope
        pulled_back = taps[KERNEL - 1 : KERNEL, :] * slope
        for lag in range(1, KERNEL):
            pulled_back = (
                pulled_back
                + taps[KERNEL - 1 - lag : KERNEL - lag, :] * tail[lag : lag + QLEN, :]
            )
        grad_pre[span, :] = pulled_back.astype(BF)
    taps_grad[...] = jnp.concatenate(tap_sums, axis=0)
    emit_outer(place, dot(feat_t[...], grad_pre[...]), outs)


def side_body(
    blocks,
    tiles_total,
    aliased,
    place,
    keep,
    feat_hbm,
    gram_grad,
    b_grad,
    c_grad,
    b_ref,
    c_ref,
    shared,
    taps,
    cols,
    decay,
    *refs,
):
    stats = refs[:tiles_total]
    outs = refs[tiles_total + 1 + aliased : -10]
    out, taps_grad, sums, ext, tail, feat_t, first, second, feat_sem, sems = refs[-10:]
    loading = pltpu.make_async_copy(feat_hbm, feat_t, feat_sem)
    loading.start()
    lower = iota((QLEN, QLEN), 0) >= iota((QLEN, QLEN), 1)
    upper = iota((QLEN, QLEN), 0) <= iota((QLEN, QLEN), 1)
    final_row = iota((QLEN, LANES), 0) == QLEN - 1
    rate = jnp.exp(decay[...])
    tap_sums = [jnp.zeros((1, TILE), F32) for _ in range(KERNEL)]
    decay_sum = jnp.zeros((1, LANES), F32)
    bias_sum = jnp.zeros((1, LANES), F32)
    tiles = sum(part.shape[0] for part in stats)
    padding = jnp.zeros((QLEN, LANES - PER * tiles), F32)
    for b in reversed(range(blocks)):
        span = slice(b * QLEN, (b + 1) * QLEN)
        final = b == blocks - 1
        gathered = [
            jnp.concatenate(
                [
                    part[j, span, PER * q : PER * q + PER]
                    for part in stats
                    for j in range(part.shape[0])
                ]
                + [padding],
                axis=1,
            )
            for q in range(4)
        ]
        pulled = gathered[0]
        grad_cum = gathered[1] - pulled + gathered[3]
        grad_cum = grad_cum + jnp.where(
            final_row, jnp.sum(gathered[2], axis=0, keepdims=True), 0.0
        )
        grad_log = dot(upper.astype(F32), grad_cum, precision=HIGH)
        raw = cols[0, span, :]
        step = cols[1, span, :]
        sigma = jax.nn.sigmoid(raw)
        ratio = jnp.where(raw < -20.0, 1.0, sigma / jnp.maximum(step, 1e-30))
        grad_raw = pulled * ratio - rate * grad_log * sigma
        decay_sum = decay_sum + jnp.sum(grad_log * cols[2, span, :], axis=0, keepdims=True)
        bias_sum = bias_sum + jnp.sum(grad_raw, axis=0, keepdims=True)
        out[span, TILE:] = grad_raw.astype(BF)
        gram_low = jnp.where(upper, gram_grad[b], 0.0).astype(BF)
        b_total = b_grad[span, :] + dot(gram_low, c_ref[span, :])
        c_total = c_grad[span, :] + dot(gram_low, b_ref[span, :], 0, 0)
        grad_act = jnp.concatenate([b_total, c_total], axis=1)
        if b > 0:
            ext[0:8, :] = shared[b * QLEN - 8 : b * QLEN, :] * keep[b]
        else:
            ext[0:8, :] = jnp.zeros((8, TILE), F32)
        ext[8 : 8 + QLEN, :] = shared[span, :]
        conv = conv_sum(ext, taps)
        slope = grad_act * silu_slope(jax.nn.sigmoid(conv), conv)
        for lag in range(KERNEL):
            tap_sums[KERNEL - 1 - lag] = tap_sums[KERNEL - 1 - lag] + jnp.sum(
                slope * ext[8 - lag : 8 - lag + QLEN, :], axis=0, keepdims=True
            )
        if final:
            tail[QLEN : QLEN + 8, :] = jnp.zeros((8, TILE), F32)
        else:
            tail[QLEN : QLEN + 8, :] = tail[0:8, :] * keep[b + 1]
        tail[0:QLEN, :] = slope
        pulled_back = taps[KERNEL - 1 : KERNEL, :] * slope
        for lag in range(1, KERNEL):
            pulled_back = (
                pulled_back
                + taps[KERNEL - 1 - lag : KERNEL - lag, :] * tail[lag : lag + QLEN, :]
            )
        out[span, :TILE] = pulled_back.astype(BF)
    taps_grad[...] = jnp.concatenate(tap_sums, axis=0)
    sums[...] = jnp.concatenate([decay_sum, bias_sum], axis=0)
    loading.wait()
    held = (first, second)[: len(outs)]
    emit_outer(place, dot(feat_t[...], out[...]), held)
    moves = []
    for i, (target, source) in enumerate(zip(outs, held)):
        start = target.shape[-1] - SIDE
        view = target.at[..., pl.ds(start, SIDE)]
        moves.append(pltpu.make_async_copy(source, view, sems.at[i]))
    for move in moves:
        move.start()
    for move in moves:
        move.wait()


def emit_outer(place, total, outs):
    if len(outs) == 1:
        outs[0][...] = total.astype(outs[0].dtype)
        return
    mine, send = outs
    low = total.astype(BF).reshape(mine.shape[0], 2, mine.shape[1], total.shape[1])

    @pl.when(place[0] == 0)
    def _():
        mine[...] = low[:, 0]
        send[...] = low[:, 1]

    @pl.when(place[0] == 1)
    def _():
        mine[...] = low[:, 1]
        send[...] = low[:, 0]


def outer_body(place, left, right, *outs):
    emit_outer(place, dot(left[...], right[...]), outs)


def back_body(place, grads, weights, out):
    out[...] = dot(grads[...], weights[...], 1, 1).astype(out.dtype)


def input_body(mine, got, hidden, cot, gain, out):
    total = (mine[...] + got[...].astype(F32)) * gain[...]
    rows = hidden[...].astype(F32)
    inverse = lax.rsqrt(jnp.mean(rows * rows, axis=1, keepdims=True) + EPSILON)
    hat = rows * inverse
    spread = jnp.mean(total * hat, axis=1, keepdims=True)
    out[...] = (cot[...].astype(F32) + (total - hat * spread) * inverse).astype(BF)


def out_body(mine, got, hidden, live, out):
    out[...] = (
        hidden[...].astype(F32) + live[...] * (mine[...] + got[...].astype(F32))
    ).astype(BF)


class Links:
    def __init__(self, devices, shard_rows):
        self.devices = devices
        self.height = shard_rows
        self.paired = devices % 4 == 0 and shard_rows % 16 == 0
        self.ring = max(devices // 4, 1)
        spot = lax.axis_index("dp")
        self.a, self.b, self.c = spot // 4, (spot // 2) % 2, spot % 2
        self.spot = spot

    def moved(self, rule):
        pairs = []
        for a in range(self.ring):
            for b in range(2):
                for c in range(2):
                    ta, tb, tc = rule(a, b, c)
                    pairs.append(((a * 2 + b) * 2 + c, (ta * 2 + tb) * 2 + tc))
        return pairs

    def over_core(self, x):
        return lax.ppermute(x, "dp", self.moved(lambda a, b, c: (a, b, 1 - c)))

    def over_pair(self, x):
        return lax.ppermute(x, "dp", self.moved(lambda a, b, c: (a, 1 - b, c)))

    def over_ring(self, x, k):
        return lax.ppermute(x, "dp", self.moved(lambda a, b, c: ((a + k) % self.ring, b, c)))

    def gather_fast(self, shard):
        if not self.paired:
            return [lax.all_gather(shard, "dp", axis=0, tiled=True)[None]], (shard,)
        near = [k for k in range(1, self.ring) if k in (1, self.ring - 1)]
        far = [k for k in range(1, self.ring) if k not in near]
        held = {0: shard}
        other = {0: self.over_pair(shard)}
        for k in near:
            held[k] = self.over_ring(shard, k)
        later = tied(shard, other[0], *[held[k] for k in near])
        for k in far:
            held[k] = self.over_ring(later, k)
        for k in near + far:
            other[k] = self.over_pair(held[k])
        pieces = [held[k] for k in range(self.ring)] + [other[k] for k in range(self.ring)]
        pieces = pieces + [self.over_core(x) for x in pieces]
        return [x[None] for x in pieces], (held[(near + far)[-1]], other[near[0]])

    def ring_parts(self, shard):
        if not self.paired:
            return [shard]
        return [shard] + [self.over_ring(shard, k) for k in range(1, self.ring)]

    def ring_stack(self, parts, *deps):
        if not self.paired:
            return parts[0]
        return jnp.stack(parts[:-1] + [tied(parts[-1], *deps)])

    def gather_rest(self, held, *deps):
        if not self.paired:
            return [lax.all_gather(held, "dp", axis=0, tiled=True)[None]]
        other = tied(self.over_pair(held), *deps)
        return [held, other, self.over_core(held), self.over_core(other)]

    def ring_halves(self, parts):
        if not self.paired:
            return [parts[0]]
        cut = max(self.ring // 2, 1)
        return [jnp.stack(parts[:cut])] + ([jnp.stack(parts[cut:])] if parts[cut:] else [])

    def pair_halves(self, halves):
        return [self.over_pair(h) for h in halves] if self.paired else []

    def join_halves(self, halves, others):
        if not self.paired:
            return [lax.all_gather(halves[0], "dp", axis=0, tiled=True)[None]]
        pieces = halves + others
        return pieces + [self.over_core(x) for x in pieces]

    def starts(self):
        if not self.paired:
            return jnp.zeros((1,), jnp.int32)
        rows = []
        for c in (self.c, 1 - self.c):
            for b in (self.b, 1 - self.b):
                for k in range(self.ring):
                    a = lax.rem(self.a - k + self.ring, self.ring)
                    rows.append(((a * 2 + b) * 2 + c) * self.height)
        return jnp.stack(rows).astype(jnp.int32)

    def scatter_core(self, parts, *deps):
        if not self.paired:
            return parts
        mine, send = parts
        send = tied(send, *deps) if deps else send
        shape = (self.ring, 2) + mine.shape[1:]
        got = self.over_core(send)
        mine, got = mine.reshape(shape), got.reshape(shape)
        away = self.pick(mine, 1 - self.b, 1).astype(F32) + self.pick(got, 1 - self.b, 1).astype(F32)
        return [away.astype(BF), mine, got]

    def pick(self, x, i, dim):
        return lax.dynamic_index_in_dim(x, i, dim, keepdims=False)

    def scatter_pair(self, parts, *deps):
        if not self.paired:
            return parts
        away, mine, got = parts
        near = tied(self.over_pair(away), *deps) if deps else self.over_pair(away)

        total = self.pick(mine, self.b, 1).astype(F32) + self.pick(got, self.b, 1).astype(F32)
        return [(total + near.astype(F32)).astype(BF)]

    def over_rings(self, x):
        groups = [
            [(a * 2 + b) * 2 + c for a in range(self.ring)] for b in range(2) for c in range(2)
        ]
        return lax.all_to_all(x, "dp", 0, 0, tiled=True, axis_index_groups=groups)

    def scatter_ring(self, parts, *deps):
        if not self.paired:
            return lax.psum_scatter(parts[0], "dp", scatter_dimension=0, tiled=True)
        moved = self.over_rings(parts[0])
        if deps:
            moved = tied(moved, *deps)
        return jnp.sum(moved.astype(F32), axis=0)

    def reduce(self, x, first, second):
        if not self.paired:
            return lax.psum(x, "dp")
        x = tied(x + self.over_core(x), first)
        x = tied(x + self.over_pair(x), second)
        total = x
        for k in range(1, self.ring):
            total = total + self.over_ring(x, k)
        return total


def over_tensor(x):
    return lax.ppermute(x, "tensor", [(0, 1), (1, 0)])


def on_device(
    hidden_in,
    segment,
    norm_gain,
    in_gate,
    in_value,
    in_shared,
    in_step,
    value_taps,
    shared_taps,
    step_bias,
    decay_log,
    skip_gain,
    gate_gain,
    out_proj,
    cotangent,
    devices,
):
    half_rows, width = hidden_in.shape
    rows = segment.shape[0]
    blocks = rows // QLEN
    half_blocks = half_rows // QLEN
    wide = in_value.shape[1]
    tiles = wide // TILE
    heads = step_bias.shape[0]
    height = in_value.shape[0]
    links = Links(devices, height)
    tensor = lax.axis_index("tensor")
    place = jnp.reshape(tensor, (1,)).astype(jnp.int32)
    core = jnp.reshape(links.c, (1,)).astype(jnp.int32)

    firsts = segment[::QLEN]
    keep = jnp.concatenate(
        [jnp.zeros((1,), F32), (firsts[1:] == firsts[:-1]).astype(F32)]
    )
    live = (segment >= 0).astype(F32)[:, None]
    live_own = lax.dynamic_slice_in_dim(live, tensor * half_rows, half_rows)
    pad = SIDE - 2 * STATE - heads - 1
    value_shard = jnp.concatenate(
        [in_value, in_shared, in_step, norm_gain[:, None], jnp.zeros((height, pad), BF)], axis=1
    )
    hidden_got = over_tensor(hidden_in)
    starts = links.starts()
    value_pieces, value_last = links.gather_fast(value_shard)
    gate_shard = tied(in_gate, *value_last)
    gate_ring = links.ring_parts(gate_shard)
    cot_sent = tied(cotangent, hidden_got)
    cot_got = over_tensor(cot_sent)

    bias_row = jnp.pad(step_bias, (0, LANES - heads)).reshape(1, LANES)
    decay_row = jnp.pad(decay_log, (0, LANES - heads)).reshape(1, LANES)
    skip_row = jnp.repeat(skip_gain, HEAD_DIM).reshape(1, wide)
    gate_row = gate_gain.reshape(1, wide)

    block_rows = lambda n: pl.BlockSpec((QLEN, n), lambda b, *_: (b, 0))
    half_spec = pl.BlockSpec((QLEN, width), lambda b, *_: (b % half_blocks, 0))
    (
        feat,
        feat_t,
        shared,
        b_low,
        c_low,
        gram,
        gram_t,
        cols,
        pack,
        rowpack,
        all_w,
        gain_row,
    ) = call(
        functools.partial(norm_body, half_blocks, len(value_pieces), 2 * STATE + heads),
        (blocks,),
        [
            smem(),
            smem(),
            smem(),
            half_spec,
            half_spec,
            whole((KERNEL, TILE)),
            whole((1, LANES)),
            whole((1, LANES)),
        ]
        + [
            pl.BlockSpec(p.shape[:2] + (SIDE,), lambda b: (0, 0, wide // SIDE))
            for p in value_pieces
        ],
        [
            block_rows(width),
            pl.BlockSpec((width, QLEN), lambda b: (0, b)),
            block_rows(TILE),
            block_rows(STATE),
            block_rows(STATE),
            pl.BlockSpec((1, QLEN, QLEN), lambda b: (b, 0, 0)),
            pl.BlockSpec((1, QLEN, QLEN), lambda b: (b, 0, 0)),
            pl.BlockSpec((3, QLEN, LANES), lambda b: (0, b, 0)),
            pl.BlockSpec((tiles, QLEN, 2 * PER), lambda b: (0, b, 0)),
            pl.BlockSpec((tiles, 1, 2 * PER, QLEN), lambda b: (0, b, 0, 0)),
            pl.BlockSpec((width, SIDE), lambda b: (0, 2 * wide // SIDE)),
            whole((1, width)),
        ],
        [
            ((rows, width), BF),
            ((width, rows), BF),
            ((rows, TILE), F32),
            ((rows, STATE), BF),
            ((rows, STATE), BF),
            ((blocks, QLEN, QLEN), F32),
            ((blocks, QLEN, QLEN), F32),
            ((3, rows, LANES), F32),
            ((tiles, rows, 2 * PER), F32),
            ((tiles, blocks, 2 * PER, QLEN), F32),
            ((width, 2 * wide + SIDE), BF),
            ((1, width), F32),
        ],
        [pltpu.VMEM((QLEN, width), F32), pltpu.VMEM((QLEN + 8, TILE), F32)],
        2 * rows * width * SIDE,
        20 * rows * width,
        starts,
        place,
        keep,
        hidden_in,
        hidden_got,
        shared_taps,
        bias_row,
        decay_row,
        *value_pieces,
        deps=(gate_shard, cot_sent),
    )

    def tile_cols(n, first=0):
        return pl.BlockSpec((n, TILE), lambda j: (0, j + first))

    def pack_spec(first):
        return pl.BlockSpec((1, rows, 2 * PER), lambda j: (j + first, 0, 0))

    def rowpack_spec(first):
        return pl.BlockSpec((1, blocks, 2 * PER, QLEN), lambda j: (j + first, 0, 0, 0))

    def entry_spec(first):
        return pl.BlockSpec((blocks, TILE, STATE), lambda j: (0, j + first, 0))

    def piece_tiles(pieces, first=0):
        return [
            pl.BlockSpec(p.shape[:2] + (TILE,), lambda j: (0, 0, j + first)) for p in pieces
        ]

    def value_part(first, count, past, deps):
        anywhere = [pl.BlockSpec(memory_space=pl.ANY)] * len(past)
        at = 3 + len(value_pieces) + 7
        return call(
            functools.partial(value_body, len(value_pieces), blocks, len(past)),
            (count,),
            [smem(), smem(), whole((rows, width))]
            + piece_tiles(value_pieces, first)
            + [
                tile_cols(KERNEL, first),
                tile_cols(1, first),
                pack_spec(first),
                rowpack_spec(first),
                whole((rows, STATE)),
                whole((rows, STATE)),
                whole((blocks, QLEN, QLEN)),
            ]
            + anywhere,
            [tile_cols(n, first) for n in (width, rows, rows, rows, rows)] + [entry_spec(first)],
            [
                ((width, 2 * wide + SIDE), BF),
                ((rows, wide), BF),
                ((rows, wide), BF),
                ((rows, wide), BF),
                ((rows, wide), F32),
                ((blocks, wide, STATE), F32),
            ],
            [
                pltpu.VMEM((QLEN, TILE), F32),
                pltpu.VMEM((QLEN + 8, TILE), F32),
                pltpu.VMEM((TILE, STATE), F32),
            ],
            4 * rows * width * count * TILE,
            20 * rows * count * TILE,
            starts,
            keep,
            feat,
            *value_pieces,
            value_taps,
            skip_row,
            pack,
            rowpack,
            b_low,
            c_low,
            gram,
            *past,
            deps=deps,
            aliases={at + i: i for i in range(len(past))},
        )

    cut = tiles // 3
    scanned = value_part(0, cut, (all_w,), ())
    gate_held = links.ring_stack(gate_ring, scanned[2])
    proj_shard = tied(out_proj.T, gate_held)
    proj_ring = links.ring_parts(proj_shard)
    scanned = value_part(cut, tiles - cut, scanned, (gate_held, proj_shard))
    all_w, pre_low, act_low, slope_low, out_rows, entry = scanned
    gate_pieces = links.gather_rest(gate_held, act_low, cot_got, *proj_ring[1:])
    proj_halves = links.ring_halves(proj_ring)
    proj_others = links.pair_halves(proj_halves)

    grad, grad_t = call(
        functools.partial(mask_body, half_blocks),
        (blocks,),
        [smem(), half_spec, half_spec, block_rows(1)],
        [block_rows(width), pl.BlockSpec((width, QLEN), lambda b: (0, b))],
        [((rows, width), BF), ((width, rows), BF)],
        [],
        rows * width,
        8 * rows * width,
        place,
        cotangent,
        cot_got,
        live.astype(BF),
        deps=(entry,),
    )

    broad = wide // WIDE_TILE

    def broad_cols(n, first=0):
        return pl.BlockSpec((n, WIDE_TILE), lambda j: (0, j + first))

    all_w, gate, squares = call(
        functools.partial(gate_body, len(gate_pieces)),
        (broad,),
        [smem(), whole((rows, width))]
        + [pl.BlockSpec(p.shape[:2] + (WIDE_TILE,), lambda j: (0, 0, j)) for p in gate_pieces]
        + [broad_cols(rows), pl.BlockSpec(memory_space=pl.ANY)],
        [broad_cols(width, broad), broad_cols(rows), whole((rows, LANES))],
        [((width, 2 * wide + SIDE), BF), ((rows, wide), BF), ((rows, LANES), F32)],
        [],
        2 * rows * width * wide,
        12 * rows * wide,
        starts,
        feat,
        *gate_pieces,
        out_rows,
        all_w,
        aliases={3 + len(gate_pieces): 0},
    )
    square_sum = jnp.sum(squares, axis=1).reshape(8, rows // 8)
    square_sum = square_sum + over_tensor(tied(square_sum, *proj_others[:1]))
    scale = lax.rsqrt(square_sum / INNER + EPSILON).reshape(rows, 1)

    def outer_outs(columns, step, first=0, paired=links.paired, kind=F32):
        if paired:
            spec = pl.BlockSpec((devices // 2, height, step), lambda j: (0, 0, j + first))
            return [spec] * 2, [((devices // 2, height, columns), BF)] * 2
        spec = pl.BlockSpec((width, step), lambda j: (0, j + first))
        return [spec], [((width, columns), kind)]

    both_kind = BF if links.paired else F32
    specs, outs = outer_outs(2 * wide, WIDE_TILE, 0, False, both_kind)
    gated, both_parts = call(
        proj_body,
        (broad,),
        [
            smem(),
            whole((width, rows)),
            broad_cols(rows),
            broad_cols(rows),
            whole((rows, 1)),
            broad_cols(1),
        ],
        [broad_cols(rows)] + specs,
        [((rows, wide), BF)] + outs,
        [],
        2 * rows * width * wide,
        14 * rows * wide,
        core,
        grad_t,
        out_rows,
        gate,
        scale,
        gate_row,
    )
    proj_others = [tied(x, gated) for x in proj_others]
    proj_pieces = links.join_halves(proj_halves, proj_others)

    def swapped(s, place_ref):
        return ((s // half_blocks + 1 - place_ref[0]) % 2) * half_blocks + s % half_blocks

    def swap_rows(n):
        return pl.BlockSpec((QLEN, n), lambda s, p, r: (swapped(s, p), 0))

    proj_w, branch_send, branch_own, row_dot = call(
        functools.partial(branch_body, len(proj_pieces)),
        (blocks,),
        [swap_rows(wide), swap_rows(width)] + [whole(p.shape) for p in proj_pieces],
        [
            whole((width, wide)),
            pl.BlockSpec((QLEN, width), lambda s, p, r: (jnp.minimum(s, half_blocks - 1), 0)),
            pl.BlockSpec((QLEN, width), lambda s, p, r: (jnp.maximum(s - half_blocks, 0), 0)),
            swap_rows(1),
        ],
        [
            ((width, wide), BF),
            ((half_rows, width), BF),
            ((half_rows, width), F32),
            ((rows, 1), F32),
        ],
        [],
        2 * rows * width * wide,
        8 * rows * wide,
        place,
        starts,
        gated,
        grad,
        *proj_pieces,
        prefetch=2,
    )
    row_total = row_dot.reshape(8, rows // 8)
    row_total = (row_total + over_tensor(row_total)).reshape(rows, 1)
    branch_got = over_tensor(branch_send)

    specs, outs = outer_outs(2 * wide, WIDE_TILE, broad, False, both_kind)
    core_grad, all_grad, channel_sums, both_parts = call(
        gating_body,
        (broad,),
        [
            smem(),
            whole((rows, width)),
            broad_cols(width),
            broad_cols(rows),
            broad_cols(rows),
            broad_cols(rows),
            whole((rows, 1)),
            whole((rows, 1)),
            broad_cols(1),
            whole((width, rows)),
            pl.BlockSpec(memory_space=pl.ANY),
        ],
        [broad_cols(rows), broad_cols(rows, broad), broad_cols(2)] + specs,
        [((rows, wide), BF), ((rows, 2 * wide + SIDE), BF), ((2, wide), F32)] + outs,
        [],
        4 * rows * width * wide,
        14 * rows * wide,
        core,
        grad,
        proj_w,
        out_rows,
        gate,
        act_low,
        scale,
        row_total,
        gate_row,
        feat_t,
        both_parts,
        aliases={10: 3},
    )
    both_sum = lax.psum_scatter(both_parts, "dp", scatter_dimension=0, tiled=True).astype(F32)
    proj_sum, gate_sum = both_sum[:, :wide], both_sum[:, wide:]

    def scan_part(first, count, past, grads, parts, columns, deps):
        summed = [whole((blocks, QLEN, QLEN)), whole((rows, STATE)), whole((rows, STATE))]
        specs, outs = outer_outs(columns, TILE, 0 if not parts else first)
        anywhere = [pl.BlockSpec(memory_space=pl.ANY)] * (1 + len(parts))
        at = 16 + len(past)
        return call(
            functools.partial(scan_body, blocks, bool(past), len(specs)),
            (count,),
            [smem(), smem(), whole((width, rows))]
            + [tile_cols(n, first) for n in (rows, rows, rows, rows, rows, 1, KERNEL)]
            + [
                pack_spec(first),
                rowpack_spec(first),
                whole((rows, STATE)),
                whole((rows, STATE)),
                whole((blocks, QLEN, QLEN)),
                entry_spec(first),
            ]
            + (summed if past else [])
            + anywhere,
            specs
            + [tile_cols(rows, first), tile_cols(KERNEL)]
            + summed
            + [pl.BlockSpec((1, rows, 4 * PER), lambda j: (j, 0, 0))],
            outs
            + [
                ((rows, 2 * wide + SIDE), BF),
                ((KERNEL, count * TILE), F32),
                ((blocks, QLEN, QLEN), F32),
                ((rows, STATE), F32),
                ((rows, STATE), F32),
                ((count, rows, 4 * PER), F32),
            ],
            [
                pltpu.VMEM((QLEN + 8, TILE), F32),
                pltpu.VMEM((QLEN + 8, TILE), F32),
                pltpu.VMEM((TILE, STATE), F32),
            ],
            6 * rows * width * count * TILE,
            20 * rows * count * TILE,
            core,
            keep,
            feat_t,
            slope_low,
            core_grad,
            act_low,
            pre_low,
            out_rows,
            skip_row,
            value_taps,
            pack,
            rowpack,
            b_low,
            c_low,
            gram_t,
            entry,
            *past,
            grads,
            *parts,
            deps=deps,
            aliases={at: len(specs), **{at + 1 + i: i for i in range(len(parts))}},
        )

    third = -(-tiles // 3)
    early_columns = 2 * third * TILE
    late_columns = wide - early_columns + SIDE
    *early_parts, all_grad, taps_a, gram_grad, b_grad, c_grad, stats_a = scan_part(
        0, third, (), all_grad, (), early_columns, ()
    )
    *early_parts, all_grad, taps_b, gram_grad, b_grad, c_grad, stats_b = scan_part(
        third,
        third,
        (gram_grad, b_grad, c_grad),
        all_grad,
        early_parts,
        early_columns,
        (),
    )
    early_parts = links.scatter_core(early_parts)
    block_out = call(
        out_body,
        (half_blocks,),
        [block_rows(width)] * 3 + [block_rows(1)],
        [block_rows(width)],
        [((half_rows, width), BF)],
        [],
        half_rows * width,
        10 * half_rows * width,
        branch_own,
        branch_got,
        hidden_in,
        live_own,
        deps=(taps_b,),
    )[0]
    *late_parts, all_grad, taps_c, gram_grad, b_grad, c_grad, stats_c = scan_part(
        2 * third,
        tiles - 2 * third,
        (gram_grad, b_grad, c_grad),
        all_grad,
        (),
        late_columns,
        (early_parts[0], block_out),
    )
    early_parts = links.scatter_pair(early_parts)
    taps_part = jnp.concatenate([taps_a, taps_b, taps_c], axis=1)
    stats = [stats_a, stats_b, stats_c]

    anywhere = pl.BlockSpec(memory_space=pl.ANY)
    held_shape = (devices // 2, height, SIDE) if links.paired else (width, SIDE)
    held_kind = BF if links.paired else F32
    at = 12 + len(stats)
    *late_parts, all_grad, sharetaps_part, head_sums = call(
        functools.partial(side_body, blocks, len(stats), len(late_parts)),
        (1,),
        [
            smem(),
            smem(),
            anywhere,
            whole((blocks, QLEN, QLEN)),
            whole((rows, STATE)),
            whole((rows, STATE)),
            whole((rows, STATE)),
            whole((rows, STATE)),
            whole((rows, TILE)),
            whole((KERNEL, TILE)),
            whole((3, rows, LANES)),
            whole((1, LANES)),
        ]
        + [whole(part.shape) for part in stats]
        + [anywhere] * (1 + len(late_parts)),
        [anywhere] * len(late_parts)
        + [
            pl.BlockSpec((rows, SIDE), lambda b: (0, 2 * wide // SIDE)),
            whole((KERNEL, TILE)),
            whole((2, LANES)),
        ],
        [(part.shape, part.dtype) for part in late_parts]
        + [((rows, 2 * wide + SIDE), BF), ((KERNEL, TILE), F32), ((2, LANES), F32)],
        [
            pltpu.VMEM((QLEN + 8, TILE), F32),
            pltpu.VMEM((QLEN + 8, TILE), F32),
            pltpu.VMEM((width, rows), BF),
            pltpu.VMEM(held_shape, held_kind),
            pltpu.VMEM(held_shape, held_kind),
            pltpu.SemaphoreType.DMA,
            pltpu.SemaphoreType.DMA((2,)),
        ],
        3 * rows * width * STATE,
        20 * rows * TILE,
        core,
        keep,
        feat_t,
        gram_grad,
        b_grad,
        c_grad,
        b_low,
        c_low,
        shared,
        shared_taps,
        cols,
        decay_row,
        *stats,
        all_grad,
        *late_parts,
        deps=(early_parts[0],),
        aliases={at: len(late_parts), **{at + 1 + i: i for i in range(len(late_parts))}},
    )

    def back(other, kind, deps=()):
        full = 2 * wide + SIDE

        def at(j, p):
            return ((1 - p[0]) if other else p[0], 0)

        return call(
            back_body,
            (width // WIDE_TILE,),
            [
                pl.BlockSpec((half_rows, full), at),
                pl.BlockSpec((WIDE_TILE, full), lambda j, p: (j, 0)),
            ],
            [pl.BlockSpec((half_rows, WIDE_TILE), lambda j, p: (0, j))],
            [((half_rows, width), kind)],
            [],
            2 * rows * width * wide,
            16 * rows * wide,
            place,
            all_grad,
            all_w,
            deps=deps,
            prefetch=1,
        )[0]

    late_parts = links.scatter_core(late_parts, early_parts[0])
    back_send = back(True, BF)
    early_sum = links.scatter_ring(early_parts, back_send)
    back_got = over_tensor(back_send)
    back_own = back(False, F32, (late_parts[0],))
    late_parts = links.scatter_pair(late_parts, back_own)
    input_grad = call(
        input_body,
        (half_blocks,),
        [block_rows(width)] * 4 + [whole((1, width))],
        [block_rows(width)],
        [((half_rows, width), BF)],
        [],
        half_rows * width,
        12 * half_rows * width,
        back_own,
        back_got,
        hidden_in,
        cotangent,
        gain_row,
    )[0]
    late_sum = links.scatter_ring(late_parts, input_grad)

    head_row = jnp.concatenate(
        [
            sharetaps_part.reshape(-1),
            head_sums[0, :heads],
            head_sums[1, :heads],
            jnp.sum(channel_sums[1].reshape(heads, HEAD_DIM), axis=1),
            jnp.zeros((wide - KERNEL * TILE - 3 * heads,), F32),
        ]
    ).reshape(1, wide)
    small = jnp.concatenate([taps_part, channel_sums[0:1], head_row], axis=0)
    small = links.reduce(small, back_send, back_own)
    sharetaps = small[5:6, : KERNEL * TILE]
    sharetaps = sharetaps + over_tensor(sharetaps)

    rest = wide - early_columns
    value_sum = jnp.concatenate([early_sum, late_sum[:, :rest]], axis=1)
    side_sum = late_sum[:, rest : rest + 2 * STATE + heads]
    side_shard = jnp.concatenate([in_shared, in_step], axis=1)
    norm_part = (
        jnp.sum(gate_sum * in_gate.astype(F32), axis=1, keepdims=True)
        + jnp.sum(value_sum * in_value.astype(F32), axis=1, keepdims=True)
        + jnp.sum(side_sum * side_shard.astype(F32), axis=1, keepdims=True)
    ) / norm_gain.astype(F32)[:, None]
    mixed = jnp.concatenate(
        [late_sum[:, rest : rest + 2 * STATE], jnp.broadcast_to(norm_part, (height, LANES))], axis=1
    )
    mixed = mixed + over_tensor(mixed)

    share = KERNEL * TILE
    return (
        block_out,
        input_grad,
        mixed[:, 2 * STATE],
        gate_sum,
        value_sum,
        mixed[:, : 2 * STATE],
        side_sum[:, 2 * STATE :],
        small[0:KERNEL],
        sharetaps.reshape(KERNEL, TILE),
        small[5, share + heads : share + 2 * heads],
        small[5, share : share + heads],
        small[5, share + 2 * heads : share + 3 * heads],
        small[4],
        proj_sum.T,
    )


def solution(mesh):
    in_specs = (
        P(("dp", "tensor"), None),
        P("dp"),
        P("dp"),
        P("dp", "tensor"),
        P("dp", "tensor"),
        P("dp", None),
        P("dp", "tensor"),
        P(None, "tensor"),
        P(),
        P("tensor"),
        P("tensor"),
        P("tensor"),
        P("tensor"),
        P("tensor", "dp"),
        P(("dp", "tensor"), None),
    )
    out_specs = (
        P(("dp", "tensor"), None),
        P(("dp", "tensor"), None),
        P("dp"),
        P("dp", "tensor"),
        P("dp", "tensor"),
        P("dp", None),
        P("dp", "tensor"),
        P(None, "tensor"),
        P(),
        P("tensor"),
        P("tensor"),
        P("tensor"),
        P("tensor"),
        P("tensor", "dp"),
    )
    return jax.shard_map(
        functools.partial(on_device, devices=mesh.shape["dp"]),
        mesh=mesh,
        in_specs=in_specs,
        out_specs=out_specs,
        check_vma=False,
    )
```

```python
import functools

import jax
import jax.numpy as jnp
from jax import lax
from jax.experimental import pallas as pl
from jax.experimental.pallas import tpu as pltpu
from jax.sharding import PartitionSpec as P

HEAD_DIM = 64
STATE = 128
KERNEL = 4
QLEN = 256
INNER = 3072
EPSILON = 1e-05
TILE = 256
SIDE = 384
WIDE_TILE = 512
LANES = 128
HALF = QLEN // 2
PER = TILE // HEAD_DIM

BF = jnp.bfloat16
F32 = jnp.float32
HIGH = lax.Precision.HIGHEST
ROOM = 53 * 1024 * 1024
WEIGHT = 3


def dot(left, right, left_dim=1, right_dim=0, precision=None):
    return lax.dot_general(
        left,
        right,
        (((left_dim,), (right_dim,)), ((), ())),
        preferred_element_type=F32,
        precision=precision,
    )


def iota(shape, dim):
    return lax.broadcasted_iota(jnp.int32, shape, dim)


def split_dot(values, chooser):
    high = values.astype(BF)
    rest = (values - high.astype(F32)).astype(BF)
    return dot(high, chooser) + dot(rest, chooser)


def whole(shape):
    return pl.BlockSpec(shape, lambda *_: (0,) * len(shape))


def smem():
    return pl.BlockSpec(memory_space=pltpu.SMEM)


def call(
    body,
    grid,
    in_specs,
    out_specs,
    out_shape,
    scratch,
    flops,
    moved,
    *args,
    deps=(),
    prefetch=0,
    aliases=None,
):
    count = len(args)

    def held(*refs):
        body(*refs[:count], *refs[count + len(deps) :])

    anywhere = [pl.BlockSpec(memory_space=pl.ANY)] * len(deps)
    return pl.pallas_call(
        held,
        grid_spec=pltpu.PrefetchScalarGridSpec(
            num_scalar_prefetch=prefetch,
            grid=grid,
            in_specs=list(in_specs) + anywhere,
            out_specs=out_specs,
            scratch_shapes=scratch,
        ),
        out_shape=[jax.ShapeDtypeStruct(shape, kind) for shape, kind in out_shape],
        input_output_aliases=aliases or {},
        compiler_params=pltpu.CompilerParams(vmem_limit_bytes=ROOM),
        cost_estimate=pl.CostEstimate(
            flops=flops * WEIGHT, bytes_accessed=moved, transcendentals=0
        ),
    )(*args, *deps)


def tied(value, *deps):
    anywhere = pl.BlockSpec(memory_space=pl.ANY)
    return pl.pallas_call(
        lambda *refs: None,
        in_specs=[anywhere] * (1 + len(deps)),
        out_specs=anywhere,
        out_shape=jax.ShapeDtypeStruct(value.shape, value.dtype),
        input_output_aliases={0: 0},
        compiler_params=pltpu.CompilerParams(vmem_limit_bytes=ROOM),
    )(value, *deps)


def silu_slope(sigma, inputs):
    return sigma * (1.0 + inputs * (1.0 - sigma))


def expand(narrow):
    first = iota((QLEN, LANES), 1) < HEAD_DIM
    parts = []
    for pair in range(PER // 2):
        left = jnp.broadcast_to(narrow[:, 2 * pair : 2 * pair + 1], (QLEN, LANES))
        right = jnp.broadcast_to(narrow[:, 2 * pair + 1 : 2 * pair + 2], (QLEN, LANES))
        parts.append(jnp.where(first, left, right))
    return jnp.concatenate(parts, axis=1)


def head_rows(narrow):
    return jnp.concatenate(
        [jnp.broadcast_to(narrow[:, h : h + 1], (HEAD_DIM, STATE)) for h in range(PER)], axis=0
    )


def lane_masks():
    first = iota((1, LANES), 1) < HEAD_DIM
    return (first.astype(BF), jnp.logical_not(first).astype(BF))


def fill_weight(out_ref, rows_ref, pieces):
    at = 0
    for piece in pieces:
        count, height = piece.shape[0], piece.shape[1]
        for i in range(count):
            start = pl.multiple_of(rows_ref[at], 16) if height % 16 == 0 else rows_ref[at]
            out_ref[pl.ds(start, height), :] = piece[i]
            at += 1


def conv_sum(ext, taps):
    total = taps[KERNEL - 1 : KERNEL, :] * ext[8 : 8 + QLEN, :]
    for lag in range(1, KERNEL):
        total = total + taps[KERNEL - 1 - lag : KERNEL - lag, :] * ext[8 - lag : 8 - lag + QLEN, :]
    return total


def norm_body(
    half_blocks,
    pieces_total,
    gain_lane,
    rows_ref,
    place,
    keep,
    own,
    got,
    taps,
    bias,
    decay,
    *refs,
):
    pieces = refs[:pieces_total]
    (
        feat,
        feat_t,
        shared,
        b_out,
        c_out,
        gram,
        gram_t,
        cols,
        pack,
        rowpack,
        side_w,
        gain,
        hold,
        ext,
    ) = refs[pieces_total:]
    b = pl.program_id(0)
    mine = (b // half_blocks) == place[0]

    @pl.when(b == 0)
    def _():
        fill_weight(side_w, rows_ref, pieces)
        edge = gain_lane // LANES * LANES
        spread = side_w[:, edge : edge + LANES].astype(F32).T
        gain[...] = spread[gain_lane - edge : gain_lane - edge + 1, :]

    @pl.when(mine)
    def _():
        hold[...] = own[...].astype(F32)

    @pl.when(jnp.logical_not(mine))
    def _():
        hold[...] = got[...].astype(F32)

    rows = hold[...]
    inverse = lax.rsqrt(jnp.mean(rows * rows, axis=1, keepdims=True) + EPSILON)
    normed = (rows * inverse * gain[...]).astype(BF)
    feat[...] = normed
    feat_t[...] = normed.T
    side = dot(normed, side_w[...])
    pre = side[:, :TILE]
    shared[...] = pre

    @pl.when(b == 0)
    def _():
        ext[...] = jnp.zeros_like(ext)

    ext[0:8, :] = ext[QLEN : QLEN + 8, :] * keep[b]
    ext[8 : 8 + QLEN, :] = pre
    conv = conv_sum(ext, taps)
    act = (conv * jax.nn.sigmoid(conv)).astype(BF)
    b_low = act[:, :STATE]
    c_low = act[:, STATE:]
    b_out[...] = b_low
    c_out[...] = c_low
    lower = iota((QLEN, QLEN), 0) >= iota((QLEN, QLEN), 1)
    upper = iota((QLEN, QLEN), 0) <= iota((QLEN, QLEN), 1)
    gram[0] = jnp.where(lower, dot(c_low, b_low, 1, 1), 0.0)
    gram_t[0] = jnp.where(upper, dot(b_low, c_low, 1, 1), 0.0)
    raw = side[:, TILE:] + bias[...]
    step = jnp.maximum(raw, 0.0) + jnp.log1p(jnp.exp(-jnp.abs(raw)))
    logdec = step * -jnp.exp(decay[...])
    cum = dot(lower.astype(F32), logdec, precision=HIGH)
    cols[0] = raw
    cols[1] = step
    cols[2] = logdec
    cum_t = cum.T
    step_t = step.T
    for j in range(pack.shape[0]):
        heads = slice(PER * j, PER * j + PER)
        pack[j] = jnp.concatenate([cum[:, heads], step[:, heads]], axis=1)
        rowpack[j, 0] = jnp.concatenate([cum_t[heads, :], step_t[heads, :]], axis=0)


def value_body(
    pieces_total,
    blocks,
    past,
    rows_ref,
    keep,
    feat,
    *refs,
):
    pieces = refs[:pieces_total]
    refs = refs[: pieces_total + 7] + refs[pieces_total + 7 + past :]
    (
        taps,
        skip,
        pack,
        rowpack,
        b_ref,
        c_ref,
        gram,
        weight,
        pre_out,
        act_out,
        slope_out,
        out_rows,
        entry,
        pre,
        ext,
        state,
    ) = refs[pieces_total:]
    fill_weight(weight, rows_ref, pieces)
    masks = lane_masks()
    for b in range(blocks):
        span = slice(b * QLEN, (b + 1) * QLEN)
        pre[...] = dot(feat[span, :], weight[...])
        pre_out[span, :] = pre[...].astype(BF)
        if b == 0:
            ext[0:8, :] = jnp.zeros((8, TILE), F32)
            state[...] = jnp.zeros_like(state)
        else:
            ext[0:8, :] = ext[QLEN : QLEN + 8, :] * keep[b]
        ext[8 : 8 + QLEN, :] = pre[...]
        conv = conv_sum(ext, taps)
        sigma = jax.nn.sigmoid(conv)
        act_low = (conv * sigma).astype(BF)
        act_out[span, :] = act_low
        slope_out[span, :] = silu_slope(sigma, conv).astype(BF)
        act = act_low.astype(F32)
        narrow = pack[0, span, :]
        cum = narrow[:, :PER]
        step = narrow[:, PER:]
        last = cum[QLEN - 1 : QLEN, :]
        stepped = (act * expand(step)).astype(BF)
        scaled = (act * expand(jnp.exp(last - cum) * step)).astype(BF)
        row_cum = rowpack[0, b]
        parts = []
        for pair in range(PER // 2):
            lanes = slice(pair * LANES, (pair + 1) * LANES)
            tops, lows, values = [], [], []
            for k in range(2):
                h = 2 * pair + k
                col = cum[:, h : h + 1]
                row = row_cum[h : h + 1, :]
                e00 = jnp.exp(jnp.minimum(col[:HALF] - row[:, :HALF], 0.0))
                e10 = jnp.exp(col[HALF:] - row[:, :HALF])
                e11 = jnp.exp(jnp.minimum(col[HALF:] - row[:, HALF:], 0.0))
                tops.append((gram[b, :HALF, :HALF] * e00).astype(BF))
                lows.append((gram[b, HALF:, :HALF] * e10).astype(BF))
                lows.append((gram[b, HALF:, HALF:] * e11).astype(BF))
                values.append(stepped[:, lanes] * masks[k])
            top = dot(
                jnp.concatenate(tops, axis=1),
                jnp.concatenate([v[:HALF] for v in values], axis=0),
            )
            low = dot(jnp.concatenate(lows, axis=1), jnp.concatenate(values, axis=0))
            parts.append(jnp.concatenate([top, low], axis=0))
        within = jnp.concatenate(parts, axis=1)
        held = state[...]
        entry[b] = held
        across = dot(c_ref[span, :], held.astype(BF), 1, 1)
        core = within + across * expand(jnp.exp(cum))
        out_rows[span, :] = core + act * skip[...]
        if b + 1 < blocks:
            fresh = dot(scaled, b_ref[span, :], 0, 0)
            state[...] = keep[b + 1] * (head_rows(jnp.exp(last)) * held + fresh)


def gate_body(pieces_total, rows_ref, feat, *refs):
    pieces = refs[:pieces_total]
    out_rows, _, weight, gate_out, squares = refs[pieces_total:]
    fill_weight(weight, rows_ref, pieces)

    @pl.when(pl.program_id(0) == 0)
    def _():
        squares[...] = jnp.zeros_like(squares)

    for b in range(feat.shape[0] // QLEN):
        span = slice(b * QLEN, (b + 1) * QLEN)
        gate = dot(feat[span, :], weight[...])
        gate_out[span, :] = gate.astype(BF)
        product = out_rows[span, :] * (gate * jax.nn.sigmoid(gate))
        power = product * product
        total = squares[span, :]
        for at in range(0, power.shape[1], LANES):
            total = total + power[:, at : at + LANES]
        squares[span, :] = total


def mask_body(half_blocks, place, own, got, live, out, out_t):
    b = pl.program_id(0)
    mine = (b // half_blocks) == place[0]

    @pl.when(mine)
    def _():
        out[...] = own[...] * live[...]

    @pl.when(jnp.logical_not(mine))
    def _():
        out[...] = got[...] * live[...]

    out_t[...] = out[...].T


def proj_body(place, left, out_rows, gate_ref, scale_ref, gain, gated_out, *outs):
    for b in range(gated_out.shape[0] // QLEN):
        span = slice(b * QLEN, (b + 1) * QLEN)
        gate = gate_ref[span, :].astype(F32)
        product = out_rows[span, :] * (gate * jax.nn.sigmoid(gate))
        gated_out[span, :] = (product * scale_ref[span, :] * gain[...]).astype(BF)
    emit_outer(place, dot(left[...], gated_out[...]), outs)


def branch_body(pieces_total, place, rows_ref, gated, grad, *refs):
    pieces = refs[:pieces_total]
    weight, send, mine, row_dot = refs[pieces_total:]
    s = pl.program_id(0)

    @pl.when(s == 0)
    def _():
        fill_weight(weight, rows_ref, pieces)

    branch = dot(gated[...], weight[...], 1, 1)
    row_dot[...] = jnp.sum(branch * grad[...].astype(F32), axis=1, keepdims=True)

    @pl.when(s < pl.num_programs(0) // 2)
    def _():
        send[...] = branch.astype(BF)

    @pl.when(s >= pl.num_programs(0) // 2)
    def _():
        mine[...] = branch


def gating_body(
    place,
    grad,
    weight,
    out_ref,
    gate_ref,
    act_ref,
    scale_ref,
    row_dot,
    gain,
    feat_t,
    _,
    core,
    gate_grad,
    sums,
    *outs,
):
    gating = jnp.zeros(gain.shape, F32)
    skipping = jnp.zeros(gain.shape, F32)
    for b in range(grad.shape[0] // QLEN):
        span = slice(b * QLEN, (b + 1) * QLEN)
        grad_gated = dot(grad[span, :], weight[...])
        gate = gate_ref[span, :].astype(F32)
        sigma = jax.nn.sigmoid(gate)
        act = gate * sigma
        out_rows = out_ref[span, :]
        scale = scale_ref[span, :]
        normal = out_rows * act * scale
        gating = gating + jnp.sum(grad_gated * normal, axis=0, keepdims=True)
        grad_product = scale * (
            grad_gated * gain[...] - normal * (row_dot[span, :] * (1.0 / INNER))
        )
        grad_out = grad_product * act
        core[span, :] = grad_out.astype(BF)
        gate_grad[span, :] = (grad_product * out_rows * silu_slope(sigma, gate)).astype(BF)
        skipping = skipping + jnp.sum(
            grad_out * act_ref[span, :].astype(F32), axis=0, keepdims=True
        )
    sums[...] = jnp.concatenate([gating, skipping], axis=0)
    emit_outer(place, dot(feat_t[...], gate_grad[...]), outs)


def scan_body(
    blocks,
    summed,
    outer_outs,
    place,
    keep,
    feat_t,
    slope_ref,
    core_ref,
    act_ref,
    pre_ref,
    out_ref,
    skip,
    taps,
    pack,
    rowpack,
    b_ref,
    c_ref,
    gram_t,
    entry,
    *refs,
):
    past = refs[:3] if summed else ()
    own = len(refs) - 9 - outer_outs
    outs = refs[own : own + outer_outs]
    grad_pre, taps_grad, gram_grad, b_grad, c_grad, stats = refs[own + outer_outs : -3]
    ext, tail, carry = refs[-3:]

    @pl.when(pl.program_id(0) == 0)
    def _():
        if past:
            gram_grad[...] = past[0][...]
            b_grad[...] = past[1][...]
            c_grad[...] = past[2][...]
        else:
            gram_grad[...] = jnp.zeros_like(gram_grad)
            b_grad[...] = jnp.zeros_like(b_grad)
            c_grad[...] = jnp.zeros_like(c_grad)

    masks = lane_masks()
    owner = iota((TILE, LANES), 0) // HEAD_DIM
    lane = iota((TILE, LANES), 1)
    chooser = [(lane == owner + PER * q).astype(BF) for q in range(4)]
    final_row = iota((QLEN, LANES), 0) == QLEN - 1
    ones = jnp.ones((8, STATE), BF)
    tap_sums = [jnp.zeros((1, TILE), F32) for _ in range(KERNEL)]
    for b in reversed(range(blocks)):
        span = slice(b * QLEN, (b + 1) * QLEN)
        final = b == blocks - 1
        grad_low = core_ref[span, :]
        grad = grad_low.astype(F32)
        act = act_ref[span, :].astype(F32)
        narrow = pack[0, span, :]
        cum = narrow[:, :PER]
        step = narrow[:, PER:]
        last = cum[QLEN - 1 : QLEN, :]
        step_wide = expand(step)
        stepped = (act * step_wide).astype(BF)
        row_cum = rowpack[0, b]
        parts = []
        upper_sum = None
        lower_sum = None
        for pair in range(PER // 2):
            lanes = slice(pair * LANES, (pair + 1) * LANES)
            grad_pair = grad_low[:, lanes]
            tops, lows, grads = [], [], []
            for k in range(2):
                h = 2 * pair + k
                col = cum[:, h : h + 1]
                row = row_cum[h : h + 1, :]
                e00 = jnp.exp(jnp.minimum(row[:, :HALF] - col[:HALF], 0.0))
                e01 = jnp.exp(row[:, HALF:] - col[:HALF])
                e11 = jnp.exp(jnp.minimum(row[:, HALF:] - col[HALF:], 0.0))
                value = stepped[:, lanes] * masks[k]
                upper = dot(value[:HALF], grad_pair, 1, 1) * jnp.concatenate([e00, e01], axis=1)
                lower = dot(value[HALF:], grad_pair[HALF:], 1, 1) * e11
                upper_sum = upper if upper_sum is None else upper_sum + upper
                lower_sum = lower if lower_sum is None else lower_sum + lower
                tops.append((gram_t[b, :HALF, :HALF] * e00).astype(BF))
                tops.append((gram_t[b, :HALF, HALF:] * e01).astype(BF))
                lows.append((gram_t[b, HALF:, HALF:] * e11).astype(BF))
                grads.append(grad_pair * masks[k])
            top = dot(jnp.concatenate(tops, axis=1), jnp.concatenate(grads, axis=0))
            low = dot(
                jnp.concatenate(lows, axis=1),
                jnp.concatenate([g[HALF:] for g in grads], axis=0),
            )
            parts.append(jnp.concatenate([top, low], axis=0))
        gram_grad[b, :HALF, :] += upper_sum
        gram_grad[b, HALF:, HALF:] += lower_sum
        mixed = jnp.concatenate(parts, axis=1)
        between = out_ref[span, :] - act * skip[...]
        flows = stepped.astype(F32) * mixed
        grad_value = step_wide * mixed + skip[...] * grad
        held = entry[b]
        across_low = (grad * expand(jnp.exp(cum))).astype(BF)
        c_grad[span, :] += dot(across_low, held.astype(BF))
        totals = split_dot(grad * between, chooser[1])
        if not final:
            states = carry[...]
            states_low = states.astype(BF)
            weights = expand(jnp.exp(last - cum) * step)
            pulled = dot(b_ref[span, :], states_low, 1, 1) * weights
            grad_value = grad_value + pulled
            weighted = act * pulled
            scaled = (act * weights).astype(BF)
            b_grad[span, :] += dot(scaled, states_low)
            totals = totals + split_dot(flows + weighted, chooser[0])
            totals = totals + split_dot(weighted, chooser[2])
            passed = head_rows(jnp.exp(last)) * states
            spread = passed * held
            high = spread.astype(BF)
            rest = (spread - high.astype(F32)).astype(BF)
            summed = dot(ones, high, 1, 1) + dot(ones, rest, 1, 1)
            last_sum = split_dot(summed, chooser[3])
            totals = totals + jnp.where(final_row, last_sum[0:1, :], 0.0)
        else:
            totals = totals + split_dot(flows, chooser[0])
        stats[0, span, :] = totals[:, : 4 * PER]
        if b > 0:
            fresh = dot(across_low, c_ref[span, :], 0, 0)
            carry[...] = keep[b] * (fresh if final else fresh + passed)
        if b > 0:
            ext[0:8, :] = pre_ref[b * QLEN - 16 : b * QLEN, :].astype(F32)[8:, :] * keep[b]
        else:
            ext[0:8, :] = jnp.zeros((8, TILE), F32)
        ext[8 : 8 + QLEN, :] = pre_ref[span, :].astype(F32)
        slope = grad_value * slope_ref[span, :].astype(F32)
        for lag in range(KERNEL):
            tap_sums[KERNEL - 1 - lag] = tap_sums[KERNEL - 1 - lag] + jnp.sum(
                slope * ext[8 - lag : 8 - lag + QLEN, :], axis=0, keepdims=True
            )
        if final:
            tail[QLEN : QLEN + 8, :] = jnp.zeros((8, TILE), F32)
        else:
            tail[QLEN : QLEN + 8, :] = tail[0:8, :] * keep[b + 1]
        tail[0:QLEN, :] = slope
        pulled_back = taps[KERNEL - 1 : KERNEL, :] * slope
        for lag in range(1, KERNEL):
            pulled_back = (
                pulled_back
                + taps[KERNEL - 1 - lag : KERNEL - lag, :] * tail[lag : lag + QLEN, :]
            )
        grad_pre[span, :] = pulled_back.astype(BF)
    taps_grad[...] = jnp.concatenate(tap_sums, axis=0)
    emit_outer(place, dot(feat_t[...], grad_pre[...]), outs)


def side_body(
    blocks,
    tiles_total,
    aliased,
    place,
    keep,
    feat_hbm,
    gram_grad,
    b_grad,
    c_grad,
    b_ref,
    c_ref,
    shared,
    taps,
    cols,
    decay,
    *refs,
):
    stats = refs[:tiles_total]
    outs = refs[tiles_total + 1 + aliased : -10]
    out, taps_grad, sums, ext, tail, feat_t, first, second, feat_sem, sems = refs[-10:]
    loading = pltpu.make_async_copy(feat_hbm, feat_t, feat_sem)
    loading.start()
    lower = iota((QLEN, QLEN), 0) >= iota((QLEN, QLEN), 1)
    upper = iota((QLEN, QLEN), 0) <= iota((QLEN, QLEN), 1)
    final_row = iota((QLEN, LANES), 0) == QLEN - 1
    rate = jnp.exp(decay[...])
    tap_sums = [jnp.zeros((1, TILE), F32) for _ in range(KERNEL)]
    decay_sum = jnp.zeros((1, LANES), F32)
    bias_sum = jnp.zeros((1, LANES), F32)
    tiles = sum(part.shape[0] for part in stats)
    padding = jnp.zeros((QLEN, LANES - PER * tiles), F32)
    for b in reversed(range(blocks)):
        span = slice(b * QLEN, (b + 1) * QLEN)
        final = b == blocks - 1
        gathered = [
            jnp.concatenate(
                [
                    part[j, span, PER * q : PER * q + PER]
                    for part in stats
                    for j in range(part.shape[0])
                ]
                + [padding],
                axis=1,
            )
            for q in range(4)
        ]
        pulled = gathered[0]
        grad_cum = gathered[1] - pulled + gathered[3]
        grad_cum = grad_cum + jnp.where(
            final_row, jnp.sum(gathered[2], axis=0, keepdims=True), 0.0
        )
        grad_log = dot(upper.astype(F32), grad_cum, precision=HIGH)
        raw = cols[0, span, :]
        step = cols[1, span, :]
        sigma = jax.nn.sigmoid(raw)
        ratio = jnp.where(raw < -20.0, 1.0, sigma / jnp.maximum(step, 1e-30))
        grad_raw = pulled * ratio - rate * grad_log * sigma
        decay_sum = decay_sum + jnp.sum(grad_log * cols[2, span, :], axis=0, keepdims=True)
        bias_sum = bias_sum + jnp.sum(grad_raw, axis=0, keepdims=True)
        out[span, TILE:] = grad_raw.astype(BF)
        gram_low = jnp.where(upper, gram_grad[b], 0.0).astype(BF)
        b_total = b_grad[span, :] + dot(gram_low, c_ref[span, :])
        c_total = c_grad[span, :] + dot(gram_low, b_ref[span, :], 0, 0)
        grad_act = jnp.concatenate([b_total, c_total], axis=1)
        if b > 0:
            ext[0:8, :] = shared[b * QLEN - 8 : b * QLEN, :] * keep[b]
        else:
            ext[0:8, :] = jnp.zeros((8, TILE), F32)
        ext[8 : 8 + QLEN, :] = shared[span, :]
        conv = conv_sum(ext, taps)
        slope = grad_act * silu_slope(jax.nn.sigmoid(conv), conv)
        for lag in range(KERNEL):
            tap_sums[KERNEL - 1 - lag] = tap_sums[KERNEL - 1 - lag] + jnp.sum(
                slope * ext[8 - lag : 8 - lag + QLEN, :], axis=0, keepdims=True
            )
        if final:
            tail[QLEN : QLEN + 8, :] = jnp.zeros((8, TILE), F32)
        else:
            tail[QLEN : QLEN + 8, :] = tail[0:8, :] * keep[b + 1]
        tail[0:QLEN, :] = slope
        pulled_back = taps[KERNEL - 1 : KERNEL, :] * slope
        for lag in range(1, KERNEL):
            pulled_back = (
                pulled_back
                + taps[KERNEL - 1 - lag : KERNEL - lag, :] * tail[lag : lag + QLEN, :]
            )
        out[span, :TILE] = pulled_back.astype(BF)
    taps_grad[...] = jnp.concatenate(tap_sums, axis=0)
    sums[...] = jnp.concatenate([decay_sum, bias_sum], axis=0)
    loading.wait()
    held = (first, second)[: len(outs)]
    emit_outer(place, dot(feat_t[...], out[...]), held)
    moves = []
    for i, (target, source) in enumerate(zip(outs, held)):
        start = target.shape[-1] - SIDE
        view = target.at[..., pl.ds(start, SIDE)]
        moves.append(pltpu.make_async_copy(source, view, sems.at[i]))
    for move in moves:
        move.start()
    for move in moves:
        move.wait()


def emit_outer(place, total, outs):
    if len(outs) == 1:
        outs[0][...] = total.astype(outs[0].dtype)
        return
    mine, send = outs
    low = total.astype(BF).reshape(mine.shape[0], 2, mine.shape[1], total.shape[1])

    @pl.when(place[0] == 0)
    def _():
        mine[...] = low[:, 0]
        send[...] = low[:, 1]

    @pl.when(place[0] == 1)
    def _():
        mine[...] = low[:, 1]
        send[...] = low[:, 0]


def outer_body(place, left, right, *outs):
    emit_outer(place, dot(left[...], right[...]), outs)


def back_body(place, grads, weights, out):
    out[...] = dot(grads[...], weights[...], 1, 1).astype(out.dtype)


def input_body(mine, got, hidden, cot, gain, out):
    total = (mine[...] + got[...].astype(F32)) * gain[...]
    rows = hidden[...].astype(F32)
    inverse = lax.rsqrt(jnp.mean(rows * rows, axis=1, keepdims=True) + EPSILON)
    hat = rows * inverse
    spread = jnp.mean(total * hat, axis=1, keepdims=True)
    out[...] = (cot[...].astype(F32) + (total - hat * spread) * inverse).astype(BF)


def out_body(mine, got, hidden, live, out):
    out[...] = (
        hidden[...].astype(F32) + live[...] * (mine[...] + got[...].astype(F32))
    ).astype(BF)


class Links:
    def __init__(self, devices, shard_rows):
        self.devices = devices
        self.height = shard_rows
        self.paired = devices % 4 == 0 and shard_rows % 16 == 0
        self.ring = max(devices // 4, 1)
        spot = lax.axis_index("dp")
        self.a, self.b, self.c = spot // 4, (spot // 2) % 2, spot % 2
        self.spot = spot

    def moved(self, rule):
        pairs = []
        for a in range(self.ring):
            for b in range(2):
                for c in range(2):
                    ta, tb, tc = rule(a, b, c)
                    pairs.append(((a * 2 + b) * 2 + c, (ta * 2 + tb) * 2 + tc))
        return pairs

    def over_core(self, x):
        return lax.ppermute(x, "dp", self.moved(lambda a, b, c: (a, b, 1 - c)))

    def over_pair(self, x):
        return lax.ppermute(x, "dp", self.moved(lambda a, b, c: (a, 1 - b, c)))

    def over_ring(self, x, k):
        return lax.ppermute(x, "dp", self.moved(lambda a, b, c: ((a + k) % self.ring, b, c)))

    def gather_fast(self, shard):
        if not self.paired:
            return [lax.all_gather(shard, "dp", axis=0, tiled=True)[None]], (shard,)
        near = [k for k in range(1, self.ring) if k in (1, self.ring - 1)]
        far = [k for k in range(1, self.ring) if k not in near]
        held = {0: shard}
        other = {0: self.over_pair(shard)}
        for k in near:
            held[k] = self.over_ring(shard, k)
        later = tied(shard, other[0], *[held[k] for k in near])
        for k in far:
            held[k] = self.over_ring(later, k)
        for k in near + far:
            other[k] = self.over_pair(held[k])
        pieces = [held[k] for k in range(self.ring)] + [other[k] for k in range(self.ring)]
        pieces = pieces + [self.over_core(x) for x in pieces]
        return [x[None] for x in pieces], (held[(near + far)[-1]], other[near[0]])

    def ring_parts(self, shard):
        if not self.paired:
            return [shard]
        return [shard] + [self.over_ring(shard, k) for k in range(1, self.ring)]

    def ring_stack(self, parts, *deps):
        if not self.paired:
            return parts[0]
        return jnp.stack(parts[:-1] + [tied(parts[-1], *deps)])

    def gather_rest(self, held, *deps):
        if not self.paired:
            return [lax.all_gather(held, "dp", axis=0, tiled=True)[None]]
        other = tied(self.over_pair(held), *deps)
        return [held, other, self.over_core(held), self.over_core(other)]

    def ring_halves(self, parts):
        if not self.paired:
            return [parts[0]]
        cut = max(self.ring // 2, 1)
        return [jnp.stack(parts[:cut])] + ([jnp.stack(parts[cut:])] if parts[cut:] else [])

    def pair_halves(self, halves):
        return [self.over_pair(h) for h in halves] if self.paired else []

    def join_halves(self, halves, others):
        if not self.paired:
            return [lax.all_gather(halves[0], "dp", axis=0, tiled=True)[None]]
        pieces = halves + others
        return pieces + [self.over_core(x) for x in pieces]

    def ring_gather(self, shard):
        if not self.paired:
            return shard
        return self.over_rings(jnp.broadcast_to(shard[None], (self.ring,) + shard.shape))

    def starts(self, rings):
        if not self.paired:
            return jnp.zeros((1,), jnp.int32)
        rows = []
        for c in (self.c, 1 - self.c):
            for b in (self.b, 1 - self.b):
                rows += [((a * 2 + b) * 2 + c) * self.height for a in rings]
        return jnp.stack(rows).astype(jnp.int32)

    def scatter_core(self, parts, *deps):
        if not self.paired:
            return parts
        mine, send = parts
        send = tied(send, *deps) if deps else send
        shape = (self.ring, 2) + mine.shape[1:]
        got = self.over_core(send)
        mine, got = mine.reshape(shape), got.reshape(shape)
        away = self.pick(mine, 1 - self.b, 1).astype(F32) + self.pick(got, 1 - self.b, 1).astype(F32)
        return [away.astype(BF), mine, got]

    def pick(self, x, i, dim):
        return lax.dynamic_index_in_dim(x, i, dim, keepdims=False)

    def scatter_pair(self, parts, *deps):
        if not self.paired:
            return parts
        away, mine, got = parts
        near = tied(self.over_pair(away), *deps) if deps else self.over_pair(away)

        total = self.pick(mine, self.b, 1).astype(F32) + self.pick(got, self.b, 1).astype(F32)
        return [(total + near.astype(F32)).astype(BF)]

    def over_rings(self, x):
        groups = [
            [(a * 2 + b) * 2 + c for a in range(self.ring)] for b in range(2) for c in range(2)
        ]
        return lax.all_to_all(x, "dp", 0, 0, tiled=True, axis_index_groups=groups)

    def scatter_ring(self, parts, *deps):
        if not self.paired:
            return lax.psum_scatter(parts[0], "dp", scatter_dimension=0, tiled=True)
        moved = self.over_rings(parts[0])
        if deps:
            moved = tied(moved, *deps)
        return jnp.sum(moved.astype(F32), axis=0)

    def reduce(self, x, first, second):
        if not self.paired:
            return lax.psum(x, "dp")
        x = tied(x + self.over_core(x), first)
        x = tied(x + self.over_pair(x), second)
        total = x
        for k in range(1, self.ring):
            total = total + self.over_ring(x, k)
        return total


def over_tensor(x):
    return lax.ppermute(x, "tensor", [(0, 1), (1, 0)])


def on_device(
    hidden_in,
    segment,
    norm_gain,
    in_gate,
    in_value,
    in_shared,
    in_step,
    value_taps,
    shared_taps,
    step_bias,
    decay_log,
    skip_gain,
    gate_gain,
    out_proj,
    cotangent,
    devices,
):
    half_rows, width = hidden_in.shape
    rows = segment.shape[0]
    blocks = rows // QLEN
    half_blocks = half_rows // QLEN
    wide = in_value.shape[1]
    tiles = wide // TILE
    heads = step_bias.shape[0]
    height = in_value.shape[0]
    links = Links(devices, height)
    tensor = lax.axis_index("tensor")
    place = jnp.reshape(tensor, (1,)).astype(jnp.int32)
    core = jnp.reshape(links.c, (1,)).astype(jnp.int32)

    firsts = segment[::QLEN]
    keep = jnp.concatenate(
        [jnp.zeros((1,), F32), (firsts[1:] == firsts[:-1]).astype(F32)]
    )
    live = (segment >= 0).astype(F32)[:, None]
    live_own = lax.dynamic_slice_in_dim(live, tensor * half_rows, half_rows)
    pad = SIDE - 2 * STATE - heads - 1
    value_shard = jnp.concatenate(
        [in_value, in_shared, in_step, norm_gain[:, None], jnp.zeros((height, pad), BF)], axis=1
    )
    hidden_got = over_tensor(hidden_in)
    ring = range(links.ring)
    starts = links.starts([lax.rem(links.a - k + links.ring, links.ring) for k in ring])
    ordered = links.starts(ring)
    value_pieces, value_last = links.gather_fast(value_shard)
    gate_shard = tied(in_gate, *value_last)
    gate_ring = links.ring_gather(gate_shard)
    cot_got = over_tensor(cotangent)

    bias_row = jnp.pad(step_bias, (0, LANES - heads)).reshape(1, LANES)
    decay_row = jnp.pad(decay_log, (0, LANES - heads)).reshape(1, LANES)
    skip_row = jnp.repeat(skip_gain, HEAD_DIM).reshape(1, wide)
    gate_row = gate_gain.reshape(1, wide)

    block_rows = lambda n: pl.BlockSpec((QLEN, n), lambda b, *_: (b, 0))
    half_spec = pl.BlockSpec((QLEN, width), lambda b, *_: (b % half_blocks, 0))
    (
        feat,
        feat_t,
        shared,
        b_low,
        c_low,
        gram,
        gram_t,
        cols,
        pack,
        rowpack,
        all_w,
        gain_row,
    ) = call(
        functools.partial(norm_body, half_blocks, len(value_pieces), 2 * STATE + heads),
        (blocks,),
        [
            smem(),
            smem(),
            smem(),
            half_spec,
            half_spec,
            whole((KERNEL, TILE)),
            whole((1, LANES)),
            whole((1, LANES)),
        ]
        + [
            pl.BlockSpec(p.shape[:2] + (SIDE,), lambda b: (0, 0, wide // SIDE))
            for p in value_pieces
        ],
        [
            block_rows(width),
            pl.BlockSpec((width, QLEN), lambda b: (0, b)),
            block_rows(TILE),
            block_rows(STATE),
            block_rows(STATE),
            pl.BlockSpec((1, QLEN, QLEN), lambda b: (b, 0, 0)),
            pl.BlockSpec((1, QLEN, QLEN), lambda b: (b, 0, 0)),
            pl.BlockSpec((3, QLEN, LANES), lambda b: (0, b, 0)),
            pl.BlockSpec((tiles, QLEN, 2 * PER), lambda b: (0, b, 0)),
            pl.BlockSpec((tiles, 1, 2 * PER, QLEN), lambda b: (0, b, 0, 0)),
            pl.BlockSpec((width, SIDE), lambda b: (0, 2 * wide // SIDE)),
            whole((1, width)),
        ],
        [
            ((rows, width), BF),
            ((width, rows), BF),
            ((rows, TILE), F32),
            ((rows, STATE), BF),
            ((rows, STATE), BF),
            ((blocks, QLEN, QLEN), F32),
            ((blocks, QLEN, QLEN), F32),
            ((3, rows, LANES), F32),
            ((tiles, rows, 2 * PER), F32),
            ((tiles, blocks, 2 * PER, QLEN), F32),
            ((width, 2 * wide + SIDE), BF),
            ((1, width), F32),
        ],
        [pltpu.VMEM((QLEN, width), F32), pltpu.VMEM((QLEN + 8, TILE), F32)],
        2 * rows * width * SIDE,
        20 * rows * width,
        starts,
        place,
        keep,
        hidden_in,
        hidden_got,
        shared_taps,
        bias_row,
        decay_row,
        *value_pieces,
        deps=(gate_shard,),
    )

    def tile_cols(n, first=0):
        return pl.BlockSpec((n, TILE), lambda j: (0, j + first))

    def pack_spec(first):
        return pl.BlockSpec((1, rows, 2 * PER), lambda j: (j + first, 0, 0))

    def rowpack_spec(first):
        return pl.BlockSpec((1, blocks, 2 * PER, QLEN), lambda j: (j + first, 0, 0, 0))

    def entry_spec(first):
        return pl.BlockSpec((blocks, TILE, STATE), lambda j: (0, j + first, 0))

    def piece_tiles(pieces, first=0):
        return [
            pl.BlockSpec(p.shape[:2] + (TILE,), lambda j: (0, 0, j + first)) for p in pieces
        ]

    def value_part(first, count, past, deps):
        anywhere = [pl.BlockSpec(memory_space=pl.ANY)] * len(past)
        at = 3 + len(value_pieces) + 7
        return call(
            functools.partial(value_body, len(value_pieces), blocks, len(past)),
            (count,),
            [smem(), smem(), whole((rows, width))]
            + piece_tiles(value_pieces, first)
            + [
                tile_cols(KERNEL, first),
                tile_cols(1, first),
                pack_spec(first),
                rowpack_spec(first),
                whole((rows, STATE)),
                whole((rows, STATE)),
                whole((blocks, QLEN, QLEN)),
            ]
            + anywhere,
            [tile_cols(n, first) for n in (width, rows, rows, rows, rows)] + [entry_spec(first)],
            [
                ((width, 2 * wide + SIDE), BF),
                ((rows, wide), BF),
                ((rows, wide), BF),
                ((rows, wide), BF),
                ((rows, wide), F32),
                ((blocks, wide, STATE), F32),
            ],
            [
                pltpu.VMEM((QLEN, TILE), F32),
                pltpu.VMEM((QLEN + 8, TILE), F32),
                pltpu.VMEM((TILE, STATE), F32),
            ],
            4 * rows * width * count * TILE,
            20 * rows * count * TILE,
            starts,
            keep,
            feat,
            *value_pieces,
            value_taps,
            skip_row,
            pack,
            rowpack,
            b_low,
            c_low,
            gram,
            *past,
            deps=deps,
            aliases={at + i: i for i in range(len(past))},
        )

    cut = tiles // 3
    scanned = value_part(0, cut, (all_w,), ())
    gate_held = tied(gate_ring, scanned[2])
    proj_shard = tied(out_proj.T, gate_held)
    proj_ring = links.ring_parts(proj_shard)
    scanned = value_part(cut, tiles - cut, scanned, (gate_held, proj_shard))
    all_w, pre_low, act_low, slope_low, out_rows, entry = scanned
    gate_pieces = links.gather_rest(gate_held, act_low, cot_got, *proj_ring[1:])
    proj_halves = links.ring_halves(proj_ring)
    proj_others = links.pair_halves(proj_halves)

    grad, grad_t = call(
        functools.partial(mask_body, half_blocks),
        (blocks,),
        [smem(), half_spec, half_spec, block_rows(1)],
        [block_rows(width), pl.BlockSpec((width, QLEN), lambda b: (0, b))],
        [((rows, width), BF), ((width, rows), BF)],
        [],
        rows * width,
        8 * rows * width,
        place,
        cotangent,
        cot_got,
        live.astype(BF),
        deps=(entry,),
    )

    broad = wide // WIDE_TILE

    def broad_cols(n, first=0):
        return pl.BlockSpec((n, WIDE_TILE), lambda j: (0, j + first))

    all_w, gate, squares = call(
        functools.partial(gate_body, len(gate_pieces)),
        (broad,),
        [smem(), whole((rows, width))]
        + [pl.BlockSpec(p.shape[:2] + (WIDE_TILE,), lambda j: (0, 0, j)) for p in gate_pieces]
        + [broad_cols(rows), pl.BlockSpec(memory_space=pl.ANY)],
        [broad_cols(width, broad), broad_cols(rows), whole((rows, LANES))],
        [((width, 2 * wide + SIDE), BF), ((rows, wide), BF), ((rows, LANES), F32)],
        [],
        2 * rows * width * wide,
        12 * rows * wide,
        ordered,
        feat,
        *gate_pieces,
        out_rows,
        all_w,
        aliases={3 + len(gate_pieces): 0},
    )
    square_sum = jnp.sum(squares, axis=1).reshape(8, rows // 8)
    square_sum = square_sum + over_tensor(tied(square_sum, *proj_others[:1]))
    scale = lax.rsqrt(square_sum / INNER + EPSILON).reshape(rows, 1)

    def outer_outs(columns, step, first=0, paired=links.paired, kind=F32):
        if paired:
            spec = pl.BlockSpec((devices // 2, height, step), lambda j: (0, 0, j + first))
            return [spec] * 2, [((devices // 2, height, columns), BF)] * 2
        spec = pl.BlockSpec((width, step), lambda j: (0, j + first))
        return [spec], [((width, columns), kind)]

    both_kind = BF if links.paired else F32
    specs, outs = outer_outs(2 * wide, WIDE_TILE, 0, False, both_kind)
    gated, both_parts = call(
        proj_body,
        (broad,),
        [
            smem(),
            whole((width, rows)),
            broad_cols(rows),
            broad_cols(rows),
            whole((rows, 1)),
            broad_cols(1),
        ],
        [broad_cols(rows)] + specs,
        [((rows, wide), BF)] + outs,
        [],
        2 * rows * width * wide,
        14 * rows * wide,
        core,
        grad_t,
        out_rows,
        gate,
        scale,
        gate_row,
    )
    proj_others = [tied(x, gated) for x in proj_others]
    proj_pieces = links.join_halves(proj_halves, proj_others)

    def swapped(s, place_ref):
        return ((s // half_blocks + 1 - place_ref[0]) % 2) * half_blocks + s % half_blocks

    def swap_rows(n):
        return pl.BlockSpec((QLEN, n), lambda s, p, r: (swapped(s, p), 0))

    proj_w, branch_send, branch_own, row_dot = call(
        functools.partial(branch_body, len(proj_pieces)),
        (blocks,),
        [swap_rows(wide), swap_rows(width)] + [whole(p.shape) for p in proj_pieces],
        [
            whole((width, wide)),
            pl.BlockSpec((QLEN, width), lambda s, p, r: (jnp.minimum(s, half_blocks - 1), 0)),
            pl.BlockSpec((QLEN, width), lambda s, p, r: (jnp.maximum(s - half_blocks, 0), 0)),
            swap_rows(1),
        ],
        [
            ((width, wide), BF),
            ((half_rows, width), BF),
            ((half_rows, width), F32),
            ((rows, 1), F32),
        ],
        [],
        2 * rows * width * wide,
        8 * rows * wide,
        place,
        starts,
        gated,
        grad,
        *proj_pieces,
        prefetch=2,
    )
    row_total = row_dot.reshape(8, rows // 8)
    row_total = (row_total + over_tensor(row_total)).reshape(rows, 1)
    branch_got = over_tensor(branch_send)

    specs, outs = outer_outs(2 * wide, WIDE_TILE, broad, False, both_kind)
    core_grad, all_grad, channel_sums, both_parts = call(
        gating_body,
        (broad,),
        [
            smem(),
            whole((rows, width)),
            broad_cols(width),
            broad_cols(rows),
            broad_cols(rows),
            broad_cols(rows),
            whole((rows, 1)),
            whole((rows, 1)),
            broad_cols(1),
            whole((width, rows)),
            pl.BlockSpec(memory_space=pl.ANY),
        ],
        [broad_cols(rows), broad_cols(rows, broad), broad_cols(2)] + specs,
        [((rows, wide), BF), ((rows, 2 * wide + SIDE), BF), ((2, wide), F32)] + outs,
        [],
        4 * rows * width * wide,
        14 * rows * wide,
        core,
        grad,
        proj_w,
        out_rows,
        gate,
        act_low,
        scale,
        row_total,
        gate_row,
        feat_t,
        both_parts,
        aliases={10: 3},
    )
    both_sum = lax.psum_scatter(both_parts, "dp", scatter_dimension=0, tiled=True).astype(F32)
    proj_sum, gate_sum = both_sum[:, :wide], both_sum[:, wide:]

    def scan_part(first, count, past, grads, parts, columns, deps):
        summed = [whole((blocks, QLEN, QLEN)), whole((rows, STATE)), whole((rows, STATE))]
        specs, outs = outer_outs(columns, TILE, 0 if not parts else first)
        anywhere = [pl.BlockSpec(memory_space=pl.ANY)] * (1 + len(parts))
        at = 16 + len(past)
        return call(
            functools.partial(scan_body, blocks, bool(past), len(specs)),
            (count,),
            [smem(), smem(), whole((width, rows))]
            + [tile_cols(n, first) for n in (rows, rows, rows, rows, rows, 1, KERNEL)]
            + [
                pack_spec(first),
                rowpack_spec(first),
                whole((rows, STATE)),
                whole((rows, STATE)),
                whole((blocks, QLEN, QLEN)),
                entry_spec(first),
            ]
            + (summed if past else [])
            + anywhere,
            specs
            + [tile_cols(rows, first), tile_cols(KERNEL)]
            + summed
            + [pl.BlockSpec((1, rows, 4 * PER), lambda j: (j, 0, 0))],
            outs
            + [
                ((rows, 2 * wide + SIDE), BF),
                ((KERNEL, count * TILE), F32),
                ((blocks, QLEN, QLEN), F32),
                ((rows, STATE), F32),
                ((rows, STATE), F32),
                ((count, rows, 4 * PER), F32),
            ],
            [
                pltpu.VMEM((QLEN + 8, TILE), F32),
                pltpu.VMEM((QLEN + 8, TILE), F32),
                pltpu.VMEM((TILE, STATE), F32),
            ],
            6 * rows * width * count * TILE,
            20 * rows * count * TILE,
            core,
            keep,
            feat_t,
            slope_low,
            core_grad,
            act_low,
            pre_low,
            out_rows,
            skip_row,
            value_taps,
            pack,
            rowpack,
            b_low,
            c_low,
            gram_t,
            entry,
            *past,
            grads,
            *parts,
            deps=deps,
            aliases={at: len(specs), **{at + 1 + i: i for i in range(len(parts))}},
        )

    early = 2 * -(-tiles // 3)
    early_columns = early * TILE
    late_columns = wide - early_columns + SIDE
    *early_parts, all_grad, taps_a, gram_grad, b_grad, c_grad, stats_a = scan_part(
        0, early, (), all_grad, (), early_columns, ()
    )
    early_parts = links.scatter_core(early_parts)
    block_out = call(
        out_body,
        (half_blocks,),
        [block_rows(width)] * 3 + [block_rows(1)],
        [block_rows(width)],
        [((half_rows, width), BF)],
        [],
        half_rows * width,
        10 * half_rows * width,
        branch_own,
        branch_got,
        hidden_in,
        live_own,
        deps=(taps_a,),
    )[0]
    *late_parts, all_grad, taps_c, gram_grad, b_grad, c_grad, stats_c = scan_part(
        early,
        tiles - early,
        (gram_grad, b_grad, c_grad),
        all_grad,
        (),
        late_columns,
        (early_parts[0], block_out),
    )
    early_parts = links.scatter_pair(early_parts)
    taps_part = jnp.concatenate([taps_a, taps_c], axis=1)
    stats = [stats_a, stats_c]

    anywhere = pl.BlockSpec(memory_space=pl.ANY)
    held_shape = (devices // 2, height, SIDE) if links.paired else (width, SIDE)
    held_kind = BF if links.paired else F32
    at = 12 + len(stats)
    *late_parts, all_grad, sharetaps_part, head_sums = call(
        functools.partial(side_body, blocks, len(stats), len(late_parts)),
        (1,),
        [
            smem(),
            smem(),
            anywhere,
            whole((blocks, QLEN, QLEN)),
            whole((rows, STATE)),
            whole((rows, STATE)),
            whole((rows, STATE)),
            whole((rows, STATE)),
            whole((rows, TILE)),
            whole((KERNEL, TILE)),
            whole((3, rows, LANES)),
            whole((1, LANES)),
        ]
        + [whole(part.shape) for part in stats]
        + [anywhere] * (1 + len(late_parts)),
        [anywhere] * len(late_parts)
        + [
            pl.BlockSpec((rows, SIDE), lambda b: (0, 2 * wide // SIDE)),
            whole((KERNEL, TILE)),
            whole((2, LANES)),
        ],
        [(part.shape, part.dtype) for part in late_parts]
        + [((rows, 2 * wide + SIDE), BF), ((KERNEL, TILE), F32), ((2, LANES), F32)],
        [
            pltpu.VMEM((QLEN + 8, TILE), F32),
            pltpu.VMEM((QLEN + 8, TILE), F32),
            pltpu.VMEM((width, rows), BF),
            pltpu.VMEM(held_shape, held_kind),
            pltpu.VMEM(held_shape, held_kind),
            pltpu.SemaphoreType.DMA,
            pltpu.SemaphoreType.DMA((2,)),
        ],
        3 * rows * width * STATE,
        20 * rows * TILE,
        core,
        keep,
        feat_t,
        gram_grad,
        b_grad,
        c_grad,
        b_low,
        c_low,
        shared,
        shared_taps,
        cols,
        decay_row,
        *stats,
        all_grad,
        *late_parts,
        deps=(early_parts[0],),
        aliases={at: len(late_parts), **{at + 1 + i: i for i in range(len(late_parts))}},
    )

    def back(other, kind, deps=()):
        full = 2 * wide + SIDE

        def at(j, p):
            return ((1 - p[0]) if other else p[0], 0)

        return call(
            back_body,
            (width // WIDE_TILE,),
            [
                pl.BlockSpec((half_rows, full), at),
                pl.BlockSpec((WIDE_TILE, full), lambda j, p: (j, 0)),
            ],
            [pl.BlockSpec((half_rows, WIDE_TILE), lambda j, p: (0, j))],
            [((half_rows, width), kind)],
            [],
            2 * rows * width * wide,
            16 * rows * wide,
            place,
            all_grad,
            all_w,
            deps=deps,
            prefetch=1,
        )[0]

    late_parts = links.scatter_core(late_parts, early_parts[0])
    back_send = back(True, BF)
    early_sum = links.scatter_ring(early_parts, back_send)
    back_got = over_tensor(back_send)
    back_own = back(False, F32, (late_parts[0],))
    late_parts = links.scatter_pair(late_parts, back_own)
    input_grad = call(
        input_body,
        (half_blocks,),
        [block_rows(width)] * 4 + [whole((1, width))],
        [block_rows(width)],
        [((half_rows, width), BF)],
        [],
        half_rows * width,
        12 * half_rows * width,
        back_own,
        back_got,
        hidden_in,
        cotangent,
        gain_row,
    )[0]
    late_sum = links.scatter_ring(late_parts, input_grad)

    head_row = jnp.concatenate(
        [
            sharetaps_part.reshape(-1),
            head_sums[0, :heads],
            head_sums[1, :heads],
            jnp.sum(channel_sums[1].reshape(heads, HEAD_DIM), axis=1),
            jnp.zeros((wide - KERNEL * TILE - 3 * heads,), F32),
        ]
    ).reshape(1, wide)
    small = jnp.concatenate([taps_part, channel_sums[0:1], head_row], axis=0)
    small = links.reduce(small, back_send, late_parts[0])
    sharetaps = small[5:6, : KERNEL * TILE]
    sharetaps = sharetaps + over_tensor(sharetaps)

    rest = wide - early_columns
    value_sum = jnp.concatenate([early_sum, late_sum[:, :rest]], axis=1)
    side_sum = late_sum[:, rest : rest + 2 * STATE + heads]
    side_shard = jnp.concatenate([in_shared, in_step], axis=1)
    norm_part = (
        jnp.sum(gate_sum * in_gate.astype(F32), axis=1, keepdims=True)
        + jnp.sum(value_sum * in_value.astype(F32), axis=1, keepdims=True)
        + jnp.sum(side_sum * side_shard.astype(F32), axis=1, keepdims=True)
    ) / norm_gain.astype(F32)[:, None]
    mixed = jnp.concatenate(
        [late_sum[:, rest : rest + 2 * STATE], jnp.broadcast_to(norm_part, (height, LANES))], axis=1
    )
    mixed = mixed + over_tensor(mixed)

    share = KERNEL * TILE
    return (
        block_out,
        input_grad,
        mixed[:, 2 * STATE],
        gate_sum,
        value_sum,
        mixed[:, : 2 * STATE],
        side_sum[:, 2 * STATE :],
        small[0:KERNEL],
        sharetaps.reshape(KERNEL, TILE),
        small[5, share + heads : share + 2 * heads],
        small[5, share : share + heads],
        small[5, share + 2 * heads : share + 3 * heads],
        small[4],
        proj_sum.T,
    )


def solution(mesh):
    in_specs = (
        P(("dp", "tensor"), None),
        P("dp"),
        P("dp"),
        P("dp", "tensor"),
        P("dp", "tensor"),
        P("dp", None),
        P("dp", "tensor"),
        P(None, "tensor"),
        P(),
        P("tensor"),
        P("tensor"),
        P("tensor"),
        P("tensor"),
        P("tensor", "dp"),
        P(("dp", "tensor"), None),
    )
    out_specs = (
        P(("dp", "tensor"), None),
        P(("dp", "tensor"), None),
        P("dp"),
        P("dp", "tensor"),
        P("dp", "tensor"),
        P("dp", None),
        P("dp", "tensor"),
        P(None, "tensor"),
        P(),
        P("tensor"),
        P("tensor"),
        P("tensor"),
        P("tensor"),
        P("tensor", "dp"),
    )
    return jax.shard_map(
        functools.partial(on_device, devices=mesh.shape["dp"]),
        mesh=mesh,
        in_specs=in_specs,
        out_specs=out_specs,
        check_vma=False,
    )
```

```python
import functools

import jax
import jax.numpy as jnp
from jax import lax
from jax.experimental import pallas as pl
from jax.experimental.pallas import tpu as pltpu
from jax.sharding import PartitionSpec as P

HEAD_DIM = 64
STATE = 128
KERNEL = 4
QLEN = 256
INNER = 3072
EPSILON = 1e-05
TILE = 256
SIDE = 384
WIDE_TILE = 512
LANES = 128
HALF = QLEN // 2
PER = TILE // HEAD_DIM

BF = jnp.bfloat16
F32 = jnp.float32
HIGH = lax.Precision.HIGHEST
ROOM = 53 * 1024 * 1024
WEIGHT = 3


def dot(left, right, left_dim=1, right_dim=0, precision=None):
    return lax.dot_general(
        left,
        right,
        (((left_dim,), (right_dim,)), ((), ())),
        preferred_element_type=F32,
        precision=precision,
    )


def iota(shape, dim):
    return lax.broadcasted_iota(jnp.int32, shape, dim)


def split_dot(values, chooser):
    high = values.astype(BF)
    rest = (values - high.astype(F32)).astype(BF)
    return dot(high, chooser) + dot(rest, chooser)


def whole(shape):
    return pl.BlockSpec(shape, lambda *_: (0,) * len(shape))


def smem():
    return pl.BlockSpec(memory_space=pltpu.SMEM)


def call(
    body,
    grid,
    in_specs,
    out_specs,
    out_shape,
    scratch,
    flops,
    moved,
    *args,
    deps=(),
    prefetch=0,
    aliases=None,
):
    count = len(args)

    def held(*refs):
        body(*refs[:count], *refs[count + len(deps) :])

    anywhere = [pl.BlockSpec(memory_space=pl.ANY)] * len(deps)
    return pl.pallas_call(
        held,
        grid_spec=pltpu.PrefetchScalarGridSpec(
            num_scalar_prefetch=prefetch,
            grid=grid,
            in_specs=list(in_specs) + anywhere,
            out_specs=out_specs,
            scratch_shapes=scratch,
        ),
        out_shape=[jax.ShapeDtypeStruct(shape, kind) for shape, kind in out_shape],
        input_output_aliases=aliases or {},
        compiler_params=pltpu.CompilerParams(vmem_limit_bytes=ROOM),
        cost_estimate=pl.CostEstimate(
            flops=flops * WEIGHT, bytes_accessed=moved, transcendentals=0
        ),
    )(*args, *deps)


def tied(value, *deps):
    anywhere = pl.BlockSpec(memory_space=pl.ANY)
    return pl.pallas_call(
        lambda *refs: None,
        in_specs=[anywhere] * (1 + len(deps)),
        out_specs=anywhere,
        out_shape=jax.ShapeDtypeStruct(value.shape, value.dtype),
        input_output_aliases={0: 0},
        compiler_params=pltpu.CompilerParams(vmem_limit_bytes=ROOM),
    )(value, *deps)


def silu_slope(sigma, inputs):
    return sigma * (1.0 + inputs * (1.0 - sigma))


def expand(narrow):
    first = iota((QLEN, LANES), 1) < HEAD_DIM
    parts = []
    for pair in range(PER // 2):
        left = jnp.broadcast_to(narrow[:, 2 * pair : 2 * pair + 1], (QLEN, LANES))
        right = jnp.broadcast_to(narrow[:, 2 * pair + 1 : 2 * pair + 2], (QLEN, LANES))
        parts.append(jnp.where(first, left, right))
    return jnp.concatenate(parts, axis=1)


def head_rows(narrow):
    return jnp.concatenate(
        [jnp.broadcast_to(narrow[:, h : h + 1], (HEAD_DIM, STATE)) for h in range(PER)], axis=0
    )


def lane_masks():
    first = iota((1, LANES), 1) < HEAD_DIM
    return (first.astype(BF), jnp.logical_not(first).astype(BF))


def fill_weight(out_ref, rows_ref, pieces):
    at = 0
    for piece in pieces:
        count, height = piece.shape[0], piece.shape[1]
        for i in range(count):
            start = pl.multiple_of(rows_ref[at], 16) if height % 16 == 0 else rows_ref[at]
            out_ref[pl.ds(start, height), :] = piece[i]
            at += 1


def conv_sum(ext, taps):
    total = taps[KERNEL - 1 : KERNEL, :] * ext[8 : 8 + QLEN, :]
    for lag in range(1, KERNEL):
        total = total + taps[KERNEL - 1 - lag : KERNEL - lag, :] * ext[8 - lag : 8 - lag + QLEN, :]
    return total


def norm_body(
    half_blocks,
    pieces_total,
    gain_lane,
    rows_ref,
    place,
    keep,
    own,
    got,
    taps,
    bias,
    decay,
    *refs,
):
    pieces = refs[:pieces_total]
    (
        feat,
        feat_t,
        shared,
        b_out,
        c_out,
        gram,
        gram_t,
        cols,
        pack,
        rowpack,
        side_w,
        gain,
        hold,
        ext,
    ) = refs[pieces_total:]
    b = pl.program_id(0)
    mine = (b // half_blocks) == place[0]

    @pl.when(b == 0)
    def _():
        fill_weight(side_w, rows_ref, pieces)
        edge = gain_lane // LANES * LANES
        spread = side_w[:, edge : edge + LANES].astype(F32).T
        gain[...] = spread[gain_lane - edge : gain_lane - edge + 1, :]

    @pl.when(mine)
    def _():
        hold[...] = own[...].astype(F32)

    @pl.when(jnp.logical_not(mine))
    def _():
        hold[...] = got[...].astype(F32)

    rows = hold[...]
    inverse = lax.rsqrt(jnp.mean(rows * rows, axis=1, keepdims=True) + EPSILON)
    normed = (rows * inverse * gain[...]).astype(BF)
    feat[...] = normed
    feat_t[...] = normed.T
    side = dot(normed, side_w[...])
    pre = side[:, :TILE]
    shared[...] = pre

    @pl.when(b == 0)
    def _():
        ext[...] = jnp.zeros_like(ext)

    ext[0:8, :] = ext[QLEN : QLEN + 8, :] * keep[b]
    ext[8 : 8 + QLEN, :] = pre
    conv = conv_sum(ext, taps)
    act = (conv * jax.nn.sigmoid(conv)).astype(BF)
    b_low = act[:, :STATE]
    c_low = act[:, STATE:]
    b_out[...] = b_low
    c_out[...] = c_low
    lower = iota((QLEN, QLEN), 0) >= iota((QLEN, QLEN), 1)
    upper = iota((QLEN, QLEN), 0) <= iota((QLEN, QLEN), 1)
    gram[0] = jnp.where(lower, dot(c_low, b_low, 1, 1), 0.0)
    gram_t[0] = jnp.where(upper, dot(b_low, c_low, 1, 1), 0.0)
    raw = side[:, TILE:] + bias[...]
    step = jnp.maximum(raw, 0.0) + jnp.log1p(jnp.exp(-jnp.abs(raw)))
    logdec = step * -jnp.exp(decay[...])
    cum = dot(lower.astype(F32), logdec, precision=HIGH)
    cols[0] = raw
    cols[1] = step
    cols[2] = logdec
    cum_t = cum.T
    step_t = step.T
    for j in range(pack.shape[0]):
        heads = slice(PER * j, PER * j + PER)
        pack[j] = jnp.concatenate([cum[:, heads], step[:, heads]], axis=1)
        rowpack[j, 0] = jnp.concatenate([cum_t[heads, :], step_t[heads, :]], axis=0)


def value_body(
    pieces_total,
    blocks,
    past,
    rows_ref,
    keep,
    feat,
    *refs,
):
    pieces = refs[:pieces_total]
    refs = refs[: pieces_total + 7] + refs[pieces_total + 7 + past :]
    (
        taps,
        skip,
        pack,
        rowpack,
        b_ref,
        c_ref,
        gram,
        weight,
        pre_out,
        act_out,
        slope_out,
        out_rows,
        entry,
        pre,
        ext,
        state,
    ) = refs[pieces_total:]
    fill_weight(weight, rows_ref, pieces)
    masks = lane_masks()
    for b in range(blocks):
        span = slice(b * QLEN, (b + 1) * QLEN)
        pre[...] = dot(feat[span, :], weight[...])
        pre_out[span, :] = pre[...].astype(BF)
        if b == 0:
            ext[0:8, :] = jnp.zeros((8, TILE), F32)
            state[...] = jnp.zeros_like(state)
        else:
            ext[0:8, :] = ext[QLEN : QLEN + 8, :] * keep[b]
        ext[8 : 8 + QLEN, :] = pre[...]
        conv = conv_sum(ext, taps)
        sigma = jax.nn.sigmoid(conv)
        act_low = (conv * sigma).astype(BF)
        act_out[span, :] = act_low
        slope_out[span, :] = silu_slope(sigma, conv).astype(BF)
        act = act_low.astype(F32)
        narrow = pack[0, span, :]
        cum = narrow[:, :PER]
        step = narrow[:, PER:]
        last = cum[QLEN - 1 : QLEN, :]
        stepped = (act * expand(step)).astype(BF)
        scaled = (act * expand(jnp.exp(last - cum) * step)).astype(BF)
        row_cum = rowpack[0, b]
        parts = []
        for pair in range(PER // 2):
            lanes = slice(pair * LANES, (pair + 1) * LANES)
            tops, lows, values = [], [], []
            for k in range(2):
                h = 2 * pair + k
                col = cum[:, h : h + 1]
                row = row_cum[h : h + 1, :]
                e00 = jnp.exp(jnp.minimum(col[:HALF] - row[:, :HALF], 0.0))
                e10 = jnp.exp(col[HALF:] - row[:, :HALF])
                e11 = jnp.exp(jnp.minimum(col[HALF:] - row[:, HALF:], 0.0))
                tops.append((gram[b, :HALF, :HALF] * e00).astype(BF))
                lows.append((gram[b, HALF:, :HALF] * e10).astype(BF))
                lows.append((gram[b, HALF:, HALF:] * e11).astype(BF))
                values.append(stepped[:, lanes] * masks[k])
            top = dot(
                jnp.concatenate(tops, axis=1),
                jnp.concatenate([v[:HALF] for v in values], axis=0),
            )
            low = dot(jnp.concatenate(lows, axis=1), jnp.concatenate(values, axis=0))
            parts.append(jnp.concatenate([top, low], axis=0))
        within = jnp.concatenate(parts, axis=1)
        held = state[...]
        entry[b] = held
        across = dot(c_ref[span, :], held.astype(BF), 1, 1)
        core = within + across * expand(jnp.exp(cum))
        out_rows[span, :] = core + act * skip[...]
        if b + 1 < blocks:
            fresh = dot(scaled, b_ref[span, :], 0, 0)
            state[...] = keep[b + 1] * (head_rows(jnp.exp(last)) * held + fresh)


def gate_body(pieces_total, rows_ref, feat, *refs):
    pieces = refs[:pieces_total]
    out_rows, _, weight, gate_out, squares = refs[pieces_total:]
    fill_weight(weight, rows_ref, pieces)

    @pl.when(pl.program_id(0) == 0)
    def _():
        squares[...] = jnp.zeros_like(squares)

    for b in range(feat.shape[0] // QLEN):
        span = slice(b * QLEN, (b + 1) * QLEN)
        gate = dot(feat[span, :], weight[...])
        gate_out[span, :] = gate.astype(BF)
        product = out_rows[span, :] * (gate * jax.nn.sigmoid(gate))
        power = product * product
        total = squares[span, :]
        for at in range(0, power.shape[1], LANES):
            total = total + power[:, at : at + LANES]
        squares[span, :] = total


def mask_body(half_blocks, place, own, got, live, out, out_t):
    b = pl.program_id(0)
    mine = (b // half_blocks) == place[0]

    @pl.when(mine)
    def _():
        out[...] = own[...] * live[...]

    @pl.when(jnp.logical_not(mine))
    def _():
        out[...] = got[...] * live[...]

    out_t[...] = out[...].T


def proj_body(place, left, out_rows, gate_ref, scale_ref, gain, gated_out, *outs):
    for b in range(gated_out.shape[0] // QLEN):
        span = slice(b * QLEN, (b + 1) * QLEN)
        gate = gate_ref[span, :].astype(F32)
        product = out_rows[span, :] * (gate * jax.nn.sigmoid(gate))
        gated_out[span, :] = (product * scale_ref[span, :] * gain[...]).astype(BF)
    emit_outer(place, dot(left[...], gated_out[...]), outs)


def branch_body(pieces_total, place, rows_ref, gated, grad, *refs):
    pieces = refs[:pieces_total]
    weight, send, mine, row_dot = refs[pieces_total:]
    s = pl.program_id(0)

    @pl.when(s == 0)
    def _():
        fill_weight(weight, rows_ref, pieces)

    branch = dot(gated[...], weight[...], 1, 1)
    row_dot[...] = jnp.sum(branch * grad[...].astype(F32), axis=1, keepdims=True)

    @pl.when(s < pl.num_programs(0) // 2)
    def _():
        send[...] = branch.astype(BF)

    @pl.when(s >= pl.num_programs(0) // 2)
    def _():
        mine[...] = branch


def gating_body(
    place,
    grad,
    weight,
    out_ref,
    gate_ref,
    act_ref,
    scale_ref,
    row_dot,
    gain,
    feat_t,
    _,
    core,
    gate_grad,
    sums,
    *outs,
):
    gating = jnp.zeros(gain.shape, F32)
    skipping = jnp.zeros(gain.shape, F32)
    for b in range(grad.shape[0] // QLEN):
        span = slice(b * QLEN, (b + 1) * QLEN)
        grad_gated = dot(grad[span, :], weight[...])
        gate = gate_ref[span, :].astype(F32)
        sigma = jax.nn.sigmoid(gate)
        act = gate * sigma
        out_rows = out_ref[span, :]
        scale = scale_ref[span, :]
        normal = out_rows * act * scale
        gating = gating + jnp.sum(grad_gated * normal, axis=0, keepdims=True)
        grad_product = scale * (
            grad_gated * gain[...] - normal * (row_dot[span, :] * (1.0 / INNER))
        )
        grad_out = grad_product * act
        core[span, :] = grad_out.astype(BF)
        gate_grad[span, :] = (grad_product * out_rows * silu_slope(sigma, gate)).astype(BF)
        skipping = skipping + jnp.sum(
            grad_out * act_ref[span, :].astype(F32), axis=0, keepdims=True
        )
    sums[...] = jnp.concatenate([gating, skipping], axis=0)
    emit_outer(place, dot(feat_t[...], gate_grad[...]), outs)


def scan_body(
    blocks,
    summed,
    outer_outs,
    place,
    keep,
    feat_t,
    slope_ref,
    core_ref,
    act_ref,
    pre_ref,
    out_ref,
    skip,
    taps,
    pack,
    rowpack,
    b_ref,
    c_ref,
    gram_t,
    entry,
    *refs,
):
    past = refs[:3] if summed else ()
    own = len(refs) - 9 - outer_outs
    outs = refs[own : own + outer_outs]
    grad_pre, taps_grad, gram_grad, b_grad, c_grad, stats = refs[own + outer_outs : -3]
    ext, tail, carry = refs[-3:]

    @pl.when(pl.program_id(0) == 0)
    def _():
        if past:
            gram_grad[...] = past[0][...]
            b_grad[...] = past[1][...]
            c_grad[...] = past[2][...]
        else:
            gram_grad[...] = jnp.zeros_like(gram_grad)
            b_grad[...] = jnp.zeros_like(b_grad)
            c_grad[...] = jnp.zeros_like(c_grad)

    masks = lane_masks()
    owner = iota((TILE, LANES), 0) // HEAD_DIM
    lane = iota((TILE, LANES), 1)
    chooser = [(lane == owner + PER * q).astype(BF) for q in range(4)]
    final_row = iota((QLEN, LANES), 0) == QLEN - 1
    ones = jnp.ones((8, STATE), BF)
    tap_sums = [jnp.zeros((1, TILE), F32) for _ in range(KERNEL)]
    for b in reversed(range(blocks)):
        span = slice(b * QLEN, (b + 1) * QLEN)
        final = b == blocks - 1
        grad_low = core_ref[span, :]
        grad = grad_low.astype(F32)
        act = act_ref[span, :].astype(F32)
        narrow = pack[0, span, :]
        cum = narrow[:, :PER]
        step = narrow[:, PER:]
        last = cum[QLEN - 1 : QLEN, :]
        step_wide = expand(step)
        stepped = (act * step_wide).astype(BF)
        row_cum = rowpack[0, b]
        parts = []
        upper_sum = None
        lower_sum = None
        for pair in range(PER // 2):
            lanes = slice(pair * LANES, (pair + 1) * LANES)
            grad_pair = grad_low[:, lanes]
            tops, lows, grads = [], [], []
            for k in range(2):
                h = 2 * pair + k
                col = cum[:, h : h + 1]
                row = row_cum[h : h + 1, :]
                e00 = jnp.exp(jnp.minimum(row[:, :HALF] - col[:HALF], 0.0))
                e01 = jnp.exp(row[:, HALF:] - col[:HALF])
                e11 = jnp.exp(jnp.minimum(row[:, HALF:] - col[HALF:], 0.0))
                value = stepped[:, lanes] * masks[k]
                upper = dot(value[:HALF], grad_pair, 1, 1) * jnp.concatenate([e00, e01], axis=1)
                lower = dot(value[HALF:], grad_pair[HALF:], 1, 1) * e11
                upper_sum = upper if upper_sum is None else upper_sum + upper
                lower_sum = lower if lower_sum is None else lower_sum + lower
                tops.append((gram_t[b, :HALF, :HALF] * e00).astype(BF))
                tops.append((gram_t[b, :HALF, HALF:] * e01).astype(BF))
                lows.append((gram_t[b, HALF:, HALF:] * e11).astype(BF))
                grads.append(grad_pair * masks[k])
            top = dot(jnp.concatenate(tops, axis=1), jnp.concatenate(grads, axis=0))
            low = dot(
                jnp.concatenate(lows, axis=1),
                jnp.concatenate([g[HALF:] for g in grads], axis=0),
            )
            parts.append(jnp.concatenate([top, low], axis=0))
        gram_grad[b, :HALF, :] += upper_sum
        gram_grad[b, HALF:, HALF:] += lower_sum
        mixed = jnp.concatenate(parts, axis=1)
        between = out_ref[span, :] - act * skip[...]
        flows = stepped.astype(F32) * mixed
        grad_value = step_wide * mixed + skip[...] * grad
        held = entry[b]
        across_low = (grad * expand(jnp.exp(cum))).astype(BF)
        c_grad[span, :] += dot(across_low, held.astype(BF))
        totals = split_dot(grad * between, chooser[1])
        if not final:
            states = carry[...]
            states_low = states.astype(BF)
            weights = expand(jnp.exp(last - cum) * step)
            pulled = dot(b_ref[span, :], states_low, 1, 1) * weights
            grad_value = grad_value + pulled
            weighted = act * pulled
            scaled = (act * weights).astype(BF)
            b_grad[span, :] += dot(scaled, states_low)
            totals = totals + split_dot(flows + weighted, chooser[0])
            passed = head_rows(jnp.exp(last)) * states
            spread = passed * held
            high = spread.astype(BF)
            rest = (spread - high.astype(F32)).astype(BF)
            summed = dot(ones, high, 1, 1) + dot(ones, rest, 1, 1)
            row_sum = jnp.broadcast_to(jnp.sum(weighted, axis=0, keepdims=True), (8, TILE))
            last_sum = split_dot(summed, chooser[3]) + split_dot(row_sum, chooser[2])
            totals = totals + jnp.where(final_row, last_sum[0:1, :], 0.0)
        else:
            totals = totals + split_dot(flows, chooser[0])
        stats[0, span, :] = totals[:, : 4 * PER]
        if b > 0:
            fresh = dot(across_low, c_ref[span, :], 0, 0)
            carry[...] = keep[b] * (fresh if final else fresh + passed)
        if b > 0:
            ext[0:8, :] = pre_ref[b * QLEN - 16 : b * QLEN, :].astype(F32)[8:, :] * keep[b]
        else:
            ext[0:8, :] = jnp.zeros((8, TILE), F32)
        ext[8 : 8 + QLEN, :] = pre_ref[span, :].astype(F32)
        slope = grad_value * slope_ref[span, :].astype(F32)
        for lag in range(KERNEL):
            tap_sums[KERNEL - 1 - lag] = tap_sums[KERNEL - 1 - lag] + jnp.sum(
                slope * ext[8 - lag : 8 - lag + QLEN, :], axis=0, keepdims=True
            )
        if final:
            tail[QLEN : QLEN + 8, :] = jnp.zeros((8, TILE), F32)
        else:
            tail[QLEN : QLEN + 8, :] = tail[0:8, :] * keep[b + 1]
        tail[0:QLEN, :] = slope
        pulled_back = taps[KERNEL - 1 : KERNEL, :] * slope
        for lag in range(1, KERNEL):
            pulled_back = (
                pulled_back
                + taps[KERNEL - 1 - lag : KERNEL - lag, :] * tail[lag : lag + QLEN, :]
            )
        grad_pre[span, :] = pulled_back.astype(BF)
    taps_grad[...] = jnp.concatenate(tap_sums, axis=0)
    emit_outer(place, dot(feat_t[...], grad_pre[...]), outs)


def side_body(
    blocks,
    tiles_total,
    aliased,
    place,
    keep,
    feat_hbm,
    gram_grad,
    b_grad,
    c_grad,
    b_ref,
    c_ref,
    shared,
    taps,
    cols,
    decay,
    *refs,
):
    stats = refs[:tiles_total]
    outs = refs[tiles_total + 1 + aliased : -10]
    out, taps_grad, sums, ext, tail, feat_t, first, second, feat_sem, sems = refs[-10:]
    loading = pltpu.make_async_copy(feat_hbm, feat_t, feat_sem)
    loading.start()
    lower = iota((QLEN, QLEN), 0) >= iota((QLEN, QLEN), 1)
    upper = iota((QLEN, QLEN), 0) <= iota((QLEN, QLEN), 1)
    final_row = iota((QLEN, LANES), 0) == QLEN - 1
    rate = jnp.exp(decay[...])
    tap_sums = [jnp.zeros((1, TILE), F32) for _ in range(KERNEL)]
    decay_sum = jnp.zeros((1, LANES), F32)
    bias_sum = jnp.zeros((1, LANES), F32)
    tiles = sum(part.shape[0] for part in stats)
    padding = jnp.zeros((QLEN, LANES - PER * tiles), F32)
    for b in reversed(range(blocks)):
        span = slice(b * QLEN, (b + 1) * QLEN)
        final = b == blocks - 1
        gathered = [
            jnp.concatenate(
                [
                    part[j, span, PER * q : PER * q + PER]
                    for part in stats
                    for j in range(part.shape[0])
                ]
                + [padding],
                axis=1,
            )
            for q in range(4)
        ]
        pulled = gathered[0]
        grad_cum = gathered[1] - pulled + gathered[3]
        grad_cum = grad_cum + jnp.where(
            final_row, jnp.sum(gathered[2], axis=0, keepdims=True), 0.0
        )
        grad_log = dot(upper.astype(F32), grad_cum, precision=HIGH)
        raw = cols[0, span, :]
        step = cols[1, span, :]
        sigma = jax.nn.sigmoid(raw)
        ratio = jnp.where(raw < -20.0, 1.0, sigma / jnp.maximum(step, 1e-30))
        grad_raw = pulled * ratio - rate * grad_log * sigma
        decay_sum = decay_sum + jnp.sum(grad_log * cols[2, span, :], axis=0, keepdims=True)
        bias_sum = bias_sum + jnp.sum(grad_raw, axis=0, keepdims=True)
        out[span, TILE:] = grad_raw.astype(BF)
        gram_low = jnp.where(upper, gram_grad[b], 0.0).astype(BF)
        b_total = b_grad[span, :] + dot(gram_low, c_ref[span, :])
        c_total = c_grad[span, :] + dot(gram_low, b_ref[span, :], 0, 0)
        grad_act = jnp.concatenate([b_total, c_total], axis=1)
        if b > 0:
            ext[0:8, :] = shared[b * QLEN - 8 : b * QLEN, :] * keep[b]
        else:
            ext[0:8, :] = jnp.zeros((8, TILE), F32)
        ext[8 : 8 + QLEN, :] = shared[span, :]
        conv = conv_sum(ext, taps)
        slope = grad_act * silu_slope(jax.nn.sigmoid(conv), conv)
        for lag in range(KERNEL):
            tap_sums[KERNEL - 1 - lag] = tap_sums[KERNEL - 1 - lag] + jnp.sum(
                slope * ext[8 - lag : 8 - lag + QLEN, :], axis=0, keepdims=True
            )
        if final:
            tail[QLEN : QLEN + 8, :] = jnp.zeros((8, TILE), F32)
        else:
            tail[QLEN : QLEN + 8, :] = tail[0:8, :] * keep[b + 1]
        tail[0:QLEN, :] = slope
        pulled_back = taps[KERNEL - 1 : KERNEL, :] * slope
        for lag in range(1, KERNEL):
            pulled_back = (
                pulled_back
                + taps[KERNEL - 1 - lag : KERNEL - lag, :] * tail[lag : lag + QLEN, :]
            )
        out[span, :TILE] = pulled_back.astype(BF)
    taps_grad[...] = jnp.concatenate(tap_sums, axis=0)
    sums[...] = jnp.concatenate([decay_sum, bias_sum], axis=0)
    loading.wait()
    held = (first, second)[: len(outs)]
    emit_outer(place, dot(feat_t[...], out[...]), held)
    moves = []
    for i, (target, source) in enumerate(zip(outs, held)):
        start = target.shape[-1] - SIDE
        view = target.at[..., pl.ds(start, SIDE)]
        moves.append(pltpu.make_async_copy(source, view, sems.at[i]))
    for move in moves:
        move.start()
    for move in moves:
        move.wait()


def emit_outer(place, total, outs):
    if len(outs) == 1:
        outs[0][...] = total.astype(outs[0].dtype)
        return
    mine, send = outs
    low = total.astype(BF).reshape(mine.shape[0], 2, mine.shape[1], total.shape[1])

    @pl.when(place[0] == 0)
    def _():
        mine[...] = low[:, 0]
        send[...] = low[:, 1]

    @pl.when(place[0] == 1)
    def _():
        mine[...] = low[:, 1]
        send[...] = low[:, 0]


def outer_body(place, left, right, *outs):
    emit_outer(place, dot(left[...], right[...]), outs)


def back_body(place, grads, weights, out):
    out[...] = dot(grads[...], weights[...], 1, 1).astype(out.dtype)


def input_body(mine, got, hidden, cot, gain, out):
    total = (mine[...] + got[...].astype(F32)) * gain[...]
    rows = hidden[...].astype(F32)
    inverse = lax.rsqrt(jnp.mean(rows * rows, axis=1, keepdims=True) + EPSILON)
    hat = rows * inverse
    spread = jnp.mean(total * hat, axis=1, keepdims=True)
    out[...] = (cot[...].astype(F32) + (total - hat * spread) * inverse).astype(BF)


def out_body(mine, got, hidden, live, out):
    out[...] = (
        hidden[...].astype(F32) + live[...] * (mine[...] + got[...].astype(F32))
    ).astype(BF)


class Links:
    def __init__(self, devices, shard_rows):
        self.devices = devices
        self.height = shard_rows
        self.paired = devices % 4 == 0 and shard_rows % 16 == 0
        self.ring = max(devices // 4, 1)
        spot = lax.axis_index("dp")
        self.a, self.b, self.c = spot // 4, (spot // 2) % 2, spot % 2
        self.spot = spot

    def moved(self, rule):
        pairs = []
        for a in range(self.ring):
            for b in range(2):
                for c in range(2):
                    ta, tb, tc = rule(a, b, c)
                    pairs.append(((a * 2 + b) * 2 + c, (ta * 2 + tb) * 2 + tc))
        return pairs

    def over_core(self, x):
        return lax.ppermute(x, "dp", self.moved(lambda a, b, c: (a, b, 1 - c)))

    def over_pair(self, x):
        return lax.ppermute(x, "dp", self.moved(lambda a, b, c: (a, 1 - b, c)))

    def over_ring(self, x, k):
        return lax.ppermute(x, "dp", self.moved(lambda a, b, c: ((a + k) % self.ring, b, c)))

    def gather_fast(self, shard):
        if not self.paired:
            return [lax.all_gather(shard, "dp", axis=0, tiled=True)[None]], (shard,)
        near = [k for k in range(1, self.ring) if k in (1, self.ring - 1)]
        far = [k for k in range(1, self.ring) if k not in near]
        held = {0: shard}
        other = {0: self.over_pair(shard)}
        for k in near:
            held[k] = self.over_ring(shard, k)
        later = tied(shard, other[0], *[held[k] for k in near])
        for k in far:
            held[k] = self.over_ring(later, k)
        for k in near + far:
            other[k] = self.over_pair(held[k])
        pieces = [held[k] for k in range(self.ring)] + [other[k] for k in range(self.ring)]
        pieces = pieces + [self.over_core(x) for x in pieces]
        return [x[None] for x in pieces], (held[(near + far)[-1]], other[near[0]])

    def ring_parts(self, shard):
        if not self.paired:
            return [shard]
        return [shard] + [self.over_ring(shard, k) for k in range(1, self.ring)]

    def ring_stack(self, parts, *deps):
        if not self.paired:
            return parts[0]
        return jnp.stack(parts[:-1] + [tied(parts[-1], *deps)])

    def gather_rest(self, held, *deps):
        if not self.paired:
            return [lax.all_gather(held, "dp", axis=0, tiled=True)[None]]
        other = tied(self.over_pair(held), *deps)
        return [held, other, self.over_core(held), self.over_core(other)]

    def ring_halves(self, parts):
        if not self.paired:
            return [parts[0]]
        cut = max(self.ring // 2, 1)
        return [jnp.stack(parts[:cut])] + ([jnp.stack(parts[cut:])] if parts[cut:] else [])

    def pair_halves(self, halves):
        return [self.over_pair(h) for h in halves] if self.paired else []

    def join_halves(self, halves, others):
        if not self.paired:
            return [lax.all_gather(halves[0], "dp", axis=0, tiled=True)[None]]
        pieces = halves + others
        return pieces + [self.over_core(x) for x in pieces]

    def ring_gather(self, shard):
        if not self.paired:
            return shard
        return self.over_rings(jnp.broadcast_to(shard[None], (self.ring,) + shard.shape))

    def starts(self, rings):
        if not self.paired:
            return jnp.zeros((1,), jnp.int32)
        rows = []
        for c in (self.c, 1 - self.c):
            for b in (self.b, 1 - self.b):
                rows += [((a * 2 + b) * 2 + c) * self.height for a in rings]
        return jnp.stack(rows).astype(jnp.int32)

    def scatter_core(self, parts, *deps):
        if not self.paired:
            return parts
        mine, send = parts
        send = tied(send, *deps) if deps else send
        shape = (self.ring, 2) + mine.shape[1:]
        got = self.over_core(send)
        mine, got = mine.reshape(shape), got.reshape(shape)
        away = self.pick(mine, 1 - self.b, 1).astype(F32) + self.pick(got, 1 - self.b, 1).astype(F32)
        return [away.astype(BF), mine, got]

    def pick(self, x, i, dim):
        return lax.dynamic_index_in_dim(x, i, dim, keepdims=False)

    def scatter_pair(self, parts, *deps):
        if not self.paired:
            return parts
        away, mine, got = parts
        near = tied(self.over_pair(away), *deps) if deps else self.over_pair(away)

        total = self.pick(mine, self.b, 1).astype(F32) + self.pick(got, self.b, 1).astype(F32)
        return [(total + near.astype(F32)).astype(BF)]

    def over_rings(self, x):
        groups = [
            [(a * 2 + b) * 2 + c for a in range(self.ring)] for b in range(2) for c in range(2)
        ]
        return lax.all_to_all(x, "dp", 0, 0, tiled=True, axis_index_groups=groups)

    def scatter_ring(self, parts, *deps):
        if not self.paired:
            return lax.psum_scatter(parts[0], "dp", scatter_dimension=0, tiled=True)
        moved = self.over_rings(parts[0])
        if deps:
            moved = tied(moved, *deps)
        return jnp.sum(moved.astype(F32), axis=0)

    def reduce(self, x, first, second):
        if not self.paired:
            return lax.psum(x, "dp")
        x = tied(x + self.over_core(x), first)
        x = tied(x + self.over_pair(x), second)
        total = x
        for k in range(1, self.ring):
            total = total + self.over_ring(x, k)
        return total


def over_tensor(x):
    return lax.ppermute(x, "tensor", [(0, 1), (1, 0)])


def on_device(
    hidden_in,
    segment,
    norm_gain,
    in_gate,
    in_value,
    in_shared,
    in_step,
    value_taps,
    shared_taps,
    step_bias,
    decay_log,
    skip_gain,
    gate_gain,
    out_proj,
    cotangent,
    devices,
):
    half_rows, width = hidden_in.shape
    rows = segment.shape[0]
    blocks = rows // QLEN
    half_blocks = half_rows // QLEN
    wide = in_value.shape[1]
    tiles = wide // TILE
    heads = step_bias.shape[0]
    height = in_value.shape[0]
    links = Links(devices, height)
    tensor = lax.axis_index("tensor")
    place = jnp.reshape(tensor, (1,)).astype(jnp.int32)
    core = jnp.reshape(links.c, (1,)).astype(jnp.int32)

    firsts = segment[::QLEN]
    keep = jnp.concatenate(
        [jnp.zeros((1,), F32), (firsts[1:] == firsts[:-1]).astype(F32)]
    )
    live = (segment >= 0).astype(F32)[:, None]
    live_own = lax.dynamic_slice_in_dim(live, tensor * half_rows, half_rows)
    pad = SIDE - 2 * STATE - heads - 1
    value_shard = jnp.concatenate(
        [in_value, in_shared, in_step, norm_gain[:, None], jnp.zeros((height, pad), BF)], axis=1
    )
    hidden_got = over_tensor(hidden_in)
    ring = range(links.ring)
    starts = links.starts([lax.rem(links.a - k + links.ring, links.ring) for k in ring])
    ordered = links.starts(ring)
    value_pieces, value_last = links.gather_fast(value_shard)
    gate_shard = tied(in_gate, *value_last)
    gate_ring = links.ring_gather(gate_shard)
    cot_got = over_tensor(cotangent)

    bias_row = jnp.pad(step_bias, (0, LANES - heads)).reshape(1, LANES)
    decay_row = jnp.pad(decay_log, (0, LANES - heads)).reshape(1, LANES)
    skip_row = jnp.repeat(skip_gain, HEAD_DIM).reshape(1, wide)
    gate_row = gate_gain.reshape(1, wide)

    block_rows = lambda n: pl.BlockSpec((QLEN, n), lambda b, *_: (b, 0))
    half_spec = pl.BlockSpec((QLEN, width), lambda b, *_: (b % half_blocks, 0))
    (
        feat,
        feat_t,
        shared,
        b_low,
        c_low,
        gram,
        gram_t,
        cols,
        pack,
        rowpack,
        all_w,
        gain_row,
    ) = call(
        functools.partial(norm_body, half_blocks, len(value_pieces), 2 * STATE + heads),
        (blocks,),
        [
            smem(),
            smem(),
            smem(),
            half_spec,
            half_spec,
            whole((KERNEL, TILE)),
            whole((1, LANES)),
            whole((1, LANES)),
        ]
        + [
            pl.BlockSpec(p.shape[:2] + (SIDE,), lambda b: (0, 0, wide // SIDE))
            for p in value_pieces
        ],
        [
            block_rows(width),
            pl.BlockSpec((width, QLEN), lambda b: (0, b)),
            block_rows(TILE),
            block_rows(STATE),
            block_rows(STATE),
            pl.BlockSpec((1, QLEN, QLEN), lambda b: (b, 0, 0)),
            pl.BlockSpec((1, QLEN, QLEN), lambda b: (b, 0, 0)),
            pl.BlockSpec((3, QLEN, LANES), lambda b: (0, b, 0)),
            pl.BlockSpec((tiles, QLEN, 2 * PER), lambda b: (0, b, 0)),
            pl.BlockSpec((tiles, 1, 2 * PER, QLEN), lambda b: (0, b, 0, 0)),
            pl.BlockSpec((width, SIDE), lambda b: (0, 2 * wide // SIDE)),
            whole((1, width)),
        ],
        [
            ((rows, width), BF),
            ((width, rows), BF),
            ((rows, TILE), F32),
            ((rows, STATE), BF),
            ((rows, STATE), BF),
            ((blocks, QLEN, QLEN), F32),
            ((blocks, QLEN, QLEN), F32),
            ((3, rows, LANES), F32),
            ((tiles, rows, 2 * PER), F32),
            ((tiles, blocks, 2 * PER, QLEN), F32),
            ((width, 2 * wide + SIDE), BF),
            ((1, width), F32),
        ],
        [pltpu.VMEM((QLEN, width), F32), pltpu.VMEM((QLEN + 8, TILE), F32)],
        2 * rows * width * SIDE,
        20 * rows * width,
        starts,
        place,
        keep,
        hidden_in,
        hidden_got,
        shared_taps,
        bias_row,
        decay_row,
        *value_pieces,
        deps=(gate_shard,),
    )

    def tile_cols(n, first=0):
        return pl.BlockSpec((n, TILE), lambda j: (0, j + first))

    def pack_spec(first):
        return pl.BlockSpec((1, rows, 2 * PER), lambda j: (j + first, 0, 0))

    def rowpack_spec(first):
        return pl.BlockSpec((1, blocks, 2 * PER, QLEN), lambda j: (j + first, 0, 0, 0))

    def entry_spec(first):
        return pl.BlockSpec((blocks, TILE, STATE), lambda j: (0, j + first, 0))

    def piece_tiles(pieces, first=0):
        return [
            pl.BlockSpec(p.shape[:2] + (TILE,), lambda j: (0, 0, j + first)) for p in pieces
        ]

    def value_part(first, count, past, deps):
        anywhere = [pl.BlockSpec(memory_space=pl.ANY)] * len(past)
        at = 3 + len(value_pieces) + 7
        return call(
            functools.partial(value_body, len(value_pieces), blocks, len(past)),
            (count,),
            [smem(), smem(), whole((rows, width))]
            + piece_tiles(value_pieces, first)
            + [
                tile_cols(KERNEL, first),
                tile_cols(1, first),
                pack_spec(first),
                rowpack_spec(first),
                whole((rows, STATE)),
                whole((rows, STATE)),
                whole((blocks, QLEN, QLEN)),
            ]
            + anywhere,
            [tile_cols(n, first) for n in (width, rows, rows, rows, rows)] + [entry_spec(first)],
            [
                ((width, 2 * wide + SIDE), BF),
                ((rows, wide), BF),
                ((rows, wide), BF),
                ((rows, wide), BF),
                ((rows, wide), F32),
                ((blocks, wide, STATE), F32),
            ],
            [
                pltpu.VMEM((QLEN, TILE), F32),
                pltpu.VMEM((QLEN + 8, TILE), F32),
                pltpu.VMEM((TILE, STATE), F32),
            ],
            4 * rows * width * count * TILE,
            20 * rows * count * TILE,
            starts,
            keep,
            feat,
            *value_pieces,
            value_taps,
            skip_row,
            pack,
            rowpack,
            b_low,
            c_low,
            gram,
            *past,
            deps=deps,
            aliases={at + i: i for i in range(len(past))},
        )

    cut = tiles // 3
    scanned = value_part(0, cut, (all_w,), ())
    gate_held = tied(gate_ring, scanned[2])
    proj_shard = tied(out_proj.T, gate_held)
    proj_ring = links.ring_parts(proj_shard)
    scanned = value_part(cut, tiles - cut, scanned, (gate_held, proj_shard))
    all_w, pre_low, act_low, slope_low, out_rows, entry = scanned
    gate_pieces = links.gather_rest(gate_held, act_low, cot_got, *proj_ring[1:])
    proj_halves = links.ring_halves(proj_ring)
    proj_others = links.pair_halves(proj_halves)

    broad = wide // WIDE_TILE

    def broad_cols(n, first=0):
        return pl.BlockSpec((n, WIDE_TILE), lambda j: (0, j + first))

    all_w, gate, squares = call(
        functools.partial(gate_body, len(gate_pieces)),
        (broad,),
        [smem(), whole((rows, width))]
        + [pl.BlockSpec(p.shape[:2] + (WIDE_TILE,), lambda j: (0, 0, j)) for p in gate_pieces]
        + [broad_cols(rows), pl.BlockSpec(memory_space=pl.ANY)],
        [broad_cols(width, broad), broad_cols(rows), whole((rows, LANES))],
        [((width, 2 * wide + SIDE), BF), ((rows, wide), BF), ((rows, LANES), F32)],
        [],
        2 * rows * width * wide,
        12 * rows * wide,
        ordered,
        feat,
        *gate_pieces,
        out_rows,
        all_w,
        aliases={3 + len(gate_pieces): 0},
    )
    grad, grad_t = call(
        functools.partial(mask_body, half_blocks),
        (blocks,),
        [smem(), half_spec, half_spec, block_rows(1)],
        [block_rows(width), pl.BlockSpec((width, QLEN), lambda b: (0, b))],
        [((rows, width), BF), ((width, rows), BF)],
        [],
        rows * width,
        8 * rows * width,
        place,
        cotangent,
        cot_got,
        live.astype(BF),
        deps=(gate,),
    )

    square_sum = jnp.sum(squares, axis=1).reshape(8, rows // 8)
    square_sum = square_sum + over_tensor(tied(square_sum, *proj_others[:1]))
    scale = lax.rsqrt(square_sum / INNER + EPSILON).reshape(rows, 1)

    def outer_outs(columns, step, first=0, paired=links.paired, kind=F32):
        if paired:
            spec = pl.BlockSpec((devices // 2, height, step), lambda j: (0, 0, j + first))
            return [spec] * 2, [((devices // 2, height, columns), BF)] * 2
        spec = pl.BlockSpec((width, step), lambda j: (0, j + first))
        return [spec], [((width, columns), kind)]

    both_kind = BF if links.paired else F32
    specs, outs = outer_outs(2 * wide, WIDE_TILE, 0, False, both_kind)
    gated, both_parts = call(
        proj_body,
        (broad,),
        [
            smem(),
            whole((width, rows)),
            broad_cols(rows),
            broad_cols(rows),
            whole((rows, 1)),
            broad_cols(1),
        ],
        [broad_cols(rows)] + specs,
        [((rows, wide), BF)] + outs,
        [],
        2 * rows * width * wide,
        14 * rows * wide,
        core,
        grad_t,
        out_rows,
        gate,
        scale,
        gate_row,
    )
    proj_others = [tied(x, gated) for x in proj_others]
    proj_pieces = links.join_halves(proj_halves, proj_others)

    def swapped(s, place_ref):
        return ((s // half_blocks + 1 - place_ref[0]) % 2) * half_blocks + s % half_blocks

    def swap_rows(n):
        return pl.BlockSpec((QLEN, n), lambda s, p, r: (swapped(s, p), 0))

    proj_w, branch_send, branch_own, row_dot = call(
        functools.partial(branch_body, len(proj_pieces)),
        (blocks,),
        [swap_rows(wide), swap_rows(width)] + [whole(p.shape) for p in proj_pieces],
        [
            whole((width, wide)),
            pl.BlockSpec((QLEN, width), lambda s, p, r: (jnp.minimum(s, half_blocks - 1), 0)),
            pl.BlockSpec((QLEN, width), lambda s, p, r: (jnp.maximum(s - half_blocks, 0), 0)),
            swap_rows(1),
        ],
        [
            ((width, wide), BF),
            ((half_rows, width), BF),
            ((half_rows, width), F32),
            ((rows, 1), F32),
        ],
        [],
        2 * rows * width * wide,
        8 * rows * wide,
        place,
        starts,
        gated,
        grad,
        *proj_pieces,
        prefetch=2,
    )
    row_total = row_dot.reshape(8, rows // 8)
    row_total = (row_total + over_tensor(row_total)).reshape(rows, 1)
    branch_got = over_tensor(branch_send)

    specs, outs = outer_outs(2 * wide, WIDE_TILE, broad, False, both_kind)
    core_grad, all_grad, channel_sums, both_parts = call(
        gating_body,
        (broad,),
        [
            smem(),
            whole((rows, width)),
            broad_cols(width),
            broad_cols(rows),
            broad_cols(rows),
            broad_cols(rows),
            whole((rows, 1)),
            whole((rows, 1)),
            broad_cols(1),
            whole((width, rows)),
            pl.BlockSpec(memory_space=pl.ANY),
        ],
        [broad_cols(rows), broad_cols(rows, broad), broad_cols(2)] + specs,
        [((rows, wide), BF), ((rows, 2 * wide + SIDE), BF), ((2, wide), F32)] + outs,
        [],
        4 * rows * width * wide,
        14 * rows * wide,
        core,
        grad,
        proj_w,
        out_rows,
        gate,
        act_low,
        scale,
        row_total,
        gate_row,
        feat_t,
        both_parts,
        aliases={10: 3},
    )
    both_sum = lax.psum_scatter(both_parts, "dp", scatter_dimension=0, tiled=True).astype(F32)
    proj_sum, gate_sum = both_sum[:, :wide], both_sum[:, wide:]

    def scan_part(first, count, past, grads, parts, columns, deps):
        summed = [whole((blocks, QLEN, QLEN)), whole((rows, STATE)), whole((rows, STATE))]
        specs, outs = outer_outs(columns, TILE, 0 if not parts else first)
        anywhere = [pl.BlockSpec(memory_space=pl.ANY)] * (1 + len(parts))
        at = 16 + len(past)
        return call(
            functools.partial(scan_body, blocks, bool(past), len(specs)),
            (count,),
            [smem(), smem(), whole((width, rows))]
            + [tile_cols(n, first) for n in (rows, rows, rows, rows, rows, 1, KERNEL)]
            + [
                pack_spec(first),
                rowpack_spec(first),
                whole((rows, STATE)),
                whole((rows, STATE)),
                whole((blocks, QLEN, QLEN)),
                entry_spec(first),
            ]
            + (summed if past else [])
            + anywhere,
            specs
            + [tile_cols(rows, first), tile_cols(KERNEL)]
            + summed
            + [pl.BlockSpec((1, rows, 4 * PER), lambda j: (j, 0, 0))],
            outs
            + [
                ((rows, 2 * wide + SIDE), BF),
                ((KERNEL, count * TILE), F32),
                ((blocks, QLEN, QLEN), F32),
                ((rows, STATE), F32),
                ((rows, STATE), F32),
                ((count, rows, 4 * PER), F32),
            ],
            [
                pltpu.VMEM((QLEN + 8, TILE), F32),
                pltpu.VMEM((QLEN + 8, TILE), F32),
                pltpu.VMEM((TILE, STATE), F32),
            ],
            6 * rows * width * count * TILE,
            20 * rows * count * TILE,
            core,
            keep,
            feat_t,
            slope_low,
            core_grad,
            act_low,
            pre_low,
            out_rows,
            skip_row,
            value_taps,
            pack,
            rowpack,
            b_low,
            c_low,
            gram_t,
            entry,
            *past,
            grads,
            *parts,
            deps=deps,
            aliases={at: len(specs), **{at + 1 + i: i for i in range(len(parts))}},
        )

    early = 2 * -(-tiles // 3)
    early_columns = early * TILE
    late_columns = wide - early_columns + SIDE
    *early_parts, all_grad, taps_a, gram_grad, b_grad, c_grad, stats_a = scan_part(
        0, early, (), all_grad, (), early_columns, ()
    )
    early_parts = links.scatter_core(early_parts)
    block_out = call(
        out_body,
        (half_blocks,),
        [block_rows(width)] * 3 + [block_rows(1)],
        [block_rows(width)],
        [((half_rows, width), BF)],
        [],
        half_rows * width,
        10 * half_rows * width,
        branch_own,
        branch_got,
        hidden_in,
        live_own,
        deps=(taps_a,),
    )[0]
    *late_parts, all_grad, taps_c, gram_grad, b_grad, c_grad, stats_c = scan_part(
        early,
        tiles - early,
        (gram_grad, b_grad, c_grad),
        all_grad,
        (),
        late_columns,
        (early_parts[0], block_out),
    )
    early_parts = links.scatter_pair(early_parts)
    taps_part = jnp.concatenate([taps_a, taps_c], axis=1)
    stats = [stats_a, stats_c]

    anywhere = pl.BlockSpec(memory_space=pl.ANY)
    held_shape = (devices // 2, height, SIDE) if links.paired else (width, SIDE)
    held_kind = BF if links.paired else F32
    at = 12 + len(stats)
    *late_parts, all_grad, sharetaps_part, head_sums = call(
        functools.partial(side_body, blocks, len(stats), len(late_parts)),
        (1,),
        [
            smem(),
            smem(),
            anywhere,
            whole((blocks, QLEN, QLEN)),
            whole((rows, STATE)),
            whole((rows, STATE)),
            whole((rows, STATE)),
            whole((rows, STATE)),
            whole((rows, TILE)),
            whole((KERNEL, TILE)),
            whole((3, rows, LANES)),
            whole((1, LANES)),
        ]
        + [whole(part.shape) for part in stats]
        + [anywhere] * (1 + len(late_parts)),
        [anywhere] * len(late_parts)
        + [
            pl.BlockSpec((rows, SIDE), lambda b: (0, 2 * wide // SIDE)),
            whole((KERNEL, TILE)),
            whole((2, LANES)),
        ],
        [(part.shape, part.dtype) for part in late_parts]
        + [((rows, 2 * wide + SIDE), BF), ((KERNEL, TILE), F32), ((2, LANES), F32)],
        [
            pltpu.VMEM((QLEN + 8, TILE), F32),
            pltpu.VMEM((QLEN + 8, TILE), F32),
            pltpu.VMEM((width, rows), BF),
            pltpu.VMEM(held_shape, held_kind),
            pltpu.VMEM(held_shape, held_kind),
            pltpu.SemaphoreType.DMA,
            pltpu.SemaphoreType.DMA((2,)),
        ],
        3 * rows * width * STATE,
        20 * rows * TILE,
        core,
        keep,
        feat_t,
        gram_grad,
        b_grad,
        c_grad,
        b_low,
        c_low,
        shared,
        shared_taps,
        cols,
        decay_row,
        *stats,
        all_grad,
        *late_parts,
        deps=(early_parts[0],),
        aliases={at: len(late_parts), **{at + 1 + i: i for i in range(len(late_parts))}},
    )

    def back(other, kind, deps=()):
        full = 2 * wide + SIDE

        def at(j, p):
            return ((1 - p[0]) if other else p[0], 0)

        return call(
            back_body,
            (width // WIDE_TILE,),
            [
                pl.BlockSpec((half_rows, full), at),
                pl.BlockSpec((WIDE_TILE, full), lambda j, p: (j, 0)),
            ],
            [pl.BlockSpec((half_rows, WIDE_TILE), lambda j, p: (0, j))],
            [((half_rows, width), kind)],
            [],
            2 * rows * width * wide,
            16 * rows * wide,
            place,
            all_grad,
            all_w,
            deps=deps,
            prefetch=1,
        )[0]

    late_parts = links.scatter_core(late_parts, early_parts[0])
    back_send = back(True, BF)
    early_sum = links.scatter_ring(early_parts, back_send)
    back_got = over_tensor(back_send)
    back_own = back(False, F32, (late_parts[0],))
    late_parts = links.scatter_pair(late_parts, back_own)
    input_grad = call(
        input_body,
        (half_blocks,),
        [block_rows(width)] * 4 + [whole((1, width))],
        [block_rows(width)],
        [((half_rows, width), BF)],
        [],
        half_rows * width,
        12 * half_rows * width,
        back_own,
        back_got,
        hidden_in,
        cotangent,
        gain_row,
    )[0]
    late_sum = links.scatter_ring(late_parts, input_grad)

    head_row = jnp.concatenate(
        [
            sharetaps_part.reshape(-1),
            head_sums[0, :heads],
            head_sums[1, :heads],
            jnp.sum(channel_sums[1].reshape(heads, HEAD_DIM), axis=1),
            jnp.zeros((wide - KERNEL * TILE - 3 * heads,), F32),
        ]
    ).reshape(1, wide)
    small = jnp.concatenate([taps_part, channel_sums[0:1], head_row], axis=0)
    small = links.reduce(small, back_send, late_parts[0])
    sharetaps = small[5:6, : KERNEL * TILE]
    sharetaps = sharetaps + over_tensor(sharetaps)

    rest = wide - early_columns
    value_sum = jnp.concatenate([early_sum, late_sum[:, :rest]], axis=1)
    side_sum = late_sum[:, rest : rest + 2 * STATE + heads]
    side_shard = jnp.concatenate([in_shared, in_step], axis=1)
    norm_part = (
        jnp.sum(gate_sum * in_gate.astype(F32), axis=1, keepdims=True)
        + jnp.sum(value_sum * in_value.astype(F32), axis=1, keepdims=True)
        + jnp.sum(side_sum * side_shard.astype(F32), axis=1, keepdims=True)
    ) / norm_gain.astype(F32)[:, None]
    mixed = jnp.concatenate(
        [late_sum[:, rest : rest + 2 * STATE], jnp.broadcast_to(norm_part, (height, LANES))], axis=1
    )
    mixed = mixed + over_tensor(mixed)

    share = KERNEL * TILE
    return (
        block_out,
        input_grad,
        mixed[:, 2 * STATE],
        gate_sum,
        value_sum,
        mixed[:, : 2 * STATE],
        side_sum[:, 2 * STATE :],
        small[0:KERNEL],
        sharetaps.reshape(KERNEL, TILE),
        small[5, share + heads : share + 2 * heads],
        small[5, share : share + heads],
        small[5, share + 2 * heads : share + 3 * heads],
        small[4],
        proj_sum.T,
    )


def solution(mesh):
    in_specs = (
        P(("dp", "tensor"), None),
        P("dp"),
        P("dp"),
        P("dp", "tensor"),
        P("dp", "tensor"),
        P("dp", None),
        P("dp", "tensor"),
        P(None, "tensor"),
        P(),
        P("tensor"),
        P("tensor"),
        P("tensor"),
        P("tensor"),
        P("tensor", "dp"),
        P(("dp", "tensor"), None),
    )
    out_specs = (
        P(("dp", "tensor"), None),
        P(("dp", "tensor"), None),
        P("dp"),
        P("dp", "tensor"),
        P("dp", "tensor"),
        P("dp", None),
        P("dp", "tensor"),
        P(None, "tensor"),
        P(),
        P("tensor"),
        P("tensor"),
        P("tensor"),
        P("tensor"),
        P("tensor", "dp"),
    )
    return jax.shard_map(
        functools.partial(on_device, devices=mesh.shape["dp"]),
        mesh=mesh,
        in_specs=in_specs,
        out_specs=out_specs,
        check_vma=False,
    )
```
